32 devices in a mesh: wide: 8 (over z, x), narrow: 4 (over y, core).
Axes of the slice: x: 2, y: 2, z: 4, core: 2. Of those that a mesh axis runs over, the one named last changes fastest.
Arguments:
- tokens: bfloat16 [16384, 512], P(('wide', 'narrow')), may hold values from -6 to 6
- cotangent: bfloat16 [16384, 512], P(('wide', 'narrow')), may hold values from -6 to 6
- segments: int32 [16384], P(('wide', 'narrow')), may hold values from 0 to 23, as said below
- padding: int32 [16384], P(('wide', 'narrow')), may hold values 0 or 1
- generative: int32 [16384], P(('wide', 'narrow')), may hold values 0 or 1
- in_weights: float32 [4, 512, 512], P(None, None, 'narrow'), may hold values from -0.25 to 0.25
- out_weights: float32 [2, 512, 512], P(None, 'narrow'), may hold values from -1.41421356 to 1.41421356
- in_momenta: float32 [4, 512, 512], P(None, None, 'narrow'), may hold values from -768 to 768
- out_momenta: float32 [2, 512, 512], P(None, 'narrow'), may hold values from -921.6 to 921.6
- in_average: float32 [4, 512, 512], P(None, None, 'narrow'), may hold values from -0.25 to 0.25
- out_average: float32 [2, 512, 512], P(None, 'narrow'), may hold values from -0.25 to 0.25
- shared_values: float32 [6, 512], replicated, may hold values from -1.2 to 1.4
- shared_moment1: float32 [6, 512], replicated, may hold values from -80 to 80
- shared_moment2: float32 [6, 512], replicated, may hold values from 16.384 to 65.536
- shared_average: float32 [6, 512], replicated, may hold values from -1.2 to 1.4
- split_values: float32 [3, 512], P(None, 'narrow'), may hold values from -1.75 to 1.75
- split_moment1: float32 [3, 512], P(None, 'narrow'), may hold values from -24 to 24
- split_moment2: float32 [3, 512], P(None, 'narrow'), may hold values from 1.6384 to 6.5536
- split_average: float32 [3, 512], P(None, 'narrow'), may hold values from -1.75 to 1.75
Outputs:
- out_tokens: bfloat16 [16384, 512], P(('wide', 'narrow'))
- grad_tokens: float32 [16384, 512], P(('wide', 'narrow'))
- in_momenta_new: float32 [4, 512, 512], P(None, None, 'narrow')
- out_momenta_new: float32 [2, 512, 512], P(None, 'narrow')
- in_weights_new: float32 [4, 512, 512], P(None, None, 'narrow')
- out_weights_new: float32 [2, 512, 512], P(None, 'narrow')
- in_weights_low: bfloat16 [4, 512, 512], P(None, None, 'narrow')
- out_weights_low: bfloat16 [2, 512, 512], P(None, 'narrow')
- in_average_new: float32 [4, 512, 512], P(None, None, 'narrow')
- out_average_new: float32 [2, 512, 512], P(None, 'narrow')
- shared_moment1_new: float32 [6, 512], replicated
- shared_moment2_new: float32 [6, 512], replicated
- shared_values_new: float32 [6, 512], replicated
- shared_average_new: float32 [6, 512], replicated
- split_moment1_new: float32 [3, 512], P(None, 'narrow')
- split_moment2_new: float32 [3, 512], P(None, 'narrow')
- split_values_new: float32 [3, 512], P(None, 'narrow')
- split_average_new: float32 [3, 512], P(None, 'narrow')
The draws below stay inside these ranges and needn't reach their ends.
Inputs may be any that keep to these rules, and one draw needn't show every extreme that they name: `segments`: never falls along the tokens; tokens of different rows have different numbers.
All inputs are finite; a program needn't handle non-finite values. No bound on the sum of `padding` or of `generative` on one device may be relied on, other than what follows from the above.
Results may differ from the reference program's by a relative error of at most 0.018.
Values may be sent and summed in bfloat16 or wider, within the bound.
A program may use at most 128 MiB of HBM per device.

```python
import math
import jax
import jax.numpy as jnp
from jax import lax

D = 512
H = 8
HD = 64
LEN = 2048
NS_ITERS = 3
STEP = 10
ROWS = 8
TOKENS = 16384


def ramp_up(length, top):
    return 1.0 + (top - 1.0) * jnp.arange(length, dtype=jnp.float32) / (length - 1)


def draw_segments(key, part):
    key = jax.random.fold_in(key, 11)
    first_key, second_key = jax.random.split(key)
    begins = jax.random.randint(first_key, (ROWS, 1), LEN // 16, LEN // 8)
    finish = jax.random.randint(second_key, (ROWS, 1), LEN - LEN // 8, LEN - LEN // 16)
    places = jnp.arange(LEN, dtype=jnp.int32)[None, :]
    row_ids = jnp.arange(ROWS, dtype=jnp.int32)[:, None]
    cells = 3 * row_ids + (places >= begins).astype(jnp.int32) + (places >= finish).astype(jnp.int32)
    return cells.reshape(TOKENS)


def draw_out_weights(key, part):
    key = jax.random.fold_in(key, 12)
    base = jax.random.truncated_normal(key, -4.0, 4.0, (2, D, D), jnp.float32)
    scales = jnp.array([(LEN / (32.0 * D)) ** 0.5, D ** (-0.5)], jnp.float32)
    return base * scales[:, None, None]


def draw_in_momenta(key, part):
    key = jax.random.fold_in(key, 13)
    base = jax.random.truncated_normal(key, -4.0, 4.0, (4, D, D), jnp.float32) * ramp_up(D, 3.0)[None, None, :]
    scales = jnp.array([0.05, 0.05, 0.1, 0.5], jnp.float32) * TOKENS ** 0.5
    return base * scales[:, None, None]


def draw_out_momenta(key, part):
    key = jax.random.fold_in(key, 14)
    base = jax.random.truncated_normal(key, -4.0, 4.0, (2, D, D), jnp.float32) * ramp_up(D, 3.0)[None, :, None]
    scales = jnp.array([0.1, 0.6], jnp.float32) * TOKENS ** 0.5
    return base * scales[:, None, None]


def vector_rows(base):
    gains = jnp.array([1.0, 0.0, 1.0, 0.0, 0.0, 0.0], jnp.float32)[:, None]
    return gains * (1.0 + 0.1 * base) + (1.0 - gains) * 0.3 * base


def draw_shared_values(key, part):
    key = jax.random.fold_in(key, 15)
    base = jax.random.truncated_normal(key, -4.0, 4.0, (6, D), jnp.float32)
    return vector_rows(base)


def draw_shared_average(key, part):
    key = jax.random.fold_in(key, 16)
    base = jax.random.truncated_normal(key, -4.0, 4.0, (6, D), jnp.float32)
    return vector_rows(base)


def place_ends(values, own_key, least, top_value):
    longest = values.shape.index(max(values.shape))
    spots = []
    for shift in (0, 1):
        where = [jax.random.randint(jax.random.fold_in(own_key, axis), (), 0, length) for axis, length in enumerate(values.shape)]
        where[longest] = (where[longest] + shift) % values.shape[longest]
        spots.append(tuple(where))
    return values.at[spots[0]].set(least).at[spots[1]].set(top_value)


def block_levels(own_key, shape, cuts, smallest, largest):
    def one(position, parts):
        draws = jax.random.uniform(jax.random.fold_in(jax.random.fold_in(own_key, 6), position), (parts,), jnp.float32, smallest / len(cuts), largest / len(cuts))
        return jnp.repeat(jnp.exp(draws), shape[position] // parts).reshape((-1,) + (1,) * (len(shape) - position - 1))

    factor_of = one(*cuts[0])
    for cut in cuts[1:]:
        factor_of = factor_of * one(*cut)
    return factor_of


def centred(stream_key, shape, scale, most, cuts=(), kind=jnp.bfloat16):
    level = block_levels(stream_key, shape, cuts, -0.22, 0.18) if cuts else 1.0
    values = jax.random.normal(stream_key, shape, jnp.float32) * scale * level
    return jnp.minimum(jnp.maximum(values, -most), most).astype(kind)


def setup_inputs(seed: int = 0) -> dict:
    streams_of = jax.random.split(jax.random.key(seed), 20)
    tokens = centred(streams_of[0], (TOKENS, D), 1.0, 6.0, ((0, 32),))
    cotangent = centred(streams_of[1], (TOKENS, D), 1.0, 6.0, ((0, 32),))
    segments = draw_segments(jax.random.fold_in(streams_of[19], 71), 0)
    padding = place_ends((jax.random.randint(streams_of[3], (TOKENS,), 0, 8) < 1).astype(jnp.int32), jax.random.fold_in(streams_of[3], 1), 0, 1)
    generative = place_ends((jax.random.randint(streams_of[4], (TOKENS,), 0, 4) < 1).astype(jnp.int32), jax.random.fold_in(streams_of[4], 1), 0, 1)
    in_weights = centred(streams_of[5], (4, D, D), D ** -0.5, 0.25, ((2, 4),), jnp.float32)
    out_weights = draw_out_weights(jax.random.fold_in(streams_of[19], 71), 0)
    in_momenta = draw_in_momenta(jax.random.fold_in(streams_of[19], 71), 0)
    out_momenta = draw_out_momenta(jax.random.fold_in(streams_of[19], 71), 0)
    in_average = centred(streams_of[9], (4, D, D), D ** -0.5, 0.25, ((2, 4),), jnp.float32)
    out_average = centred(streams_of[10], (2, D, D), D ** -0.5, 0.25, ((1, 4),), jnp.float32)
    shared_values = draw_shared_values(jax.random.fold_in(streams_of[19], 71), 0)
    shared_moment1 = centred(streams_of[12], (6, D), (0.11 * TOKENS ** 0.5), 80.0, (), jnp.float32)
    shared_moment2 = jnp.clip(jnp.exp(jax.random.uniform(streams_of[13], (6, D), jnp.float32, math.log(16.384), math.log(65.536))), 16.384, 65.536)
    shared_average = draw_shared_average(jax.random.fold_in(streams_of[19], 71), 0)
    split_values = centred(streams_of[15], (3, D), 0.3, 1.75, ((1, 4),), jnp.float32)
    split_moment1 = centred(streams_of[16], (3, D), (0.03 * TOKENS ** 0.5), 24.0, ((1, 4),), jnp.float32)
    split_moment2 = jnp.clip(jnp.exp(math.log(6.5536) - 1.3862944 * jax.random.uniform(streams_of[17], (3, D), jnp.float32) ** block_levels(streams_of[17], (3, D), ((1, 4),), -0.2, 0.2)), 1.6384, 6.5536)
    split_average = centred(streams_of[18], (3, D), 0.3, 1.75, ((1, 4),), jnp.float32)
    return dict(tokens=tokens, cotangent=cotangent, segments=segments, padding=padding, generative=generative, in_weights=in_weights, out_weights=out_weights, in_momenta=in_momenta, out_momenta=out_momenta, in_average=in_average, out_average=out_average, shared_values=shared_values, shared_moment1=shared_moment1, shared_moment2=shared_moment2, shared_average=shared_average, split_values=split_values, split_moment1=split_moment1, split_moment2=split_moment2, split_average=split_average)


@jax.custom_vjp
def low(v):
    return lax.optimization_barrier(v.astype(jnp.bfloat16)).astype(jnp.float32)

@jax.custom_vjp
def low_back(v):
    return v

def low_keep(v):
    return (low(v), None)

def low_pass(kept, grad):
    return (grad,)

def back_keep(v):
    return (v, None)

def back_low(kept, grad):
    return (low(grad),)
low.defvjp(low_keep, low_pass)
low_back.defvjp(back_keep, back_low)
coef_a = 3.4445
coef_b = -4.775
coef_c = 2.0315

def matmul(left, right):
    return jnp.dot(left, right, precision=lax.Precision.HIGHEST, preferred_element_type=jnp.float32)

def layer_norm(values, gain_vec, shift_vec):
    center = values - lax.optimization_barrier(jnp.mean(values, axis=-1, keepdims=True))
    spread = lax.optimization_barrier(jnp.mean(center * center, axis=-1, keepdims=True))
    return center * lax.rsqrt(spread + 1e-05) * gain_vec + shift_vec

def gelu_exact(values):
    return jax.nn.gelu(values, approximate=False)

def row_forward(params, x_row, seg_row, pad_row, gen_row):
    w_in, w_out, shared, split = params
    low_in = low(w_in)
    low_out = low(w_out)
    q_rows = low(low_back(matmul(x_row, low_in[0]) + split[0])).reshape(LEN, H, HD)
    k_rows = low(low_back(matmul(x_row, low_in[1]))).reshape(LEN, H, HD)
    v_rows = low(low_back(matmul(x_row, low_in[2]) + split[1])).reshape(LEN, H, HD)
    block_len = min(512, LEN)
    block_num = LEN // block_len
    places = jnp.arange(LEN, dtype=jnp.int32)
    open_keys = (pad_row == 0) & (gen_row == 0)
    score_scale = HD ** (-0.5)

    def attend(pieces):
        q_block, seg_block, pos_block = pieces
        raw_scores = low_back(jnp.einsum('qhe,khe->hqk', q_block, k_rows, precision=lax.Precision.HIGHEST) * score_scale)
        allowed = (seg_block[:, None] == seg_row[None, :]) & (open_keys[None, :] | (pos_block[:, None] == places[None, :]))
        masked = jnp.where(allowed[None], raw_scores, -1e+30)
        prob_rows = jax.nn.softmax(masked, axis=-1)
        return jnp.einsum('hqk,khe->qhe', low(prob_rows), v_rows, precision=lax.Precision.HIGHEST)
    context = lax.map(jax.checkpoint(attend), (q_rows.reshape(block_num, block_len, H, HD), seg_row.reshape(block_num, block_len), places.reshape(block_num, block_len)))
    context = low(low_back(context.reshape(LEN, D)))
    attention = low_back(matmul(context, low_out[0])) + shared[4]
    hidden = layer_norm(x_row + attention, shared[0], shared[1])
    upper_in = low_back(matmul(low(hidden), low_in[3]) + split[2])
    active = low(gelu_exact(upper_in))
    ff_out = low_back(matmul(active, low_out[1])) + shared[5]
    return layer_norm(hidden + ff_out, shared[2], shared[3])

def forward(params, tokens32, segments, padding, generative):

    def per_seq(row_parts):
        return row_forward(params, row_parts[0], row_parts[1], row_parts[2], row_parts[3])
    row_parts = (tokens32.reshape(ROWS, LEN, D), segments.reshape(ROWS, LEN), padding.reshape(ROWS, LEN), generative.reshape(ROWS, LEN))
    return lax.map(jax.checkpoint(per_seq), row_parts).reshape(TOKENS, D)

def newton(moments):
    norms = jnp.sqrt(lax.optimization_barrier(jnp.sum(moments * moments, axis=(1, 2))))
    current = moments / (norms + 1e-07)[:, None, None]
    for iteration in range(NS_ITERS):
        gram = jnp.einsum('kde,kfe->kdf', current, current, precision=lax.Precision.HIGHEST)
        poly = coef_b * gram + coef_c * jnp.einsum('kde,kef->kdf', gram, gram, precision=lax.Precision.HIGHEST)
        current = coef_a * current + jnp.einsum('kde,kef->kdf', poly, current, precision=lax.Precision.HIGHEST)
    return current

def muon_step(weights, orthogonal):
    return weights - 0.2 * (0.2 * math.sqrt(D) * orthogonal + 0.01 * weights)

def adam_step(values, moment_one, moment_two, gradient):
    moment_one = 0.9 * moment_one + 0.1 * gradient
    moment_two = 0.999 * moment_two + 0.001 * gradient * gradient
    step_ratio = moment_one / (1.0 - 0.9 ** STEP) / (jnp.sqrt(moment_two / (1.0 - 0.999 ** STEP)) + 1e-08)
    return (moment_one, moment_two, values - 0.3 * (step_ratio + 0.01 * values))

def blend(average, weights):
    return 0.6 * average + 0.4 * weights

def reference(tokens, cotangent, segments, padding, generative, in_weights, out_weights, in_momenta, out_momenta, in_average, out_average, shared_values, shared_moment1, shared_moment2, shared_average, split_values, split_moment1, split_moment2, split_average):
    tokens32 = tokens.astype(jnp.float32)

    def run_layer(params, inputs):
        return forward(params, inputs, segments, padding, generative)
    params = (in_weights, out_weights, shared_values, split_values)
    result, pullback = jax.vjp(run_layer, params, tokens32)
    grads, grad_tokens = pullback(cotangent.astype(jnp.float32))
    grad_in, grad_out, grad_shared, grad_split = grads
    mom_in = 0.5 * in_momenta + grad_in
    mom_out = 0.5 * out_momenta + grad_out
    orthogonal = newton(jnp.concatenate([mom_in, mom_out], axis=0))
    new_in = muon_step(in_weights, orthogonal[:4])
    new_out = muon_step(out_weights, orthogonal[4:])
    shared_one, shared_two, shared_new = adam_step(shared_values, shared_moment1, shared_moment2, grad_shared)
    split_one, split_two, split_new = adam_step(split_values, split_moment1, split_moment2, grad_split)
    return (result.astype(jnp.bfloat16), grad_tokens, mom_in, mom_out, new_in, new_out, new_in.astype(jnp.bfloat16), new_out.astype(jnp.bfloat16), blend(in_average, new_in), blend(out_average, new_out), shared_one, shared_two, shared_new, blend(shared_average, shared_new), split_one, split_two, split_new, blend(split_average, split_new))
```

```python
import functools
import math

import jax
import jax.numpy as jnp
from jax import lax
from jax.experimental import pallas as pl
from jax.experimental.pallas import tpu as pltpu
from jax.sharding import PartitionSpec as P

D = 512
HD = 64
LEN = 2048
NS_ITERS = 3
STEP = 10
NAR = 4
TB = LEN // NAR
CW = D // NAR
OWN = 8
PR = CW // OWN
MID = 256

F32 = jnp.float32
BF16 = jnp.bfloat16
MESH = pl.DeviceIdType.MESH

COEF_A = 3.4445
COEF_B = -4.775
COEF_C = 2.0315
NEG = -1e30
MB = 2**20


def mm(a, b):
    return jnp.dot(a, b, preferred_element_type=F32)


def mm_nt(a, b):
    return lax.dot_general(a, b, (((1,), (1,)), ((), ())), preferred_element_type=F32)


def mm_tn(a, b):
    return lax.dot_general(a, b, (((0,), (0,)), ((), ())), preferred_element_type=F32)


def layer_kernel(wide, *refs):
    (
        tok_h, cot_h, pay_i, win_h, wout_h, min_h, mout_h, shared, split,
        otok_h, ograd_h, omom_h, oorth_h, ovec, ovec2,
        tok, cot, pay, win_f, wout_f, mT, wqkvT, wqkv, wup, wod, bcol,
        qp, kTp, vTp, qT, rdn, s_ref, e_ref, ctxn, ctx_s, ctxf,
        hr, act, du, dr2r, dr1r, dr1, dcst, dcr, vecs, vecw, dkT, dvT, gT,
        gst, gr1, gs2, gr2, est, erx, lst, lrx, lv, mom, grp,
        dxs, dxr1, dxs2, dxr2,
        loc_sem, ag_s, ag_r, rly_s, rly_r, pay_s, pay_r, wg_s, wg_r, wr_s, wr_r,
        ctx_sem, ctx_rem, dc_sem, dc_rem, vn_s, vn_r, vw_s, vw_r,
        g1_s, g1_r, g2_s, g2_r, es_s, es_r, ls_s, ls_r, lv_s, lv_r, gp_s, gp_r,
        aw_s, aw_r, an_s, an_r, ar_s, ar_r, dx1_s, dx1_r, dx2_s, dx2_r,
    ) = refs
    n = lax.axis_index("narrow")
    w = lax.axis_index("wide")
    groups = wide // OWN
    g = w // OWN if groups > 1 else 0
    o = lax.rem(w, OWN) if groups > 1 else w
    b0 = lax.rem(n, 2)
    b1 = n // 2

    def rel(x):
        return lax.rem(b0 + x % 2, 2) + 2 * lax.rem(b1 + x // 2, 2)

    n1, n2, n3 = rel(1), rel(2), rel(3)

    def rows(t, size):
        return pl.ds(pl.multiple_of(t * size, size), size)

    def ncopy(src, dst, ssem, rsem, t):
        return pltpu.make_async_remote_copy(
            src_ref=src, dst_ref=dst, send_sem=ssem, recv_sem=rsem,
            device_id={"narrow": t}, device_id_type=MESH,
        )

    def wcopy(src, dst, ssem, rsem, u):
        return pltpu.make_async_remote_copy(
            src_ref=src, dst_ref=dst, send_sem=ssem, recv_sem=rsem,
            device_id={"wide": u}, device_id_type=MESH,
        )

    pending = []

    def start(copy):
        copy.start()
        pending.append(copy)
        return copy

    own = rows(n, TB)
    xbuf = s_ref.at[:, 0:D]
    ograd = s_ref.at[:, D:2 * D]
    orth = mT
    rln = rdn
    otok = cot

    l_tok = pltpu.make_async_copy(tok_h, tok.at[own], loc_sem.at[0])
    l_win = pltpu.make_async_copy(win_h, win_f, loc_sem.at[1])
    l_wout = pltpu.make_async_copy(wout_h, wout_f, loc_sem.at[2])
    l_cot = pltpu.make_async_copy(cot_h, cot, loc_sem.at[3])
    l_min = pltpu.make_async_copy(min_h, win_f, loc_sem.at[4])
    l_mout = pltpu.make_async_copy(mout_h, mT.at[pl.ds(4, 2)], loc_sem.at[5])
    for c in (l_tok, l_win, l_wout, l_cot, l_mout):
        c.start()

    barrier = pltpu.get_barrier_semaphore()
    for x in (1, 2, 3):
        pl.semaphore_signal(barrier, inc=1, device_id={"narrow": rel(x)}, device_id_type=MESH)

    def greet(i, c):
        pl.semaphore_signal(
            barrier, inc=1, device_id={"wide": g * OWN + lax.rem(o + i, OWN)}, device_id_type=MESH
        )
        return c

    lax.fori_loop(1, OWN, greet, 0)

    def greet_group(i, c):
        pl.semaphore_signal(
            barrier, inc=1, device_id={"wide": lax.rem(g + i, groups) * OWN + o}, device_id_type=MESH
        )
        return c

    if groups > 1:
        lax.fori_loop(1, groups, greet_group, 0)
    pay[n] = pay_i[...]
    l_tok.wait()
    pl.semaphore_wait(barrier, 3 + (OWN - 1) + (groups - 1))

    half = TB // 2

    def ag_rows(t, c):
        return tok.at[pl.ds(pl.multiple_of(t * TB + c * half, half), half)]

    for x in (1, 2, 3):
        start(ncopy(pay.at[n], pay.at[n], pay_s.at[x], pay_r.at[x], rel(x)))
    for c in (0, 1):
        start(ncopy(ag_rows(n, c), ag_rows(n, c), ag_s.at[2 + c], ag_r.at[2 + c], n2))
    for c in (0, 1):
        start(ncopy(ag_rows(n, c), ag_rows(n, c), ag_s.at[c], ag_r.at[c], n1))

    def arrived(slot, sem_s, sem_r, t):
        ncopy(slot, slot, sem_s, sem_r, t).wait_recv()

    l_win.wait()
    for k in range(3):
        piece = win_f[k]
        wqkvT[k * CW:(k + 1) * CW, :] = piece.T.astype(BF16)
        wqkv[:, k * CW:(k + 1) * CW] = piece.astype(BF16)
    mycols = pl.ds(pl.multiple_of(n * CW, CW), CW)
    wup[:, mycols] = win_f[3].astype(BF16)
    l_min.start()
    l_wout.wait()
    for k in range(2):
        wod[k, mycols, :] = wout_f[k].astype(BF16)

    def wg_list(sems, semr, x, t, target):
        cols = pl.ds(pl.multiple_of(t * CW, CW), CW)
        return [
            ncopy(wod.at[:, cols, :], wod.at[:, cols, :], sems.at[x, 0], semr.at[x, 0], target),
            ncopy(wup.at[:, cols], wup.at[:, cols], sems.at[x, 1], semr.at[x, 1], target),
        ]

    for x in (2, 1):
        for c in wg_list(wg_s, wg_r, x, n, rel(x)):
            start(c)

    bcol[0] = jnp.broadcast_to(split[0:1, :], (CW, CW)).T
    bcol[1] = jnp.broadcast_to(split[1:2, :], (CW, CW)).T

    def project(t):
        tb = tok[rows(t, TB), :]
        qk = mm(tb, wqkv[:, 0:2 * CW])
        q = (qk[:, :CW] + split[0:1, :]).astype(BF16)
        k = qk[:, CW:].astype(BF16)
        q8 = q.astype(F32) * 0.125
        prod = q8 * k.astype(F32)
        lane = lax.broadcasted_iota(jnp.int32, (TB, CW), 1)
        low = lane < HD
        d0 = jnp.sum(jnp.where(low, prod, 0.0), axis=1, keepdims=True)
        d1 = jnp.sum(jnp.where(low, 0.0, prod), axis=1, keepdims=True)
        rdn[rows(t, TB), :] = jnp.where(low, d0, d1)
        lane1 = lax.broadcasted_iota(jnp.int32, (CW, CW), 1).astype(F32)
        for j in range(TB // CW):
            seg = jnp.broadcast_to(pay[t, j:j + 1, :], (CW, CW)).T
            part = q8[j * CW:(j + 1) * CW, :]
            lowj = lane1 < HD
            hot = lambda base: jnp.where(seg == lane1 + base, 1.0, 0.0)
            rr = pl.ds(pl.multiple_of(t * TB + j * CW, CW), CW)
            qp[0, rr, 0:CW] = jnp.where(lowj, part, hot(-float(HD))).astype(BF16)
            qp[1, rr, 0:CW] = jnp.where(lowj, hot(0.0), part).astype(BF16)
            rest = hot(float(HD)).astype(BF16)
            qp[0, rr, CW:] = rest
            qp[1, rr, CW:] = rest
        tT = mm_nt(wqkvT[...], tb)
        bq = jnp.concatenate([bcol[0]] * (TB // CW), axis=1)
        bv = jnp.concatenate([bcol[1]] * (TB // CW), axis=1)
        cols = rows(t, TB)
        qT[:, cols] = ((tT[0:CW] + bq).astype(BF16).astype(F32) * 0.125).astype(BF16)
        kT = tT[CW:2 * CW].astype(BF16)
        vT = (tT[2 * CW:] + bv).astype(BF16)
        code = jnp.concatenate([pay[t, 4 + j:5 + j, :] for j in range(TB // CW)], axis=1)
        rowi = lax.broadcasted_iota(jnp.int32, (HD, TB), 0).astype(F32)
        keep = lambda base: jnp.where(code == rowi + base, 0.0, NEG).astype(BF16)
        first, second, third = keep(0.0), keep(float(HD)), keep(float(2 * HD))
        ones = jnp.ones((HD, TB), BF16)
        kTp[0, 0:HD, cols] = kT[0:HD]
        kTp[0, HD:CW, cols] = first
        kTp[1, 0:HD, cols] = first
        kTp[1, HD:CW, cols] = kT[HD:]
        vTp[0, 0:HD, cols] = vT[0:HD]
        vTp[0, HD:, cols] = ones
        vTp[1, 0:HD, cols] = ones
        vTp[1, HD:, cols] = vT[HD:]
        for h in range(2):
            kTp[h, CW:CW + HD, cols] = second
            kTp[h, CW + HD:, cols] = third

    def project_step(i, _):
        @pl.when(i == 1)
        def _():
            arrived(pay.at[n1], pay_s.at[1], pay_r.at[1], n1)
            for c in (0, 1):
                arrived(ag_rows(n1, c), ag_s.at[c], ag_r.at[c], n1)
            l_min.wait()
            for k in range(4):
                mT[k] = win_f[k].T

        @pl.when(i == 2)
        def _():
            arrived(pay.at[n2], pay_s.at[2], pay_r.at[2], n2)
            arrived(pay.at[n3], pay_s.at[3], pay_r.at[3], n3)
            for c in (0, 1):
                arrived(ag_rows(n2, c), ag_s.at[2 + c], ag_r.at[2 + c], n2)
                ncopy(ag_rows(n2, c), ag_rows(n2, c), rly_s.at[c], rly_r.at[c], n1).start()

        @pl.when(i == 3)
        def _():
            for c in (0, 1):
                arrived(ag_rows(n3, c), rly_s.at[c], rly_r.at[c], n1)

        project(rel(i))
        return 0

    lax.fori_loop(0, NAR, project_step, 0)
    for c in (0, 1):
        pending.append(ncopy(ag_rows(n2, c), ag_rows(n2, c), rly_s.at[c], rly_r.at[c], n1))

    eye = lax.broadcasted_iota(jnp.int32, (CW, CW), 0) == lax.broadcasted_iota(jnp.int32, (CW, CW), 1)

    def ctx_copy(x, t):
        return ncopy(
            ctx_s.at[rows(t, TB)], ctxf.at[:, mycols], ctx_sem.at[x], ctx_rem.at[x], t
        )

    def attend(i, _):
        hi = 1 - i // 2
        lo = lax.rem((i + 1) // 2, 2)
        t = lax.rem(b0 + lo, 2) + 2 * lax.rem(b1 + hi, 2)
        rr = rows(t, TB)
        parts = []
        for h in range(2):
            s_ref[...] = mm(qp[h, rr, :], kTp[h])
            for j in range(TB // CW):
                cc = pl.ds(pl.multiple_of(t * TB + j * CW, CW), CW)
                diag = rdn[cc, h * HD:h * HD + 1]
                sub = pl.ds(j * CW, CW)
                s_ref[sub, cc] = jnp.where(eye, diag, s_ref[sub, cc])
            s = s_ref[...]
            top = jnp.max(s, axis=1, keepdims=True)
            e = jnp.exp(s - top).astype(BF16)
            e_ref[h, rr, :] = e
            parts.append(mm_nt(vTp[h], e))
        num = jnp.concatenate([parts[0][:HD], parts[1][HD:]], axis=0)
        den = 1.0 / jnp.concatenate([parts[0][HD:], parts[1][:HD]], axis=0)
        cn = (num * den).T
        ctxn[rr, :] = cn
        rln[rr, :] = den.T
        ctx_s[rr, :] = cn.astype(BF16)

        @pl.when(i < 3)
        def _():
            x = lo + 2 * hi
            ctx_copy(x, t).start()

        @pl.when(i == 0)
        def _():
            for c in wg_list(wg_s, wg_r, 2, n2, n2):
                c.wait_recv()
            for c in wg_list(wr_s, wr_r, 0, n2, n1):
                c.start()

        return 0

    lax.fori_loop(0, NAR, attend, 0)
    pending.extend(wg_list(wr_s, wr_r, 0, n2, n1))
    for x in (1, 2, 3):
        pending.append(ctx_copy(x, rel(x)))
    ctxf[:, mycols] = ctx_s[own, :]
    for c in wg_list(wg_s, wg_r, 1, n1, n1):
        c.wait_recv()
    for c in wg_list(wr_s, wr_r, 0, n3, n1):
        c.wait_recv()
    l_cot.wait()
    l_mout.wait()
    for x in (2, 3, 1):
        cols = pl.ds(pl.multiple_of(rel(x) * CW, CW), CW)
        ncopy(ctx_s.at[own], ctxf.at[:, cols], ctx_sem.at[x], ctx_rem.at[x], rel(x)).wait_recv()

    up_bias = jnp.concatenate([pay[t, 8:9, :] for t in range(NAR)], axis=1)
    vecs[n] = jnp.zeros((8, D), F32)

    def dc_copy(x, c, t, me):
        rr = pl.ds(c * MID, MID)
        cols = pl.ds(pl.multiple_of(t * CW, CW), CW)
        dst = dcr.at[pl.ds(pl.multiple_of(me * TB + c * MID, MID), MID)]
        return ncopy(dcst.at[rr, cols], dst, dc_sem.at[x, c], dc_rem.at[x, c], t)

    def middle(c, _):
        rr = pl.ds(pl.multiple_of(c * MID, MID), MID)
        ga1, be1, ga2, be2, ba, bd = (shared[k:k + 1, :] for k in range(6))
        x0 = tok[pl.ds(pl.multiple_of(n * TB + c * MID, MID), MID), :].astype(F32)
        r1 = x0 + (mm(ctxf[rr, :], wod[0]) + ba)
        c1 = r1 - jnp.mean(r1, axis=1, keepdims=True)
        s1 = lax.rsqrt(jnp.mean(c1 * c1, axis=1, keepdims=True) + 1e-05)
        x1 = c1 * s1
        hidden = x1 * ga1 + be1
        low = hidden.astype(BF16)
        hr[rr, :] = low
        upper = mm(low, wup[...]) + up_bias
        cdf = 0.5 * (1.0 + lax.erf(upper * (1.0 / math.sqrt(2.0))))
        pdf = jnp.exp(-0.5 * upper * upper) * (1.0 / math.sqrt(2.0 * math.pi))
        slope = cdf + upper * pdf
        a = (upper * cdf).astype(BF16)
        act[rr, :] = a
        r2 = hidden + (mm(a, wod[1]) + bd)
        c2 = r2 - jnp.mean(r2, axis=1, keepdims=True)
        s2 = lax.rsqrt(jnp.mean(c2 * c2, axis=1, keepdims=True) + 1e-05)
        x2 = c2 * s2
        dy = cot[rr, :].astype(F32)
        otok[rr, :] = (x2 * ga2 + be2).astype(BF16)
        dn = dy * ga2
        dr2 = s2 * (
            dn - jnp.mean(dn, axis=1, keepdims=True) - x2 * jnp.mean(dn * x2, axis=1, keepdims=True)
        )
        d2 = dr2.astype(BF16)
        dr2r[rr, :] = d2
        dup = (mm_nt(d2, wod[1]) * slope).astype(BF16)
        du[rr, :] = dup
        dh = dr2 + mm_nt(dup, wup[...])
        en = dh * ga1
        d1f = s1 * (
            en - jnp.mean(en, axis=1, keepdims=True) - x1 * jnp.mean(en * x1, axis=1, keepdims=True)
        )
        dr1[rr, :] = d1f
        d1 = d1f.astype(BF16)
        dr1r[rr, :] = d1
        dcst[rr, :] = mm_nt(d1, wod[0]).astype(BF16)
        add = lambda v: jnp.sum(v, axis=0, keepdims=True)
        vecs[n] += jnp.concatenate(
            [
                add(dh * x1), add(dh), add(dy * x2), add(dy), add(d1f), add(dr2),
                add(dup.astype(F32)), jnp.zeros((1, D), F32),
            ],
            axis=0,
        )
        for k in range(TB // MID):
            @pl.when(c == k)
            def _():
                for x in (2, 3, 1):
                    dc_copy(x, k, rel(x), n).start()

        dcr[pl.ds(pl.multiple_of(n * TB + c * MID, MID), MID), :] = dcst[rr, mycols]
        return 0

    lax.fori_loop(0, TB // MID, middle, 0)
    for x in (1, 2, 3):
        for c in range(TB // MID):
            pending.append(dc_copy(x, c, rel(x), n))
    l_otok = pltpu.make_async_copy(otok, otok_h, loc_sem.at[6])
    l_otok.start()
    for x in (1, 2, 3):
        start(ncopy(vecs.at[n], vecs.at[n], vn_s.at[x], vn_r.at[x], rel(x)))

    for k, (left, right) in enumerate(((du, hr), (ctxf, dr1r), (act, dr2r))):
        grad = mm_tn(left[...], right[...]).astype(BF16)
        for t in range(NAR):
            gst[t, k] = grad[t * CW:(t + 1) * CW]
    start(ncopy(gst.at[n3], gr1.at[1], g1_s.at[1], g1_r.at[1], n1))
    start(ncopy(gst.at[n1], gr1.at[0], g1_s.at[0], g1_r.at[0], n1))

    def group_loop(fn, first=1, count=OWN):
        def go(i, c):
            fn(i)
            return c

        lax.fori_loop(first, count, go, 0)

    def member(i):
        return lax.rem(o + i, OWN)

    def scatter(i, src, dst, ssem, rsem):
        u = member(i)
        piece = pl.ds(pl.multiple_of(u * PR, PR), PR)
        return wcopy(src.at[:, piece, :], dst.at[o], ssem.at[i], rsem.at[o], g * OWN + u)

    def scatter_all(*where):
        group_loop(lambda i: scatter(i, *where).start())

    def scatter_done(*where):
        group_loop(lambda i: scatter(i, *where).wait_send())

    mine = pl.ds(pl.multiple_of(o * PR, PR), PR)
    place = pl.ds(pl.multiple_of(n * CW + o * PR, PR), PR)

    def across(k, i):
        return wcopy(
            grp.at[k, g], grp.at[k, g], gp_s.at[k, i], gp_r.at[k, g], lax.rem(g + i, groups) * OWN + o
        )

    def collect(base, src, dst, ssem, rsem):
        k = 0 if base == 3 else 1
        dst[o] = src[:, mine, :]

        def take(i):
            v = member(i)
            wcopy(src.at[:, mine, :], dst.at[v], ssem.at[0], rsem.at[v], g * OWN + v).wait_recv()

        group_loop(take)
        total = lax.fori_loop(
            0, OWN, lambda v, t: t + dst[v].astype(F32), jnp.zeros((3, PR, D), F32)
        )
        if groups > 1:
            grp[k, g] = total.astype(BF16)
            group_loop(lambda i: across(k, i).start(), 1, groups)

            def meet(i):
                v = lax.rem(g + i, groups)
                wcopy(grp.at[k, v], grp.at[k, v], gp_s.at[k, i], gp_r.at[k, v], v * OWN + o).wait_recv()

            group_loop(meet, 1, groups)
            total = lax.fori_loop(
                0, groups, lambda v, t: t + grp[k, v].astype(F32), jnp.zeros((3, PR, D), F32)
            )
        total = total + 0.5 * mT[pl.ds(base, 3), mine, :]
        mom[pl.ds(base, 3), place, :] = total.astype(BF16)
        group_loop(lambda i: share(base, o, i).start())

    def share(base, u, i):
        ref = mom.at[pl.ds(base, 3), pl.ds(pl.multiple_of(n * CW + u * PR, PR), PR), :]
        k = 0 if base == 3 else 1
        return wcopy(ref, ref, aw_s.at[k, i], aw_r.at[k, u], g * OWN + member(i))

    def share_wait(base):
        group_loop(lambda i: share(base, member(i), i).wait_recv())

    def share_done(base):
        group_loop(lambda i: share(base, o, i).wait_send())

    def vec_copy(buf, ss, rs, i, v):
        return wcopy(buf.at[v], buf.at[v], ss.at[i], rs.at[v], g * OWN + member(i))

    def vec_across(buf, ss, rs, i, v):
        ref = buf.at[OWN + v]
        return wcopy(ref, ref, ss.at[OWN + i], rs.at[OWN + v], lax.rem(g + i, groups) * OWN + o)

    def vec_send(*where):
        group_loop(lambda i: vec_copy(*where, i, o).start())

    def vec_sum(buf, ss, rs):
        group_loop(lambda i: vec_copy(buf, ss, rs, i, member(i)).wait_recv())
        zero = jnp.zeros(buf.shape[1:], F32)
        total = lax.fori_loop(0, OWN, lambda v, t: t + buf[v], zero)
        if groups > 1:
            buf[OWN + g] = total
            group_loop(lambda i: vec_across(buf, ss, rs, i, g).start(), 1, groups)
            group_loop(
                lambda i: vec_across(buf, ss, rs, i, lax.rem(g + i, groups)).wait_recv(), 1, groups
            )
            total = lax.fori_loop(0, groups, lambda v, t: t + buf[OWN + v], zero)
        return total

    def vec_done(buf, ss, rs):
        group_loop(lambda i: vec_copy(buf, ss, rs, i, o).wait_send())
        if groups > 1:
            group_loop(lambda i: vec_across(buf, ss, rs, i, g).wait_send(), 1, groups)

    def spread(m, x, t, target, sems, semr):
        ref = mom.at[m, pl.ds(pl.multiple_of(t * CW, CW), CW), :]
        return ncopy(ref, ref, sems.at[m, x], semr.at[m, x], target)

    dkT[...] = jnp.zeros_like(dkT)
    dvT[...] = jnp.zeros_like(dvT)
    lane = lax.broadcasted_iota(jnp.int32, (TB, CW), 1)
    low_lane = lane < HD

    def backward(i, _):
        t = rel(i)
        rr = rows(t, TB)

        @pl.when(i > 0)
        def _():
            for c in range(TB // MID):
                dst = dcr.at[pl.ds(pl.multiple_of(t * TB + c * MID, MID), MID)]
                ncopy(
                    dcst.at[pl.ds(c * MID, MID), mycols], dst, dc_sem.at[i, c], dc_rem.at[i, c], t
                ).wait_recv()

        dcs = (dcr[rr, :].astype(F32) * rln[rr, :]).astype(BF16)
        full = dcs.astype(F32)
        prod = full * ctxn[rr, :]
        delta = (
            jnp.sum(jnp.where(low_lane, prod, 0.0), axis=1, keepdims=True),
            jnp.sum(jnp.where(low_lane, 0.0, prod), axis=1, keepdims=True),
        )
        dcT = full.T.astype(BF16)
        for h in range(2):
            hs = slice(h * HD, (h + 1) * HD)
            top = delta[h].astype(BF16).astype(F32)
            tail = delta[h] - top
            base = (1 - h) * HD
            extra = jnp.where(lane == base, -top, jnp.where(lane == base + 1, -tail, 0.0))
            left = jnp.where(low_lane == (h == 0), full, extra).astype(BF16)
            s_ref[...] = mm(left, vTp[h])
            e = e_ref[h, rr, :]
            ds = e * s_ref[...].astype(BF16)
            gT[hs, rr] = (mm_nt(kTp[h, hs, :], ds) * 0.125).astype(BF16)
            dkT[hs, :] += mm(qT[hs, rr], ds)
            dvT[hs, :] += mm(dcT[hs, :], e)

        @pl.when(i == 0)
        def _():
            for k in (1, 0):
                ncopy(gst.at[n1], gr1.at[k], g1_s.at[k], g1_r.at[k], n1).wait_recv()
            gs2[...] = (gst[n2].astype(F32) + gr1[1].astype(F32)).astype(BF16)
            ncopy(gs2, gr2, g2_s, g2_r, n2).start()
            for x in (1, 2, 3):
                arrived(vecs.at[rel(x)], vn_s.at[x], vn_r.at[x], rel(x))
            vecw[o] = ((vecs[0] + vecs[1]) + vecs[2]) + vecs[3]
            vec_send(vecw, vw_s, vw_r)

        @pl.when(i == 2)
        def _():
            ncopy(gs2, gr2, g2_s, g2_r, n2).wait_recv()
            est[...] = (gst[n].astype(F32) + gr1[0].astype(F32) + gr2[...].astype(F32)).astype(BF16)
            scatter_all(est, erx, es_s, es_r)

        return 0

    lax.fori_loop(0, NAR, backward, 0)
    pending.append(ncopy(gs2, gr2, g2_s, g2_r, n2))
    gT[CW:2 * CW, :] = dkT[...].astype(BF16)
    gT[2 * CW:, :] = dvT[...].astype(BF16)

    gin = mm(gT[...], tok[...]).astype(BF16)
    for k in range(3):
        lst[k] = gin[k * CW:(k + 1) * CW]
    scatter_all(lst, lrx, ls_s, ls_r)
    one = jnp.ones((8, LEN), BF16)
    lv[o, 0:8, :] = mm_nt(one, gT[0:CW, :])
    lv[o, 8:16, :] = mm_nt(one, gT[2 * CW:, :])
    vec_send(lv, lv_s, lv_r)
    collect(3, est, erx, es_s, es_r)

    def dx(t):
        return mm(wqkv[...], gT[:, rows(t, TB)])

    dxs[1] = dx(n3).astype(BF16)
    start(ncopy(dxs.at[1], dxr1.at[1], dx1_s.at[1], dx1_r.at[1], n1))
    dxs[0] = dx(n1).astype(BF16)
    start(ncopy(dxs.at[0], dxr1.at[0], dx1_s.at[0], dx1_r.at[0], n1))
    over = dx(n2)
    ncopy(dxs.at[1], dxr1.at[1], dx1_s.at[1], dx1_r.at[1], n1).wait_recv()
    dxs2[...] = (over + dxr1[1].astype(F32)).astype(BF16)
    start(ncopy(dxs2, dxr2, dx2_s, dx2_r, n2))
    ograd[...] = dx(n).T + dr1[...]

    share_wait(3)

    def fan(base):
        for m in range(base, base + 3):
            start(spread(m, 1, n, n2, an_s, an_r))
            start(spread(m, 0, n, n1, an_s, an_r))

    def newton(m):
        xin = mom[m].astype(F32)
        norm = jnp.sqrt(jnp.sum(xin * xin)) + 1e-07
        xbuf[...] = xin / norm

        def step(_, c):
            x = xbuf[...]
            xl = x.astype(BF16)
            a = mm_nt(xl, xl)
            al = a.astype(BF16)
            p = (COEF_B * a + COEF_C * mm(al, al)).astype(BF16)
            xbuf[...] = COEF_A * x + mm(p, xl)
            return c

        lax.fori_loop(0, NS_ITERS, step, 0)
        orth[m] = xbuf[mycols, :]

    fan(3)
    collect(0, lst, lrx, ls_s, ls_r)
    for m in range(3, 6):
        spread(m, 1, n2, n2, an_s, an_r).wait_recv()
        start(spread(m, 0, n2, n1, ar_s, ar_r))
    share_wait(0)
    fan(0)
    for m in range(3, 6):
        spread(m, 0, n1, n1, an_s, an_r).wait_recv()
        spread(m, 0, n3, n1, ar_s, ar_r).wait_recv()

    def newton_late(m, c):
        newton(m)
        return c

    lax.fori_loop(3, 6, newton_late, 0)
    for m in range(0, 3):
        spread(m, 1, n2, n2, an_s, an_r).wait_recv()
        start(spread(m, 0, n2, n1, ar_s, ar_r))

    ncopy(dxs.at[0], dxr1.at[0], dx1_s.at[0], dx1_r.at[0], n1).wait_recv()
    ncopy(dxs2, dxr2, dx2_s, dx2_r, n2).wait_recv()
    ograd[...] = ograd[...] + (dxr1[0].astype(F32) + dxr2[...].astype(F32)).T
    l_ograd = pltpu.make_async_copy(ograd, ograd_h, loc_sem.at[7])
    l_ograd.start()

    for m in range(0, 3):
        spread(m, 0, n1, n1, an_s, an_r).wait_recv()
        spread(m, 0, n3, n1, ar_s, ar_r).wait_recv()
    l_mom = pltpu.make_async_copy(mom.at[:, mycols, :], omom_h, loc_sem.at[8])
    l_mom.start()
    lax.fori_loop(0, 3, newton_late, 0)
    l_orth = pltpu.make_async_copy(orth, oorth_h, loc_sem.at[9])
    l_orth.start()

    ovec[...] = vec_sum(vecw, vw_s, vw_r)
    ovec2[...] = vec_sum(lv, lv_s, lv_r)

    for c in pending:
        c.wait_send()
    vec_done(vecw, vw_s, vw_r)
    vec_done(lv, lv_s, lv_r)
    if groups > 1:
        for k in (0, 1):
            group_loop(lambda i: across(k, i).wait_send(), 1, groups)
    scatter_done(est, erx, es_s, es_r)
    scatter_done(lst, lrx, ls_s, ls_r)
    share_done(3)
    share_done(0)
    l_otok.wait()
    l_ograd.wait()
    l_mom.wait()
    l_orth.wait()


def run_layer(wide, tokens, cotangent, pay, in_w, out_w, in_m, out_m, shared, split):
    any_ = pl.BlockSpec(memory_space=pl.ANY)
    vm = pl.BlockSpec(memory_space=pltpu.VMEM)
    V = pltpu.VMEM
    dma = lambda *s: pltpu.SemaphoreType.DMA(s)
    one = pltpu.SemaphoreType.DMA
    groups = wide // OWN
    vslots = OWN + (groups if groups > 1 else 0)
    scratch = [
        V((LEN, D), BF16), V((TB, D), BF16), V((NAR, 16, CW), F32),
        V((4, D, CW), F32), V((2, CW, D), F32), V((6, CW, D), F32),
        V((3 * CW, D), BF16), V((D, 3 * CW), BF16),
        V((D, D), BF16), V((2, D, D), BF16), V((2, CW, CW), F32),
        V((2, LEN, 2 * CW), BF16), V((2, 2 * CW, LEN), BF16), V((2, CW, LEN), BF16), V((CW, LEN), BF16),
        V((LEN, CW), F32), V((TB, LEN), F32), V((2, LEN, LEN), BF16),
        V((LEN, CW), F32), V((LEN, CW), BF16), V((TB, D), BF16),
        V((TB, D), BF16), V((TB, D), BF16), V((TB, D), BF16), V((TB, D), BF16), V((TB, D), BF16),
        V((TB, D), F32), V((TB, D), BF16), V((LEN, CW), BF16),
        V((NAR, 8, D), F32), V((vslots, 8, D), F32), V((CW, LEN), F32), V((CW, LEN), F32), V((3 * CW, LEN), BF16),
        V((NAR, 3, CW, D), BF16), V((2, 3, CW, D), BF16), V((3, CW, D), BF16), V((3, CW, D), BF16),
        V((3, CW, D), BF16), V((OWN, 3, PR, D), BF16), V((3, CW, D), BF16), V((OWN, 3, PR, D), BF16),
        V((vslots, 16, CW), F32), V((6, D, D), BF16), V((2, groups if groups > 1 else 1, 3, PR, D), BF16),
        V((2, D, TB), BF16), V((2, D, TB), BF16), V((D, TB), BF16), V((D, TB), BF16),
        dma(10), dma(4), dma(4), dma(2), dma(2), dma(4), dma(4), dma(3, 2), dma(3, 2), dma(1, 2), dma(1, 2),
        dma(4), dma(4), dma(4, TB // MID), dma(4, TB // MID), dma(4), dma(4), dma(vslots), dma(vslots),
        dma(2), dma(2), one, one, dma(OWN), dma(OWN), dma(OWN), dma(OWN), dma(vslots), dma(vslots),
        dma(2, groups), dma(2, groups), dma(2, OWN), dma(2, OWN), dma(6, 2), dma(6, 2), dma(6, 2), dma(6, 2), dma(2), dma(2), one, one,
    ]
    return pl.pallas_call(
        functools.partial(layer_kernel, wide),
        out_shape=[
            jax.ShapeDtypeStruct((TB, D), BF16),
            jax.ShapeDtypeStruct((TB, D), F32),
            jax.ShapeDtypeStruct((6, CW, D), BF16),
            jax.ShapeDtypeStruct((6, CW, D), F32),
            jax.ShapeDtypeStruct((8, D), F32),
            jax.ShapeDtypeStruct((16, CW), F32),
        ],
        in_specs=[any_, any_, vm, any_, any_, any_, any_, vm, vm],
        out_specs=[any_, any_, any_, any_, vm, vm],
        scratch_shapes=scratch,
        compiler_params=pltpu.CompilerParams(
            collective_id=0, has_side_effects=True, vmem_limit_bytes=62 * MB
        ),
        name="layer",
    )(tokens, cotangent, pay, in_w, out_w, in_m, out_m, shared, split)


def muon_step(weights, orthogonal):
    return weights - 0.2 * (0.2 * math.sqrt(D) * orthogonal + 0.01 * weights)


def adam_step(values, moment_one, moment_two, gradient):
    moment_one = 0.9 * moment_one + 0.1 * gradient
    moment_two = 0.999 * moment_two + 0.001 * gradient * gradient
    step_ratio = (
        moment_one / (1.0 - 0.9**STEP) / (jnp.sqrt(moment_two / (1.0 - 0.999**STEP)) + 1e-08)
    )
    return (moment_one, moment_two, values - 0.3 * (step_ratio + 0.01 * values))


def blend(average, weights):
    return 0.6 * average + 0.4 * weights


def update_kernel(
    otok, ograd, mom, orth, in_w, out_w, in_a, out_a,
    tok_o, grad_o, inm_o, outm_o, inw_o, outw_o, inl_o, outl_o, ina_o, outa_o,
):
    tok_o[...] = otok[...]
    grad_o[...] = ograd[...]
    for k in range(4):
        inm_o[k] = mom[k].astype(F32).T
        new = muon_step(in_w[k], orth[k].T)
        inw_o[k] = new
        inl_o[k] = new.astype(BF16)
        ina_o[k] = blend(in_a[k], new)
    for k in range(2):
        outm_o[k] = mom[4 + k].astype(F32)
        new = muon_step(out_w[k], orth[4 + k])
        outw_o[k] = new
        outl_o[k] = new.astype(BF16)
        outa_o[k] = blend(out_a[k], new)


def run_update(otok, ograd, mom, orth, in_w, out_w, in_a, out_a):
    vm = pl.BlockSpec(memory_space=pltpu.VMEM)
    S = jax.ShapeDtypeStruct
    return pl.pallas_call(
        update_kernel,
        out_shape=[
            S((TB, D), BF16), S((TB, D), F32), S((4, D, CW), F32), S((2, CW, D), F32),
            S((4, D, CW), F32), S((2, CW, D), F32), S((4, D, CW), BF16), S((2, CW, D), BF16),
            S((4, D, CW), F32), S((2, CW, D), F32),
        ],
        in_specs=[vm] * 8,
        out_specs=[vm] * 10,
        compiler_params=pltpu.CompilerParams(vmem_limit_bytes=40 * MB),
        name="update",
    )(otok, ograd, mom, orth, in_w, out_w, in_a, out_a)


def body(
    wide, tokens, cotangent, segments, padding, generative, in_weights, out_weights, in_momenta,
    out_momenta, in_average, out_average, shared_values, shared_moment1, shared_moment2,
    shared_average, split_values, split_moment1, split_moment2, split_average,
):
    is_open = (padding == 0) & (generative == 0)
    pay = jnp.concatenate(
        [
            segments.reshape(TB // CW, CW).astype(F32),
            jnp.where(is_open, segments, -1).reshape(TB // CW, CW).astype(F32),
            split_values[2:3],
            jnp.zeros((7, CW), F32),
        ],
        axis=0,
    )
    otok, ograd, mom, orth, vec, vec2 = run_layer(
        wide, tokens, cotangent, pay, in_weights, out_weights, in_momenta, out_momenta,
        shared_values, split_values,
    )
    (
        result, grad_tokens, moment_in, moment_out, new_in, new_out, low_in, low_out, avg_in, avg_out,
    ) = run_update(otok, ograd, mom, orth, in_weights, out_weights, in_average, out_average)
    place = lax.axis_index("narrow") * CW
    sum_split = jnp.concatenate(
        [vec2[0:1], vec2[8:9], lax.dynamic_slice(vec, (6, place), (1, CW))], axis=0
    )
    shared_one, shared_two, shared_new = adam_step(
        shared_values, shared_moment1, shared_moment2, vec[:6]
    )
    split_one, split_two, split_new = adam_step(
        split_values, split_moment1, split_moment2, sum_split
    )
    return (
        result, grad_tokens, moment_in, moment_out, new_in, new_out, low_in, low_out, avg_in, avg_out,
        shared_one, shared_two, shared_new, blend(shared_average, shared_new),
        split_one, split_two, split_new, blend(split_average, split_new),
    )


def solution(mesh):
    rows = P(("wide", "narrow"), None)
    flat = P(("wide", "narrow"))
    cols = P(None, None, "narrow")
    outs = P(None, "narrow", None)
    vec = P(None, "narrow")
    return jax.shard_map(
        functools.partial(body, mesh.shape["wide"]),
        mesh=mesh,
        in_specs=(
            rows, rows, flat, flat, flat, cols, outs, cols, outs, cols, outs,
            P(), P(), P(), P(), vec, vec, vec, vec,
        ),
        out_specs=(
            rows, rows, cols, outs, cols, outs, cols, outs, cols, outs,
            P(), P(), P(), P(), vec, vec, vec, vec,
        ),
        check_vma=False,
    )
```

```python
import functools
import math

import jax
import jax.numpy as jnp
from jax import lax
from jax.experimental import pallas as pl
from jax.experimental.pallas import tpu as pltpu
from jax.sharding import PartitionSpec as P

D = 512
HD = 64
LEN = 2048
NS_ITERS = 3
STEP = 10
NAR = 4
TB = LEN // NAR
CW = D // NAR
OWN = 8
LINE = OWN // 2
HR = CW // 2
PR = CW // OWN
MID = 256

F32 = jnp.float32
BF16 = jnp.bfloat16
MESH = pl.DeviceIdType.MESH

COEF_A = 3.4445
COEF_B = -4.775
COEF_C = 2.0315
NEG = -1e30
MB = 2**20


def mm(a, b):
    return jnp.dot(a, b, preferred_element_type=F32)


def mm_nt(a, b):
    return lax.dot_general(a, b, (((1,), (1,)), ((), ())), preferred_element_type=F32)


def mm_tn(a, b):
    return lax.dot_general(a, b, (((0,), (0,)), ((), ())), preferred_element_type=F32)


def layer_kernel(wide, *refs):
    (
        tok_h, cot_h, seg_i, pad_i, gen_i, win_h, wout_h, min_h, mout_h, shared, split,
        otok_h, ograd_h, omom_h, oorth_h, ovec, ovec2,
        tok, cot, pay, win_f, wout_f, mT, wqkvT, wqkv, wup, wod, bcol,
        qp, kTp, vTp, qT, rdn, s_ref, e_ref, ctxn, ctx_s, ctxf,
        hr, act, du, dr2r, dr1r, dcst, dcr, vecs, vecw, dkT, dvT, gT,
        gst, gr1, es1, er1, zse, zre, yf, ybs, ybr, lr1, zs, zr, lv, mom, grp, grl,
        dxr1, dxr2,
        loc_sem, ag_s, ag_r, rly_s, rly_r, pay_s, pay_r, wg_s, wg_r, wr_s, wr_r,
        ctx_sem, ctx_rem, dc_sem, dc_rem, vn_s, vn_r, vw_s, vw_r, lv_s, lv_r,
        g1_s, g1_r, g2_s, g2_r, g3_s, g3_r, l1_s, l1_r, zs_s, zs_r, gp_s, gp_r,
        aq_s, aq_r, ap_s, ap_r, an_s, an_r, ar_s, ar_r, ow_s, ow_r, ez_s, ez_r, la_s, la_r, sw_s, sw_r, dx1_s, dx1_r, dx2_s, dx2_r,
    ) = refs
    n = lax.axis_index("narrow")
    w = lax.axis_index("wide")
    groups = wide // OWN
    g = w // OWN if groups > 1 else 0
    o = lax.rem(w, OWN) if groups > 1 else w
    b0 = lax.rem(n, 2)
    b1 = n // 2

    def rel(x):
        return lax.rem(b0 + x % 2, 2) + 2 * lax.rem(b1 + x // 2, 2)

    n1, n2, n3 = rel(1), rel(2), rel(3)

    def rows(t, size):
        return pl.ds(pl.multiple_of(t * size, size), size)

    def ncopy(src, dst, ssem, rsem, t):
        return pltpu.make_async_remote_copy(
            src_ref=src, dst_ref=dst, send_sem=ssem, recv_sem=rsem,
            device_id={"narrow": t}, device_id_type=MESH,
        )

    def wcopy(src, dst, ssem, rsem, u):
        return pltpu.make_async_remote_copy(
            src_ref=src, dst_ref=dst, send_sem=ssem, recv_sem=rsem,
            device_id={"wide": u}, device_id_type=MESH,
        )

    pending = []

    def start(copy):
        copy.start()
        pending.append(copy)
        return copy

    own = rows(n, TB)
    ograd = s_ref.at[:, 3 * D:4 * D]
    orth = mT
    rln = rdn
    otok = cot
    dxs, dxs2 = (act, du), dr2r

    l_tok = pltpu.make_async_copy(tok_h, tok.at[own], loc_sem.at[0])
    l_win = pltpu.make_async_copy(win_h, win_f, loc_sem.at[1])
    l_wout = pltpu.make_async_copy(wout_h, wout_f, loc_sem.at[2])
    l_cot = pltpu.make_async_copy(cot_h, cot, loc_sem.at[3])
    l_min = pltpu.make_async_copy(min_h, win_f, loc_sem.at[4])
    l_mout = pltpu.make_async_copy(mout_h, mT.at[pl.ds(4, 2)], loc_sem.at[5])
    for c in (l_tok, l_win, l_wout, l_cot, l_mout):
        c.start()

    barrier = pltpu.get_barrier_semaphore()
    for x in (1, 2, 3):
        pl.semaphore_signal(barrier, inc=1, device_id={"narrow": rel(x)}, device_id_type=MESH)

    def greet(i, c):
        pl.semaphore_signal(
            barrier, inc=1, device_id={"wide": g * OWN + lax.rem(o + i, OWN)}, device_id_type=MESH
        )
        return c

    lax.fori_loop(1, OWN, greet, 0)

    def greet_group(i, c):
        pl.semaphore_signal(
            barrier, inc=1, device_id={"wide": lax.rem(g + i, groups) * OWN + o}, device_id_type=MESH
        )
        return c

    if groups > 1:
        lax.fori_loop(1, groups, greet_group, 0)
    seg = seg_i[...]
    closed = jnp.logical_or(pad_i[...] != 0, gen_i[...] != 0)
    pay[n] = jnp.concatenate(
        [
            seg.astype(F32), jnp.where(closed, -1, seg).astype(F32),
            split[2:3, :], jnp.zeros((7, CW), F32),
        ],
        axis=0,
    )
    l_tok.wait()
    pl.semaphore_wait(barrier, 3 + (OWN - 1) + (groups - 1))

    half = TB // 2

    def ag_rows(t, c):
        return tok.at[pl.ds(pl.multiple_of(t * TB + c * half, half), half)]

    for x in (1, 2, 3):
        start(ncopy(pay.at[n], pay.at[n], pay_s.at[x], pay_r.at[x], rel(x)))
    for c in (0, 1):
        start(ncopy(ag_rows(n, c), ag_rows(n, c), ag_s.at[2 + c], ag_r.at[2 + c], n2))
    for c in (0, 1):
        start(ncopy(ag_rows(n, c), ag_rows(n, c), ag_s.at[c], ag_r.at[c], n1))

    def arrived(slot, sem_s, sem_r, t):
        ncopy(slot, slot, sem_s, sem_r, t).wait_recv()

    l_win.wait()
    for k in range(3):
        piece = win_f[k]
        wqkvT[k * CW:(k + 1) * CW, :] = piece.T.astype(BF16)
        wqkv[:, k * CW:(k + 1) * CW] = piece.astype(BF16)
    mycols = pl.ds(pl.multiple_of(n * CW, CW), CW)
    wup[:, mycols] = win_f[3].astype(BF16)
    l_min.start()
    l_wout.wait()
    for k in range(2):
        wod[k, mycols, :] = wout_f[k].astype(BF16)

    def wg_list(sems, semr, x, t, target):
        cols = pl.ds(pl.multiple_of(t * CW, CW), CW)
        return [
            ncopy(wod.at[:, cols, :], wod.at[:, cols, :], sems.at[x, 0], semr.at[x, 0], target),
            ncopy(wup.at[:, cols], wup.at[:, cols], sems.at[x, 1], semr.at[x, 1], target),
        ]

    for x in (2, 1):
        for c in wg_list(wg_s, wg_r, x, n, rel(x)):
            start(c)

    bcol[0] = jnp.broadcast_to(split[0:1, :], (CW, CW)).T
    bcol[1] = jnp.broadcast_to(split[1:2, :], (CW, CW)).T

    def project(t):
        tb = tok[rows(t, TB), :]
        qk = mm(tb, wqkv[:, 0:2 * CW])
        q = (qk[:, :CW] + split[0:1, :]).astype(BF16)
        k = qk[:, CW:].astype(BF16)
        q8 = q.astype(F32) * 0.125
        prod = q8 * k.astype(F32)
        lane = lax.broadcasted_iota(jnp.int32, (TB, CW), 1)
        low = lane < HD
        d0 = jnp.sum(jnp.where(low, prod, 0.0), axis=1, keepdims=True)
        d1 = jnp.sum(jnp.where(low, 0.0, prod), axis=1, keepdims=True)
        rdn[rows(t, TB), :] = jnp.where(low, d0, d1)
        lane1 = lax.broadcasted_iota(jnp.int32, (CW, CW), 1).astype(F32)
        for j in range(TB // CW):
            seg = jnp.broadcast_to(pay[t, j:j + 1, :], (CW, CW)).T
            part = q8[j * CW:(j + 1) * CW, :]
            lowj = lane1 < HD
            hot = lambda base: jnp.where(seg == lane1 + base, 1.0, 0.0)
            rr = pl.ds(pl.multiple_of(t * TB + j * CW, CW), CW)
            qp[0, rr, 0:CW] = jnp.where(lowj, part, hot(-float(HD))).astype(BF16)
            qp[1, rr, 0:CW] = jnp.where(lowj, hot(0.0), part).astype(BF16)
            rest = hot(float(HD)).astype(BF16)
            qp[0, rr, CW:] = rest
            qp[1, rr, CW:] = rest
        tT = mm_nt(wqkvT[...], tb)
        bq = jnp.concatenate([bcol[0]] * (TB // CW), axis=1)
        bv = jnp.concatenate([bcol[1]] * (TB // CW), axis=1)
        cols = rows(t, TB)
        qT[:, cols] = ((tT[0:CW] + bq).astype(BF16).astype(F32) * 0.125).astype(BF16)
        kT = tT[CW:2 * CW].astype(BF16)
        vT = (tT[2 * CW:] + bv).astype(BF16)
        code = jnp.concatenate([pay[t, 4 + j:5 + j, :] for j in range(TB // CW)], axis=1)
        rowi = lax.broadcasted_iota(jnp.int32, (HD, TB), 0).astype(F32)
        keep = lambda base: jnp.where(code == rowi + base, 0.0, NEG).astype(BF16)
        first, second, third = keep(0.0), keep(float(HD)), keep(float(2 * HD))
        ones = jnp.ones((HD, TB), BF16)
        kTp[0, 0:HD, cols] = kT[0:HD]
        kTp[0, HD:CW, cols] = first
        kTp[1, 0:HD, cols] = first
        kTp[1, HD:CW, cols] = kT[HD:]
        vTp[0, 0:HD, cols] = vT[0:HD]
        vTp[0, HD:, cols] = ones
        vTp[1, 0:HD, cols] = ones
        vTp[1, HD:, cols] = vT[HD:]
        for h in range(2):
            kTp[h, CW:CW + HD, cols] = second
            kTp[h, CW + HD:, cols] = third

    def project_step(i, _):
        @pl.when(i == 1)
        def _():
            arrived(pay.at[n1], pay_s.at[1], pay_r.at[1], n1)
            for c in (0, 1):
                arrived(ag_rows(n1, c), ag_s.at[c], ag_r.at[c], n1)
            l_min.wait()
            for k in range(4):
                mT[k] = win_f[k].T

        @pl.when(i == 2)
        def _():
            arrived(pay.at[n2], pay_s.at[2], pay_r.at[2], n2)
            arrived(pay.at[n3], pay_s.at[3], pay_r.at[3], n3)
            for c in (0, 1):
                arrived(ag_rows(n2, c), ag_s.at[2 + c], ag_r.at[2 + c], n2)
                ncopy(ag_rows(n2, c), ag_rows(n2, c), rly_s.at[c], rly_r.at[c], n1).start()

        @pl.when(i == 3)
        def _():
            for c in (0, 1):
                arrived(ag_rows(n3, c), rly_s.at[c], rly_r.at[c], n1)

        project(rel(i))
        return 0

    lax.fori_loop(0, NAR, project_step, 0)
    for c in (0, 1):
        pending.append(ncopy(ag_rows(n2, c), ag_rows(n2, c), rly_s.at[c], rly_r.at[c], n1))

    eye = lax.broadcasted_iota(jnp.int32, (CW, CW), 0) == lax.broadcasted_iota(jnp.int32, (CW, CW), 1)

    def ctx_copy(x, t):
        return ncopy(
            ctx_s.at[rows(t, TB)], ctxf.at[:, mycols], ctx_sem.at[x], ctx_rem.at[x], t
        )

    def attend(i, _):
        hi = 1 - i // 2
        lo = lax.rem((i + 1) // 2, 2)
        t = lax.rem(b0 + lo, 2) + 2 * lax.rem(b1 + hi, 2)
        rr = rows(t, TB)
        parts = []
        for h in range(2):
            s_ref[...] = mm(qp[h, rr, :], kTp[h])
            for j in range(TB // CW):
                cc = pl.ds(pl.multiple_of(t * TB + j * CW, CW), CW)
                diag = rdn[cc, h * HD:h * HD + 1]
                sub = pl.ds(j * CW, CW)
                s_ref[sub, cc] = jnp.where(eye, diag, s_ref[sub, cc])
            s = s_ref[...]
            top = jnp.max(s, axis=1, keepdims=True)
            e = jnp.exp(s - top).astype(BF16)
            e_ref[h, rr, :] = e
            parts.append(mm_nt(vTp[h], e))
        num = jnp.concatenate([parts[0][:HD], parts[1][HD:]], axis=0)
        den = 1.0 / jnp.concatenate([parts[0][HD:], parts[1][:HD]], axis=0)
        cn = (num * den).T
        ctxn[rr, :] = cn
        rln[rr, :] = den.T
        ctx_s[rr, :] = cn.astype(BF16)

        @pl.when(i < 3)
        def _():
            x = lo + 2 * hi
            ctx_copy(x, t).start()

        @pl.when(i == 0)
        def _():
            for c in wg_list(wg_s, wg_r, 2, n2, n2):
                c.wait_recv()
            for c in wg_list(wr_s, wr_r, 0, n2, n1):
                c.start()

        return 0

    lax.fori_loop(0, NAR, attend, 0)
    pending.extend(wg_list(wr_s, wr_r, 0, n2, n1))
    for x in (1, 2, 3):
        pending.append(ctx_copy(x, rel(x)))
    ctxf[:, mycols] = ctx_s[own, :]
    for c in wg_list(wg_s, wg_r, 1, n1, n1):
        c.wait_recv()
    for c in wg_list(wr_s, wr_r, 0, n3, n1):
        c.wait_recv()
    l_cot.wait()
    l_mout.wait()
    for x in (2, 3, 1):
        cols = pl.ds(pl.multiple_of(rel(x) * CW, CW), CW)
        ncopy(ctx_s.at[own], ctxf.at[:, cols], ctx_sem.at[x], ctx_rem.at[x], rel(x)).wait_recv()

    up_bias = jnp.concatenate([pay[t, 8:9, :] for t in range(NAR)], axis=1)
    vecs[n] = jnp.zeros((8, D), F32)

    def dc_copy(x, c, t, me):
        rr = pl.ds(c * MID, MID)
        cols = pl.ds(pl.multiple_of(t * CW, CW), CW)
        dst = dcr.at[pl.ds(pl.multiple_of(me * TB + c * MID, MID), MID)]
        return ncopy(dcst.at[rr, cols], dst, dc_sem.at[x, c], dc_rem.at[x, c], t)

    def middle(c, _):
        rr = pl.ds(pl.multiple_of(c * MID, MID), MID)
        ga1, be1, ga2, be2, ba, bd = (shared[k:k + 1, :] for k in range(6))
        x0 = tok[pl.ds(pl.multiple_of(n * TB + c * MID, MID), MID), :].astype(F32)
        r1 = x0 + (mm(ctxf[rr, :], wod[0]) + ba)
        c1 = r1 - jnp.mean(r1, axis=1, keepdims=True)
        s1 = lax.rsqrt(jnp.mean(c1 * c1, axis=1, keepdims=True) + 1e-05)
        x1 = c1 * s1
        hidden = x1 * ga1 + be1
        low = hidden.astype(BF16)
        hr[rr, :] = low
        upper = mm(low, wup[...]) + up_bias
        cdf = 0.5 * (1.0 + lax.erf(upper * (1.0 / math.sqrt(2.0))))
        pdf = jnp.exp(-0.5 * upper * upper) * (1.0 / math.sqrt(2.0 * math.pi))
        slope = cdf + upper * pdf
        a = (upper * cdf).astype(BF16)
        act[rr, :] = a
        r2 = hidden + (mm(a, wod[1]) + bd)
        c2 = r2 - jnp.mean(r2, axis=1, keepdims=True)
        s2 = lax.rsqrt(jnp.mean(c2 * c2, axis=1, keepdims=True) + 1e-05)
        x2 = c2 * s2
        dy = cot[rr, :].astype(F32)
        otok[rr, :] = (x2 * ga2 + be2).astype(BF16)
        dn = dy * ga2
        dr2 = s2 * (
            dn - jnp.mean(dn, axis=1, keepdims=True) - x2 * jnp.mean(dn * x2, axis=1, keepdims=True)
        )
        d2 = dr2.astype(BF16)
        dr2r[rr, :] = d2
        dup = (mm_nt(d2, wod[1]) * slope).astype(BF16)
        du[rr, :] = dup
        dh = dr2 + mm_nt(dup, wup[...])
        en = dh * ga1
        d1f = s1 * (
            en - jnp.mean(en, axis=1, keepdims=True) - x1 * jnp.mean(en * x1, axis=1, keepdims=True)
        )
        for k in range(NAR):
            win_f[k, rr, :] = d1f[:, k * CW:(k + 1) * CW]
        d1 = d1f.astype(BF16)
        dr1r[rr, :] = d1
        dcst[rr, :] = mm_nt(d1, wod[0]).astype(BF16)
        add = lambda v: jnp.sum(v, axis=0, keepdims=True)
        vecs[n] += jnp.concatenate(
            [
                add(dh * x1), add(dh), add(dy * x2), add(dy), add(d1f), add(dr2),
                add(dup.astype(F32)), jnp.zeros((1, D), F32),
            ],
            axis=0,
        )
        for k in range(TB // MID):
            @pl.when(c == k)
            def _():
                for x in (2, 3, 1):
                    dc_copy(x, k, rel(x), n).start()

        dcr[pl.ds(pl.multiple_of(n * TB + c * MID, MID), MID), :] = dcst[rr, mycols]
        return 0

    lax.fori_loop(0, TB // MID, middle, 0)
    for x in (1, 2, 3):
        for c in range(TB // MID):
            pending.append(dc_copy(x, c, rel(x), n))
    l_otok = pltpu.make_async_copy(otok, otok_h, loc_sem.at[6])
    l_otok.start()
    for x in (1, 2, 3):
        start(ncopy(vecs.at[n], vecs.at[n], vn_s.at[x], vn_r.at[x], rel(x)))

    for k, (left, right) in enumerate(((du, hr), (ctxf, dr1r), (act, dr2r))):
        grad = mm_tn(left[...], right[...]).astype(BF16)
        for t in range(NAR):
            gst[k, t % 2, t // 2] = grad[t * CW:(t + 1) * CW]
        start(ncopy(gst.at[k, 1 - b0], gr1.at[k], g1_s.at[k], g1_r.at[k], n1))

    def loop(fn, first, count):
        def go(i, c):
            fn(i)
            return c

        lax.fori_loop(first, count, go, 0)

    def group_loop(fn, first=1, count=OWN):
        loop(fn, first, count)

    def member(i):
        return lax.rem(o + i, OWN)

    pb = lax.rem(o, 2)
    qa = o // 2
    pair = g * OWN + 2 * qa + (1 - pb)

    def line(i):
        return lax.rem(qa + i, LINE)

    def line_dev(u):
        return g * OWN + 2 * u + pb

    keep = pl.ds(pl.multiple_of(pb * HR, HR), HR)
    away = pl.ds(pl.multiple_of((1 - pb) * HR, HR), HR)

    def at_rows(first, size):
        return pl.ds(pl.multiple_of(b0 * CW + first, PR), size)

    def batch(k):
        return pl.ds(k, 1)

    def z_copy(k, i):
        u = line(i)
        src = zs.at[batch(k), pl.ds(pl.multiple_of(u * PR, PR), PR), :]
        return wcopy(src, zr.at[qa, batch(k)], zs_s.at[k, i], zs_r.at[k, qa], line_dev(u))

    def z_scatter(k):
        loop(lambda i: z_copy(k, i).start(), 1, LINE)

    def across(k, i):
        ref = grl.at[g, batch(k)]
        return wcopy(ref, ref, gp_s.at[k, i], gp_r.at[k, g], lax.rem(g + i, groups) * OWN + o)

    def share(k, u, i):
        ref = mom.at[batch(k), b1, at_rows(pb * HR + u * PR, PR), :]
        return wcopy(ref, ref, aq_s.at[k, i], aq_r.at[k, u], line_dev(line(i)))

    def z_collect(k):
        bt = batch(k)
        zr[qa, bt] = zs[bt, pl.ds(pl.multiple_of(qa * PR, PR), PR), :]

        def take(i):
            v = line(i)
            wcopy(zr.at[v, bt], zr.at[v, bt], zs_s.at[k, 0], zs_r.at[k, v], line_dev(v)).wait_recv()

        loop(take, 1, LINE)
        total = zr[0, bt].astype(F32)
        for v in range(1, LINE):
            total = total + zr[v, bt].astype(F32)
        if groups > 1:
            grl[g, bt] = total.astype(BF16)
            loop(lambda i: across(k, i).start(), 1, groups)

            def meet(i):
                v = lax.rem(g + i, groups)
                ref = grl.at[v, bt]
                wcopy(ref, ref, gp_s.at[k, i], gp_r.at[k, v], v * OWN + o).wait_recv()

            loop(meet, 1, groups)
            total = lax.fori_loop(
                0, groups, lambda v, t: t + grl[v, bt].astype(F32), jnp.zeros_like(total)
            )
        mine = pl.ds(pl.multiple_of(pb * HR + qa * PR, PR), PR)
        total = total + 0.5 * mT[bt, mine, :]
        mom[bt, b1, at_rows(pb * HR + qa * PR, PR), :] = total.astype(BF16)
        loop(lambda i: share(k, qa, i).start(), 1, LINE)

    def half_copy(k, b):
        ref = mom.at[batch(k), b1, at_rows(b * HR, HR), :]
        return wcopy(ref, ref, ap_s.at[k], ap_r.at[k], pair)

    def half_send(k):
        loop(lambda i: share(k, line(i), i).wait_recv(), 1, LINE)
        half_copy(k, pb).start()

    def spread(k, x, t, target, sems, semr):
        ref = quarter(k, t)
        return ncopy(ref, ref, sems.at[x], semr.at[x], target)

    def quarter(k, t):
        return mom.at[k, t // 2, pl.ds(pl.multiple_of(lax.rem(t, 2) * CW, CW), CW), :]

    def late_fan(m):
        half_copy(m, 1 - pb).wait_recv()
        if m < 2:
            @pl.when(b0 != m)
            def _():
                near_copy(m).start()

            start(far_copy(m))
        else:
            start(spread(2, 1, n, n2, an_s, an_r))
            start(spread(2, 0, n, n1, an_s, an_r))

    def near_copy(m):
        return ncopy(quarter(m, n), quarter(m, n), la_s.at[m, 0], la_r.at[n], m + 2 * b1)

    def far_copy(m):
        return ncopy(quarter(m, n), quarter(m, n), la_s.at[m, 1], la_r.at[n], m + 2 * (1 - b1))

    def late_wait():
        for x in (1, 2, 3):
            t = rel(x)
            ncopy(quarter(b0, t), quarter(b0, t), la_s.at[0, 0], la_r.at[t], t).wait_recv()

    def relay(k):
        spread(k, 1, n2, n2, an_s, an_r).wait_recv()
        start(spread(k, 0, n2, n1, ar_s, ar_r))

    def gathered(k):
        spread(k, 0, n1, n1, an_s, an_r).wait_recv()
        spread(k, 0, n3, n1, ar_s, ar_r).wait_recv()

    def vec_copy(buf, ss, rs, i, v):
        return wcopy(buf.at[v], buf.at[v], ss.at[i], rs.at[v], g * OWN + member(i))

    def vec_across(buf, ss, rs, i, v):
        ref = buf.at[OWN + v]
        return wcopy(ref, ref, ss.at[OWN + i], rs.at[OWN + v], lax.rem(g + i, groups) * OWN + o)

    def vec_send(*where):
        group_loop(lambda i: vec_copy(*where, i, o).start())

    def vec_sum(buf, ss, rs):
        group_loop(lambda i: vec_copy(buf, ss, rs, i, member(i)).wait_recv())
        zero = jnp.zeros(buf.shape[1:], F32)
        total = lax.fori_loop(0, OWN, lambda v, t: t + buf[v], zero)
        if groups > 1:
            buf[OWN + g] = total
            group_loop(lambda i: vec_across(buf, ss, rs, i, g).start(), 1, groups)
            group_loop(
                lambda i: vec_across(buf, ss, rs, i, lax.rem(g + i, groups)).wait_recv(), 1, groups
            )
            total = lax.fori_loop(0, groups, lambda v, t: t + buf[OWN + v], zero)
        return total

    def vec_done(buf, ss, rs):
        group_loop(lambda i: vec_copy(buf, ss, rs, i, o).wait_send())
        if groups > 1:
            group_loop(lambda i: vec_across(buf, ss, rs, i, g).wait_send(), 1, groups)

    def pair_copy(m):
        return wcopy(es1.at[m], er1.at[m], g2_s.at[m], g2_r.at[m], pair)

    def chip_sum(m, part):
        return gst[m, b0, :, part, :].astype(F32) + gr1[m, :, part, :].astype(F32)

    def early_pair(m):
        ncopy(gst.at[m, b0], gr1.at[m], g1_s.at[m], g1_r.at[m], n1).wait_recv()
        es1[m] = chip_sum(m, away).astype(BF16)
        start(pair_copy(m))

    def e_line(m, i):
        u = line(i)
        src = zse.at[m, :, pl.ds(pl.multiple_of(u * PR, PR), PR), :]
        return wcopy(src, zre.at[m, qa], ez_s.at[m, i], ez_r.at[m, qa], line_dev(u))

    def early_line(m):
        pair_copy(m).wait_recv()
        zse[m] = (chip_sum(m, keep) + er1[m].astype(F32)).astype(BF16)
        loop(lambda i: e_line(m, i).start(), 1, LINE)

    def e_across(m, i):
        ref = grp.at[g, m]
        return wcopy(ref, ref, gp_s.at[3 + m, i], gp_r.at[3 + m, g], lax.rem(g + i, groups) * OWN + o)

    def over_copy(m):
        return ncopy(ybs.at[m], ybr.at[m], g3_s.at[m], g3_r.at[m], n2)

    def early_over(m):
        zre[m, qa] = zse[m, :, pl.ds(pl.multiple_of(qa * PR, PR), PR), :]

        def take(i):
            v = line(i)
            ref = zre.at[m, v]
            wcopy(ref, ref, ez_s.at[m, 0], ez_r.at[m, v], line_dev(v)).wait_recv()

        loop(take, 1, LINE)
        total = zre[m, 0].astype(F32)
        for v in range(1, LINE):
            total = total + zre[m, v].astype(F32)
        if groups > 1:
            grp[g, m] = total.astype(BF16)
            loop(lambda i: e_across(m, i).start(), 1, groups)

            def meet(i):
                v = lax.rem(g + i, groups)
                ref = grp.at[v, m]
                wcopy(ref, ref, gp_s.at[3 + m, i], gp_r.at[3 + m, v], v * OWN + o).wait_recv()

            loop(meet, 1, groups)
            total = lax.fori_loop(
                0, groups, lambda v, t: t + grp[v, m].astype(F32), jnp.zeros_like(total)
            )
        mine = pl.ds(pl.multiple_of(pb * HR + qa * PR, PR), PR)
        old = 0.5 * mT[3 + m, mine, :]
        for y in range(2):
            part = total[y] + jnp.where(b1 == y, old, 0.0)
            yf[m, y] = part
            ybs[m, y] = part.astype(BF16)
        start(over_copy(m))

    def e_share(m, u, i):
        ref = mom.at[3 + m, :, at_rows(pb * HR + u * PR, PR), :]
        return wcopy(ref, ref, aq_s.at[3 + m, i], aq_r.at[3 + m, u], line_dev(line(i)))

    def early_back(m):
        over_copy(m).wait_recv()
        mom[3 + m, :, at_rows(pb * HR + qa * PR, PR), :] = (yf[m] + ybr[m].astype(F32)).astype(BF16)
        loop(lambda i: e_share(m, qa, i).start(), 1, LINE)

    def e_half(m, b):
        ref = mom.at[3 + m, :, at_rows(b * HR, HR), :]
        return wcopy(ref, ref, ap_s.at[3 + m], ap_r.at[3 + m], pair)

    def early_half(m):
        loop(lambda i: e_share(m, line(i), i).wait_recv(), 1, LINE)
        start(e_half(m, pb))

    def e_near(m, c):
        ref = mom.at[3 + m, :, pl.ds(pl.multiple_of(c * CW, CW), CW), :]
        return ncopy(ref, ref, ow_s.at[m], ow_r.at[m], n1)

    def early_near(m):
        e_half(m, 1 - pb).wait_recv()
        start(e_near(m, b0))

    def early_got(m):
        e_near(m, 1 - b0).wait_recv()

    def vec_early():
        for x in (1, 2, 3):
            arrived(vecs.at[rel(x)], vn_s.at[x], vn_r.at[x], rel(x))
        vecw[o] = ((vecs[0] + vecs[1]) + vecs[2]) + vecs[3]
        vec_send(vecw, vw_s, vw_r)

    plan = {
        0: [(early_pair, 0), (early_pair, 1), (early_pair, 2)],
        1: [(lambda m: vec_early(), 0)],
        2: [(early_line, 0)],
        3: [(early_line, 1)],
        4: [(early_over, 0)],
        5: [(early_line, 2), (early_over, 1)],
        6: [(early_back, 0)],
        7: [(early_back, 1), (early_over, 2)],
    }

    dkT[...] = jnp.zeros_like(dkT)
    dvT[...] = jnp.zeros_like(dvT)
    lane = lax.broadcasted_iota(jnp.int32, (TB, CW), 1)
    low_lane = lane < HD

    def after(k):
        held = len(pending)
        for fn, arg in plan.get(k, ()):
            fn(arg)
        del pending[held:]

    def backward(i, _):
        t = rel(i)
        rr = rows(t, TB)

        @pl.when(i > 0)
        def _():
            for c in range(TB // MID):
                dst = dcr.at[pl.ds(pl.multiple_of(t * TB + c * MID, MID), MID)]
                ncopy(
                    dcst.at[pl.ds(c * MID, MID), mycols], dst, dc_sem.at[i, c], dc_rem.at[i, c], t
                ).wait_recv()

        dcs = (dcr[rr, :].astype(F32) * rln[rr, :]).astype(BF16)
        full = dcs.astype(F32)
        prod = full * ctxn[rr, :]
        delta = (
            jnp.sum(jnp.where(low_lane, prod, 0.0), axis=1, keepdims=True),
            jnp.sum(jnp.where(low_lane, 0.0, prod), axis=1, keepdims=True),
        )
        dcT = full.T.astype(BF16)
        for h in range(2):
            hs = slice(h * HD, (h + 1) * HD)
            top = delta[h].astype(BF16).astype(F32)
            tail = delta[h] - top
            base = (1 - h) * HD
            extra = jnp.where(lane == base, -top, jnp.where(lane == base + 1, -tail, 0.0))
            left = jnp.where(low_lane == (h == 0), full, extra).astype(BF16)
            s_ref[...] = mm(left, vTp[h])
            e = e_ref[h, rr, :]
            ds = e * s_ref[...].astype(BF16)
            gT[hs, rr] = (mm_nt(kTp[h, hs, :], ds) * 0.125).astype(BF16)
            dkT[hs, :] += mm(qT[hs, rr], ds)
            dvT[hs, :] += mm(dcT[hs, :], e)
            for k in range(NAR):
                pl.when(i == k)(functools.partial(after, 2 * k + h))

        return 0

    lax.fori_loop(0, NAR, backward, 0)
    gT[CW:2 * CW, :] = dkT[...].astype(BF16)
    gT[2 * CW:, :] = dvT[...].astype(BF16)

    def late_pair(m):
        src = dr1r.at[pl.ds(pl.multiple_of(m * CW + (1 - pb) * HR, HR), HR)]
        return wcopy(src, lr1.at[m], l1_s.at[m], l1_r.at[m], pair)

    for m in range(3):
        dr1r[m * CW:(m + 1) * CW, :] = mm(gT[m * CW:(m + 1) * CW, :], tok[...]).astype(BF16)
        start(late_pair(m))
    one = jnp.ones((8, LEN), BF16)
    lv[o, 0:8, :] = mm_nt(one, gT[0:CW, :])
    lv[o, 8:16, :] = mm_nt(one, gT[2 * CW:, :])
    vec_send(lv, lv_s, lv_r)
    def dx(t):
        return mm(wqkv[...], gT[:, rows(t, TB)])

    def late_line(m):
        late_pair(m).wait_recv()
        kept = dr1r[pl.ds(pl.multiple_of(m * CW + pb * HR, HR), HR), :]
        zs[m] = (kept.astype(F32) + lr1[m].astype(F32)).astype(BF16)
        z_scatter(m)

    def newton_begin(m, j):
        xin = mom[m].reshape(D, D).astype(F32)
        s_ref[:, j * D:(j + 1) * D] = xin * (1.0 / (jnp.sqrt(jnp.sum(xin * xin)) + 1e-07))

    def newton_step(j):
        xb = s_ref.at[:, j * D:(j + 1) * D]
        x = xb[...]
        xl = x.astype(BF16)
        a = mm_nt(xl, xl)
        al = a.astype(BF16)
        p = (COEF_B * a + COEF_C * mm(al, al)).astype(BF16)
        xb[...] = COEF_A * x + mm(p, xl)

    def newton_last(j, part):
        xb = s_ref.at[:, j * D:(j + 1) * D]
        xl = xb[...].astype(BF16)
        xo = xb[part, :]
        a = mm_nt(xo.astype(BF16), xl).astype(BF16)
        y = mm(a, xl)
        z = mm_nt(y.astype(BF16), xl).astype(BF16)
        return COEF_A * xo + COEF_B * y + COEF_C * mm(z, xl)

    def newton(m, j, part):
        newton_begin(m, j)
        for _ in range(NS_ITERS - 1):
            newton_step(j)
        return newton_last(j, part)

    dxs[1][...] = dx(n3).astype(BF16)
    start(ncopy(dxs[1], dxr1.at[1], dx1_s.at[1], dx1_r.at[1], n1))
    dxs[0][...] = dx(n1).astype(BF16)
    start(ncopy(dxs[0], dxr1.at[0], dx1_s.at[0], dx1_r.at[0], n1))
    early_back(2)
    late_line(0)
    late_line(1)
    late_line(2)
    early_half(0)
    over = dx(n2)
    ncopy(dxs[1], dxr1.at[1], dx1_s.at[1], dx1_r.at[1], n1).wait_recv()
    dxs2[...] = (over + dxr1[1].astype(F32)).astype(BF16)
    start(ncopy(dxs2, dxr2, dx2_s, dx2_r, n2))
    early_half(1)
    z_collect(0)
    early_near(0)
    early_half(2)
    z_collect(1)
    early_near(1)
    dxo = dx(n).T
    for k in range(NAR):
        cols = slice(k * CW, (k + 1) * CW)
        ograd[:, cols] = dxo[:, cols] + win_f[k]
    z_collect(2)
    early_near(2)
    early_got(0)
    early_got(1)

    both = pl.ds(pl.multiple_of(b1 * 2 * CW, 2 * CW), 2 * CW)

    def swap(m, k):
        return ncopy(dkT.at[:, k * D:(k + 1) * D], orth.at[m], sw_s.at[k], sw_r.at[k], n1)

    def give(base, k, res):
        first, second = res[0:CW], res[CW:]
        orth[base + b0] = jnp.where(b0 == 0, first, second)
        dkT[:, k * D:(k + 1) * D] = jnp.where(b0 == 0, second, first)
        start(swap(base + b0, k))

    newton_begin(3 + b0, 0)
    half_send(0)
    newton_step(0)
    half_send(1)
    half_send(2)
    newton_step(0)
    late_fan(0)
    late_fan(1)
    give(3, 1, newton_last(0, both))
    late_fan(2)
    early_got(2)
    newton_begin(5, 1)
    newton_step(1)
    newton_step(1)
    orth[5] = newton_last(1, mycols)
    relay(2)

    ncopy(dxs[0], dxr1.at[0], dx1_s.at[0], dx1_r.at[0], n1).wait_recv()
    ncopy(dxs2, dxr2, dx2_s, dx2_r, n2).wait_recv()
    ograd[...] = ograd[...] + (dxr1[0].astype(F32) + dxr2[...].astype(F32)).T
    l_ograd = pltpu.make_async_copy(ograd, ograd_h, loc_sem.at[7])
    l_ograd.start()

    late_wait()
    give(0, 0, newton(b0, 0, both))
    gathered(2)
    l_mom = pltpu.make_async_copy(
        mom.at[:, b1, pl.ds(pl.multiple_of(b0 * CW, CW), CW), :], omom_h, loc_sem.at[8]
    )
    l_mom.start()
    orth[2] = newton(2, 1, mycols)
    swap(4 - b0, 1).wait_recv()
    swap(1 - b0, 0).wait_recv()
    l_orth = pltpu.make_async_copy(orth, oorth_h, loc_sem.at[9])
    l_orth.start()

    ovec[...] = vec_sum(vecw, vw_s, vw_r)
    late = vec_sum(lv, lv_s, lv_r)
    ovec2[0:1, :] = late[0:1]
    ovec2[1:2, :] = late[8:9]
    ovec2[2:3, :] = ovec[6:7, mycols]
    ovec2[3:8, :] = jnp.zeros((5, CW), F32)

    for m in range(3):
        pending.extend((pair_copy(m), over_copy(m)))
    for m in range(2):
        @pl.when(b0 != m)
        def _():
            near_copy(m).wait_send()

    for c in pending:
        c.wait_send()
    vec_done(vecw, vw_s, vw_r)
    vec_done(lv, lv_s, lv_r)
    for k in range(3):
        half_copy(k, pb).wait_send()
        loop(lambda i: z_copy(k, i).wait_send(), 1, LINE)
        loop(lambda i: share(k, qa, i).wait_send(), 1, LINE)
        loop(lambda i: e_line(k, i).wait_send(), 1, LINE)
        loop(lambda i: e_share(k, qa, i).wait_send(), 1, LINE)
        if groups > 1:
            loop(lambda i: across(k, i).wait_send(), 1, groups)
            loop(lambda i: e_across(k, i).wait_send(), 1, groups)
    l_otok.wait()
    l_ograd.wait()
    l_mom.wait()
    l_orth.wait()


def run_layer(wide, tokens, cotangent, seg, pad, gen, in_w, out_w, in_m, out_m, shared, split):
    any_ = pl.BlockSpec(memory_space=pl.ANY)
    vm = pl.BlockSpec(memory_space=pltpu.VMEM)
    V = pltpu.VMEM
    dma = lambda *s: pltpu.SemaphoreType.DMA(s)
    one = pltpu.SemaphoreType.DMA
    groups = wide // OWN
    vslots = OWN + (groups if groups > 1 else 0)
    scratch = [
        V((LEN, D), BF16), V((TB, D), BF16), V((NAR, 16, CW), F32),
        V((4, D, CW), F32), V((2, CW, D), F32), V((6, CW, D), F32),
        V((3 * CW, D), BF16), V((D, 3 * CW), BF16),
        V((D, D), BF16), V((2, D, D), BF16), V((2, CW, CW), F32),
        V((2, LEN, 2 * CW), BF16), V((2, 2 * CW, LEN), BF16), V((2, CW, LEN), BF16), V((CW, LEN), BF16),
        V((LEN, CW), F32), V((TB, LEN), F32), V((2, LEN, LEN), BF16),
        V((LEN, CW), F32), V((LEN, CW), BF16), V((TB, D), BF16),
        V((TB, D), BF16), V((TB, D), BF16), V((TB, D), BF16), V((TB, D), BF16), V((TB, D), BF16),
        V((TB, D), BF16), V((LEN, CW), BF16),
        V((NAR, 8, D), F32), V((vslots, 8, D), F32), V((CW, LEN), F32), V((CW, LEN), F32), V((3 * CW, LEN), BF16),
        V((3, 2, 2, CW, D), BF16), V((3, 2, CW, D), BF16), V((3, 2, HR, D), BF16), V((3, 2, HR, D), BF16),
        V((3, 2, HR, D), BF16), V((3, LINE, 2, PR, D), BF16), V((3, 2, PR, D), F32), V((3, 2, PR, D), BF16),
        V((3, 2, PR, D), BF16), V((3, HR, D), BF16),
        V((3, HR, D), BF16), V((LINE, 3, PR, D), BF16), V((vslots, 16, CW), F32), V((6, 2, D // 2, D), BF16),
        V((groups, 3, 2, PR, D) if groups > 1 else (1, 1, 1, PR, D), BF16),
        V((groups, 3, PR, D) if groups > 1 else (1, 1, PR, D), BF16),
        V((2, D, TB), BF16), V((D, TB), BF16),
        dma(10), dma(4), dma(4), dma(2), dma(2), dma(4), dma(4), dma(3, 2), dma(3, 2), dma(1, 2), dma(1, 2),
        dma(4), dma(4), dma(4, TB // MID), dma(4, TB // MID), dma(4), dma(4), dma(vslots), dma(vslots),
        dma(vslots), dma(vslots),
        dma(3), dma(3), dma(3), dma(3), dma(3), dma(3), dma(3), dma(3), dma(3, LINE), dma(3, LINE),
        dma(6, groups), dma(6, groups),
        dma(6, LINE), dma(6, LINE), dma(6), dma(6), dma(2), dma(2), dma(2), dma(2),
        dma(3), dma(3), dma(3, LINE), dma(3, LINE), dma(2, 2), dma(4), dma(2), dma(2),
        dma(2), dma(2), one, one,
    ]
    return pl.pallas_call(
        functools.partial(layer_kernel, wide),
        out_shape=[
            jax.ShapeDtypeStruct((TB, D), BF16),
            jax.ShapeDtypeStruct((TB, D), F32),
            jax.ShapeDtypeStruct((6, CW, D), BF16),
            jax.ShapeDtypeStruct((6, CW, D), F32),
            jax.ShapeDtypeStruct((8, D), F32),
            jax.ShapeDtypeStruct((8, CW), F32),
        ],
        in_specs=[any_, any_, vm, vm, vm, any_, any_, any_, any_, vm, vm],
        out_specs=[any_, any_, any_, any_, vm, vm],
        scratch_shapes=scratch,
        compiler_params=pltpu.CompilerParams(
            collective_id=0, has_side_effects=True, vmem_limit_bytes=62 * MB
        ),
        name="layer",
    )(tokens, cotangent, seg, pad, gen, in_w, out_w, in_m, out_m, shared, split)


def muon_step(weights, orthogonal):
    return weights - 0.2 * (0.2 * math.sqrt(D) * orthogonal + 0.01 * weights)


def adam_step(values, moment_one, moment_two, gradient):
    moment_one = 0.9 * moment_one + 0.1 * gradient
    moment_two = 0.999 * moment_two + 0.001 * gradient * gradient
    step_ratio = (
        moment_one / (1.0 - 0.9**STEP) / (jnp.sqrt(moment_two / (1.0 - 0.999**STEP)) + 1e-08)
    )
    return (moment_one, moment_two, values - 0.3 * (step_ratio + 0.01 * values))


def blend(average, weights):
    return 0.6 * average + 0.4 * weights


def update_kernel(
    otok, ograd, mom, orth, in_w, out_w, in_a, out_a, vec, vec2,
    sv, s1, s2, sa, pv, p1, p2, pa,
    tok_o, grad_o, inm_o, outm_o, inw_o, outw_o, inl_o, outl_o, ina_o, outa_o,
    s1_o, s2_o, sv_o, sa_o, p1_o, p2_o, pv_o, pa_o,
    mom_b, orth_b, inw_b, outw_b, ina_b, outa_b,
    inm_v, outm_v, inw_v, outw_v, inl_v, outl_v, ina_v, outa_v, grad_v, tok_v, thru, rsem, wsem,
):
    whole = [
        pltpu.make_async_copy(ograd, grad_v, thru.at[0]),
        pltpu.make_async_copy(otok, tok_v, thru.at[1]),
    ]
    back = [
        pltpu.make_async_copy(grad_v, grad_o, thru.at[2]),
        pltpu.make_async_copy(tok_v, tok_o, thru.at[3]),
    ]
    reads, writes = [], []
    for k in range(6):
        j, inner = (k, True) if k < 4 else (k - 4, False)
        srcs = (mom.at[k], orth.at[k], (in_w if inner else out_w).at[j], (in_a if inner else out_a).at[j])
        dsts = (
            mom_b.at[k], orth_b.at[k], (inw_b if inner else outw_b).at[j], (ina_b if inner else outa_b).at[j],
        )
        reads.append([pltpu.make_async_copy(s, d, rsem.at[k, i]) for i, (s, d) in enumerate(zip(srcs, dsts))])
        bufs = (inm_v, inw_v, inl_v, ina_v) if inner else (outm_v, outw_v, outl_v, outa_v)
        outs = (inm_o, inw_o, inl_o, ina_o) if inner else (outm_o, outw_o, outl_o, outa_o)
        writes.append(
            [pltpu.make_async_copy(s.at[j], d.at[j], wsem.at[k, i]) for i, (s, d) in enumerate(zip(bufs, outs))]
        )
    for c in reads[0]:
        c.start()
    for c in reads[1]:
        c.start()
    for c in whole:
        c.start()
    for k in range(2, 6):
        for c in reads[k]:
            c.start()
    s1_o[...], s2_o[...], shared_new = adam_step(sv[...], s1[...], s2[...], vec[0:6, :])
    sv_o[...] = shared_new
    sa_o[...] = blend(sa[...], shared_new)
    p1_o[...], p2_o[...], split_new = adam_step(pv[...], p1[...], p2[...], vec2[0:3, :])
    pv_o[...] = split_new
    pa_o[...] = blend(pa[...], split_new)
    for k in range(6):
        if k in (1, 2):
            whole[k - 1].wait()
            back[k - 1].start()
        for c in reads[k]:
            c.wait()
        if k < 4:
            inm_v[k] = mom_b[k].astype(F32).T
            new = muon_step(inw_b[k], orth_b[k].T)
            inw_v[k] = new
            inl_v[k] = new.astype(BF16)
            ina_v[k] = blend(ina_b[k], new)
        else:
            j = k - 4
            outm_v[j] = mom_b[k].astype(F32)
            new = muon_step(outw_b[j], orth_b[k])
            outw_v[j] = new
            outl_v[j] = new.astype(BF16)
            outa_v[j] = blend(outa_b[j], new)
        for c in writes[k]:
            c.start()
    for c in back:
        c.wait()
    for k in range(6):
        for c in writes[k]:
            c.wait()


def run_update(*args):
    vm = pl.BlockSpec(memory_space=pltpu.VMEM)
    any_ = pl.BlockSpec(memory_space=pl.ANY)
    S = jax.ShapeDtypeStruct
    V = pltpu.VMEM
    inner, outer = (4, D, CW), (2, CW, D)
    return pl.pallas_call(
        update_kernel,
        out_shape=[
            S((TB, D), BF16), S((TB, D), F32), S(inner, F32), S(outer, F32), S(inner, F32), S(outer, F32),
            S(inner, BF16), S(outer, BF16), S(inner, F32), S(outer, F32),
        ]
        + [S((6, D), F32)] * 4
        + [S((3, CW), F32)] * 4,
        in_specs=[any_] * 8 + [vm] * 10,
        out_specs=[any_] * 10 + [vm] * 8,
        scratch_shapes=[
            V((6, CW, D), BF16), V((6, CW, D), F32), V(inner, F32), V(outer, F32), V(inner, F32), V(outer, F32),
            V(inner, F32), V(outer, F32), V(inner, F32), V(outer, F32), V(inner, BF16), V(outer, BF16),
            V(inner, F32), V(outer, F32), V((TB, D), F32), V((TB, D), BF16),
            pltpu.SemaphoreType.DMA((4,)), pltpu.SemaphoreType.DMA((6, 4)), pltpu.SemaphoreType.DMA((6, 4)),
        ],
        compiler_params=pltpu.CompilerParams(vmem_limit_bytes=60 * MB),
        name="update",
    )(*args)


def body(
    wide, tokens, cotangent, segments, padding, generative, in_weights, out_weights, in_momenta,
    out_momenta, in_average, out_average, shared_values, shared_moment1, shared_moment2,
    shared_average, split_values, split_moment1, split_moment2, split_average,
):
    flags = [v.reshape(TB // CW, CW) for v in (segments, padding, generative)]
    otok, ograd, mom, orth, vec, vec2 = run_layer(
        wide, tokens, cotangent, *flags, in_weights, out_weights, in_momenta, out_momenta,
        shared_values, split_values,
    )
    return tuple(
        run_update(
            otok, ograd, mom, orth, in_weights, out_weights, in_average, out_average, vec, vec2,
            shared_values, shared_moment1, shared_moment2, shared_average,
            split_values, split_moment1, split_moment2, split_average,
        )
    )


def solution(mesh):
    rows = P(("wide", "narrow"), None)
    flat = P(("wide", "narrow"))
    cols = P(None, None, "narrow")
    outs = P(None, "narrow", None)
    vec = P(None, "narrow")
    return jax.shard_map(
        functools.partial(body, mesh.shape["wide"]),
        mesh=mesh,
        in_specs=(
            rows, rows, flat, flat, flat, cols, outs, cols, outs, cols, outs,
            P(), P(), P(), P(), vec, vec, vec, vec,
        ),
        out_specs=(
            rows, rows, cols, outs, cols, outs, cols, outs, cols, outs,
            P(), P(), P(), P(), vec, vec, vec, vec,
        ),
        check_vma=False,
    )
```

```python
import functools
import math

import jax
import jax.numpy as jnp
from jax import lax
from jax.experimental import pallas as pl
from jax.experimental.pallas import tpu as pltpu
from jax.sharding import PartitionSpec as P

D = 512
HD = 64
LEN = 2048
NS_ITERS = 3
STEP = 10
NAR = 4
TB = LEN // NAR
CW = D // NAR
OWN = 8
LINE = OWN // 2
HR = CW // 2
HC = D // 2
PR = CW // OWN
MID = 256

F32 = jnp.float32
BF16 = jnp.bfloat16
MESH = pl.DeviceIdType.MESH

COEF_A = 3.4445
COEF_B = -4.775
COEF_C = 2.0315
NEG = -1e30
MB = 2**20


def mm(a, b):
    return jnp.dot(a, b, preferred_element_type=F32)


def mm_nt(a, b):
    return lax.dot_general(a, b, (((1,), (1,)), ((), ())), preferred_element_type=F32)


def mm_tn(a, b):
    return lax.dot_general(a, b, (((0,), (0,)), ((), ())), preferred_element_type=F32)


def layer_kernel(wide, *refs):
    (
        tok_h, cot_h, seg_i, pad_i, gen_i, win_h, wout_h, min_h, mout_h, shared, split,
        otok_h, ograd_h, omom_h, oorth_h, ovec, ovec2,
        tok, cot, pay, win_f, wout_f, mT, wqkvT, wqkv, wup, wod, bcol,
        qp, kTp, vTp, qT, rdn, s_ref, e_ref, ctxn, ctx_s, ctxf,
        hr, act, du, dr2r, dr1r, dcst, dcr, vecs, vecw, dkT, dvT, gT,
        gst, gr1, eys, eyr, es1, er1, zse, zre, lr1, zs, zr, zd, zdr, lv, mom, grp, grl,
        dxr1, dxr2,
        loc_sem, ag_s, ag_r, rly_s, rly_r, pay_s, pay_r, wg_s, wg_r, wr_s, wr_r,
        ctx_sem, ctx_rem, dc_sem, dc_rem, vn_s, vn_r, vw_s, vw_r, lv_s, lv_r,
        g1_s, g1_r, g2_s, g2_r, g3_s, g3_r, l1_s, l1_r, zs_s, zs_r, zd_s, zd_r, ad_s, ad_r, gp_s, gp_r,
        aq_s, aq_r, ap_s, ap_r, ow_s, ow_r, ez_s, ez_r, ey_s, ey_r, la_s, la_r, sw_s, sw_r, dx1_s, dx1_r, dx2_s, dx2_r,
    ) = refs
    n = lax.axis_index("narrow")
    w = lax.axis_index("wide")
    groups = wide // OWN
    g = w // OWN if groups > 1 else 0
    o = lax.rem(w, OWN) if groups > 1 else w
    b0 = lax.rem(n, 2)
    b1 = n // 2

    def rel(x):
        return lax.rem(b0 + x % 2, 2) + 2 * lax.rem(b1 + x // 2, 2)

    n1, n2, n3 = rel(1), rel(2), rel(3)

    def rows(t, size):
        return pl.ds(pl.multiple_of(t * size, size), size)

    def ncopy(src, dst, ssem, rsem, t):
        return pltpu.make_async_remote_copy(
            src_ref=src, dst_ref=dst, send_sem=ssem, recv_sem=rsem,
            device_id={"narrow": t}, device_id_type=MESH,
        )

    def wcopy(src, dst, ssem, rsem, u):
        return pltpu.make_async_remote_copy(
            src_ref=src, dst_ref=dst, send_sem=ssem, recv_sem=rsem,
            device_id={"wide": u}, device_id_type=MESH,
        )

    pending = []

    def start(copy):
        copy.start()
        pending.append(copy)
        return copy

    own = rows(n, TB)
    ograd = s_ref.at[:, 3 * D:4 * D]
    orth = mT
    rln = rdn
    otok = cot
    dxs, dxs2 = (act, du), dr2r

    l_tok = pltpu.make_async_copy(tok_h, tok.at[own], loc_sem.at[0])
    l_win = pltpu.make_async_copy(win_h, win_f, loc_sem.at[1])
    l_wout = pltpu.make_async_copy(wout_h, wout_f, loc_sem.at[2])
    l_cot = pltpu.make_async_copy(cot_h, cot, loc_sem.at[3])
    l_min = pltpu.make_async_copy(min_h, win_f, loc_sem.at[4])
    l_mout = pltpu.make_async_copy(mout_h, mT.at[pl.ds(4, 2)], loc_sem.at[5])
    for c in (l_tok, l_win, l_wout, l_cot, l_mout):
        c.start()

    barrier = pltpu.get_barrier_semaphore()
    for x in (1, 2, 3):
        pl.semaphore_signal(barrier, inc=1, device_id={"narrow": rel(x)}, device_id_type=MESH)

    def greet(i, c):
        pl.semaphore_signal(
            barrier, inc=1, device_id={"wide": g * OWN + lax.rem(o + i, OWN)}, device_id_type=MESH
        )
        return c

    lax.fori_loop(1, OWN, greet, 0)

    def greet_group(i, c):
        pl.semaphore_signal(
            barrier, inc=1, device_id={"wide": lax.rem(g + i, groups) * OWN + o}, device_id_type=MESH
        )
        return c

    if groups > 1:
        lax.fori_loop(1, groups, greet_group, 0)
    seg = seg_i[...]
    closed = jnp.logical_or(pad_i[...] != 0, gen_i[...] != 0)
    pay[n] = jnp.concatenate(
        [
            seg.astype(F32), jnp.where(closed, -1, seg).astype(F32),
            split[2:3, :], jnp.zeros((7, CW), F32),
        ],
        axis=0,
    )
    l_tok.wait()
    pl.semaphore_wait(barrier, 3 + (OWN - 1) + (groups - 1))

    half = TB // 2

    def ag_rows(t, c):
        return tok.at[pl.ds(pl.multiple_of(t * TB + c * half, half), half)]

    for x in (1, 2, 3):
        start(ncopy(pay.at[n], pay.at[n], pay_s.at[x], pay_r.at[x], rel(x)))
    for c in (0, 1):
        start(ncopy(ag_rows(n, c), ag_rows(n, c), ag_s.at[2 + c], ag_r.at[2 + c], n2))
    for c in (0, 1):
        start(ncopy(ag_rows(n, c), ag_rows(n, c), ag_s.at[c], ag_r.at[c], n1))

    def arrived(slot, sem_s, sem_r, t):
        ncopy(slot, slot, sem_s, sem_r, t).wait_recv()

    l_win.wait()
    for k in range(3):
        piece = win_f[k]
        wqkvT[k * CW:(k + 1) * CW, :] = piece.T.astype(BF16)
        wqkv[:, k * CW:(k + 1) * CW] = piece.astype(BF16)
    mycols = pl.ds(pl.multiple_of(n * CW, CW), CW)
    wup[:, mycols] = win_f[3].astype(BF16)
    l_min.start()
    l_wout.wait()
    for k in range(2):
        wod[k, mycols, :] = wout_f[k].astype(BF16)

    def wg_list(sems, semr, x, t, target):
        cols = pl.ds(pl.multiple_of(t * CW, CW), CW)
        return [
            ncopy(wod.at[:, cols, :], wod.at[:, cols, :], sems.at[x, 0], semr.at[x, 0], target),
            ncopy(wup.at[:, cols], wup.at[:, cols], sems.at[x, 1], semr.at[x, 1], target),
        ]

    bcol[0] = jnp.broadcast_to(split[0:1, :], (CW, CW)).T
    bcol[1] = jnp.broadcast_to(split[1:2, :], (CW, CW)).T

    def project(t):
        tb = tok[rows(t, TB), :]
        qk = mm(tb, wqkv[:, 0:2 * CW])
        q = (qk[:, :CW] + split[0:1, :]).astype(BF16)
        k = qk[:, CW:].astype(BF16)
        q8 = q.astype(F32) * 0.125
        prod = q8 * k.astype(F32)
        lane = lax.broadcasted_iota(jnp.int32, (TB, CW), 1)
        low = lane < HD
        d0 = jnp.sum(jnp.where(low, prod, 0.0), axis=1, keepdims=True)
        d1 = jnp.sum(jnp.where(low, 0.0, prod), axis=1, keepdims=True)
        rdn[rows(t, TB), :] = jnp.where(low, d0, d1)
        lane1 = lax.broadcasted_iota(jnp.int32, (CW, CW), 1).astype(F32)
        for j in range(TB // CW):
            seg = jnp.broadcast_to(pay[t, j:j + 1, :], (CW, CW)).T
            part = q8[j * CW:(j + 1) * CW, :]
            lowj = lane1 < HD
            hot = lambda base: jnp.where(seg == lane1 + base, 1.0, 0.0)
            rr = pl.ds(pl.multiple_of(t * TB + j * CW, CW), CW)
            qp[0, rr, 0:CW] = jnp.where(lowj, part, hot(-float(HD))).astype(BF16)
            qp[1, rr, 0:CW] = jnp.where(lowj, hot(0.0), part).astype(BF16)
            rest = hot(float(HD)).astype(BF16)
            qp[0, rr, CW:] = rest
            qp[1, rr, CW:] = rest
        tT = mm_nt(wqkvT[...], tb)
        bq = jnp.concatenate([bcol[0]] * (TB // CW), axis=1)
        bv = jnp.concatenate([bcol[1]] * (TB // CW), axis=1)
        cols = rows(t, TB)
        qT[:, cols] = ((tT[0:CW] + bq).astype(BF16).astype(F32) * 0.125).astype(BF16)
        kT = tT[CW:2 * CW].astype(BF16)
        vT = (tT[2 * CW:] + bv).astype(BF16)
        code = jnp.concatenate([pay[t, 4 + j:5 + j, :] for j in range(TB // CW)], axis=1)
        rowi = lax.broadcasted_iota(jnp.int32, (HD, TB), 0).astype(F32)
        keep = lambda base: jnp.where(code == rowi + base, 0.0, NEG).astype(BF16)
        first, second, third = keep(0.0), keep(float(HD)), keep(float(2 * HD))
        ones = jnp.ones((HD, TB), BF16)
        kTp[0, 0:HD, cols] = kT[0:HD]
        kTp[0, HD:CW, cols] = first
        kTp[1, 0:HD, cols] = first
        kTp[1, HD:CW, cols] = kT[HD:]
        vTp[0, 0:HD, cols] = vT[0:HD]
        vTp[0, HD:, cols] = ones
        vTp[1, 0:HD, cols] = ones
        vTp[1, HD:, cols] = vT[HD:]
        for h in range(2):
            kTp[h, CW:CW + HD, cols] = second
            kTp[h, CW + HD:, cols] = third

    def project_step(i, _):
        @pl.when(i == 1)
        def _():
            arrived(pay.at[n1], pay_s.at[1], pay_r.at[1], n1)
            for c in (0, 1):
                arrived(ag_rows(n1, c), ag_s.at[c], ag_r.at[c], n1)
            l_min.wait()
            for k in range(4):
                mT[k] = win_f[k].T

        @pl.when(i == 2)
        def _():
            arrived(pay.at[n2], pay_s.at[2], pay_r.at[2], n2)
            arrived(pay.at[n3], pay_s.at[3], pay_r.at[3], n3)
            for c in (0, 1):
                arrived(ag_rows(n2, c), ag_s.at[2 + c], ag_r.at[2 + c], n2)
                ncopy(ag_rows(n2, c), ag_rows(n2, c), rly_s.at[c], rly_r.at[c], n1).start()
            for x in (2, 1):
                for c in wg_list(wg_s, wg_r, x, n, rel(x)):
                    c.start()

        @pl.when(i == 3)
        def _():
            for c in (0, 1):
                arrived(ag_rows(n3, c), rly_s.at[c], rly_r.at[c], n1)

        project(rel(i))
        return 0

    lax.fori_loop(0, NAR, project_step, 0)
    for x in (2, 1):
        pending.extend(wg_list(wg_s, wg_r, x, n, rel(x)))
    for c in (0, 1):
        pending.append(ncopy(ag_rows(n2, c), ag_rows(n2, c), rly_s.at[c], rly_r.at[c], n1))

    eye = lax.broadcasted_iota(jnp.int32, (CW, CW), 0) == lax.broadcasted_iota(jnp.int32, (CW, CW), 1)

    def ctx_copy(x, t):
        return ncopy(
            ctx_s.at[rows(t, TB)], ctxf.at[:, mycols], ctx_sem.at[x], ctx_rem.at[x], t
        )

    def attend(i, _):
        hi = 1 - i // 2
        lo = lax.rem((i + 1) // 2, 2)
        t = lax.rem(b0 + lo, 2) + 2 * lax.rem(b1 + hi, 2)
        rr = rows(t, TB)
        parts = []
        for h in range(2):
            s_ref[...] = mm(qp[h, rr, :], kTp[h])
            for j in range(TB // CW):
                cc = pl.ds(pl.multiple_of(t * TB + j * CW, CW), CW)
                diag = rdn[cc, h * HD:h * HD + 1]
                sub = pl.ds(j * CW, CW)
                s_ref[sub, cc] = jnp.where(eye, diag, s_ref[sub, cc])
            s = s_ref[...]
            top = jnp.max(s, axis=1, keepdims=True)
            e = jnp.exp(s - top).astype(BF16)
            e_ref[h, rr, :] = e
            parts.append(mm_nt(vTp[h], e))
        num = jnp.concatenate([parts[0][:HD], parts[1][HD:]], axis=0)
        den = 1.0 / jnp.concatenate([parts[0][HD:], parts[1][:HD]], axis=0)
        cn = (num * den).T
        ctxn[rr, :] = cn
        rln[rr, :] = den.T
        ctx_s[rr, :] = cn.astype(BF16)

        @pl.when(i < 3)
        def _():
            x = lo + 2 * hi
            ctx_copy(x, t).start()

        @pl.when(i == 2)
        def _():
            for c in wg_list(wg_s, wg_r, 2, n2, n2):
                c.wait_recv()
            for c in wg_list(wr_s, wr_r, 0, n2, n1):
                c.start()

        return 0

    lax.fori_loop(0, NAR, attend, 0)
    pending.extend(wg_list(wr_s, wr_r, 0, n2, n1))
    for x in (1, 2, 3):
        pending.append(ctx_copy(x, rel(x)))
    ctxf[:, mycols] = ctx_s[own, :]
    for c in wg_list(wg_s, wg_r, 1, n1, n1):
        c.wait_recv()
    for c in wg_list(wr_s, wr_r, 0, n3, n1):
        c.wait_recv()
    l_cot.wait()
    l_mout.wait()
    for x in (2, 3, 1):
        cols = pl.ds(pl.multiple_of(rel(x) * CW, CW), CW)
        ncopy(ctx_s.at[own], ctxf.at[:, cols], ctx_sem.at[x], ctx_rem.at[x], rel(x)).wait_recv()

    up_bias = jnp.concatenate([pay[t, 8:9, :] for t in range(NAR)], axis=1)
    vecs[n] = jnp.zeros((8, D), F32)

    def dc_copy(x, c, t, me):
        rr = pl.ds(c * MID, MID)
        cols = pl.ds(pl.multiple_of(t * CW, CW), CW)
        dst = dcr.at[pl.ds(pl.multiple_of(me * TB + c * MID, MID), MID)]
        return ncopy(dcst.at[rr, cols], dst, dc_sem.at[x, c], dc_rem.at[x, c], t)

    def middle(c, _):
        rr = pl.ds(pl.multiple_of(c * MID, MID), MID)
        ga1, be1, ga2, be2, ba, bd = (shared[k:k + 1, :] for k in range(6))
        x0 = tok[pl.ds(pl.multiple_of(n * TB + c * MID, MID), MID), :].astype(F32)
        r1 = x0 + (mm(ctxf[rr, :], wod[0]) + ba)
        c1 = r1 - jnp.mean(r1, axis=1, keepdims=True)
        s1 = lax.rsqrt(jnp.mean(c1 * c1, axis=1, keepdims=True) + 1e-05)
        x1 = c1 * s1
        hidden = x1 * ga1 + be1
        low = hidden.astype(BF16)
        hr[rr, :] = low
        upper = mm(low, wup[...]) + up_bias
        cdf = 0.5 * (1.0 + lax.erf(upper * (1.0 / math.sqrt(2.0))))
        pdf = jnp.exp(-0.5 * upper * upper) * (1.0 / math.sqrt(2.0 * math.pi))
        slope = cdf + upper * pdf
        a = (upper * cdf).astype(BF16)
        act[rr, :] = a
        r2 = hidden + (mm(a, wod[1]) + bd)
        c2 = r2 - jnp.mean(r2, axis=1, keepdims=True)
        s2 = lax.rsqrt(jnp.mean(c2 * c2, axis=1, keepdims=True) + 1e-05)
        x2 = c2 * s2
        dy = cot[rr, :].astype(F32)
        otok[rr, :] = (x2 * ga2 + be2).astype(BF16)
        dn = dy * ga2
        dr2 = s2 * (
            dn - jnp.mean(dn, axis=1, keepdims=True) - x2 * jnp.mean(dn * x2, axis=1, keepdims=True)
        )
        d2 = dr2.astype(BF16)
        dr2r[rr, :] = d2
        dup = (mm_nt(d2, wod[1]) * slope).astype(BF16)
        du[rr, :] = dup
        dh = dr2 + mm_nt(dup, wup[...])
        en = dh * ga1
        d1f = s1 * (
            en - jnp.mean(en, axis=1, keepdims=True) - x1 * jnp.mean(en * x1, axis=1, keepdims=True)
        )
        for k in range(NAR):
            win_f[k, rr, :] = d1f[:, k * CW:(k + 1) * CW]
        d1 = d1f.astype(BF16)
        dr1r[rr, :] = d1
        dcst[rr, :] = mm_nt(d1, wod[0]).astype(BF16)
        add = lambda v: jnp.sum(v, axis=0, keepdims=True)
        vecs[n] += jnp.concatenate(
            [
                add(dh * x1), add(dh), add(dy * x2), add(dy), add(d1f), add(dr2),
                add(dup.astype(F32)), jnp.zeros((1, D), F32),
            ],
            axis=0,
        )
        for k in range(TB // MID):
            @pl.when(c == k)
            def _():
                for x in (2, 3, 1):
                    dc_copy(x, k, rel(x), n).start()

        dcr[pl.ds(pl.multiple_of(n * TB + c * MID, MID), MID), :] = dcst[rr, mycols]
        return 0

    lax.fori_loop(0, TB // MID, middle, 0)
    for x in (1, 2, 3):
        for c in range(TB // MID):
            pending.append(dc_copy(x, c, rel(x), n))
    l_otok = pltpu.make_async_copy(otok, otok_h, loc_sem.at[6])
    l_otok.start()
    for x in (1, 2, 3):
        start(ncopy(vecs.at[n], vecs.at[n], vn_s.at[x], vn_r.at[x], rel(x)))

    for k, (left, right) in enumerate(((du, hr), (ctxf, dr1r), (act, dr2r))):
        grad = mm_tn(left[...], right[...]).astype(BF16)
        for t in range(NAR):
            gst[k, t % 2, t // 2] = grad[t * CW:(t + 1) * CW]
        start(ncopy(gst.at[k, 1 - b0], gr1.at[k], g1_s.at[k], g1_r.at[k], n1))

    def loop(fn, first, count):
        def go(i, c):
            fn(i)
            return c

        lax.fori_loop(first, count, go, 0)

    def group_loop(fn, first=1, count=OWN):
        loop(fn, first, count)

    def member(i):
        return lax.rem(o + i, OWN)

    pb = lax.rem(o, 2)
    qa = o // 2
    pair = g * OWN + 2 * qa + (1 - pb)

    def line(i):
        return lax.rem(qa + i, LINE)

    def line_dev(u):
        return g * OWN + 2 * u + pb

    keep = pl.ds(pl.multiple_of(pb * HR, HR), HR)
    away = pl.ds(pl.multiple_of((1 - pb) * HR, HR), HR)

    keepc = pl.ds(pl.multiple_of(pb * HC, HC), HC)
    awayc = pl.ds(pl.multiple_of((1 - pb) * HC, HC), HC)

    def piece(v):
        return pl.ds(pl.multiple_of(v * PR, PR), PR)

    def unit_rows(u):
        return pl.ds(u * CW, CW)

    def unit_mom(u, part, cols):
        if u == 0:
            return mom.at[2, b1, b0, :, part, cols]
        return mom.at[pl.ds(0, 2), b1, b0, u - 1, part, cols]

    def l1_copy(u):
        return wcopy(dr1r.at[unit_rows(u), awayc], lr1.at[u], l1_s.at[u], l1_r.at[u], pair)

    def l1(u, lhs):
        dr1r[unit_rows(u), :] = mm(lhs, tok[...]).astype(BF16)
        start(l1_copy(u))

    def z_copy(u, i):
        v = line(i)
        return wcopy(zs.at[u, :, piece(v), :], zr.at[u, qa], zs_s.at[u, i], zs_r.at[u, qa], line_dev(v))

    def owned(u, total):
        if groups > 1:
            grl[g, u] = total.astype(BF16)
            loop(lambda i: across(u, i).start(), 1, groups)

            def meet(i):
                v = lax.rem(g + i, groups)
                ref = grl.at[v, u]
                wcopy(ref, ref, gp_s.at[u, i], gp_r.at[u, v], v * OWN + o).wait_recv()

            loop(meet, 1, groups)
            total = lax.fori_loop(
                0, groups, lambda v, t: t + grl[v, u].astype(F32), jnp.zeros_like(total)
            )
        for k in range(2):
            m, first = (2, k * HR) if u == 0 else (k, (u - 1) * HR)
            old = mT[m, pl.ds(pl.multiple_of(first + qa * PR, PR), PR), keepc]
            new = (total[k] + 0.5 * old).astype(BF16)
            if u == 0:
                mom[2, b1, b0, k, piece(qa), keepc] = new
            else:
                mom[k, b1, b0, u - 1, piece(qa), keepc] = new

    def half_cols(b):
        return pl.ds(pl.multiple_of(b * HC, HC), HC)

    def d1_copy(i):
        v = member(i)
        src = zd.at[:, piece(v // 2), half_cols(lax.rem(v, 2))]
        return wcopy(src, zdr.at[o], zd_s.at[i], zd_r.at[o], g * OWN + v)

    def d1(lhs):
        zd[...] = mm(lhs, tok[...]).astype(BF16).reshape(2, HR, D)
        group_loop(lambda i: d1_copy(i).start())

    def d2_copy(v, i):
        ref = unit_mom(2, piece(v // 2), half_cols(lax.rem(v, 2)))
        return wcopy(ref, ref, ad_s.at[i], ad_r.at[v], g * OWN + member(i))

    def d2():
        zdr[o] = zd[:, piece(qa), keepc]

        def take(i):
            v = member(i)
            wcopy(zdr.at[v], zdr.at[v], zd_s.at[0], zd_r.at[v], g * OWN + v).wait_recv()

        group_loop(take)
        total = zdr[0].astype(F32)
        for v in range(1, OWN):
            total = total + zdr[v].astype(F32)
        owned(2, total)
        group_loop(lambda i: d2_copy(o, i).start())

    def l2(u):
        l1_copy(u).wait_recv()
        both = dr1r[unit_rows(u), keepc].astype(F32) + lr1[u].astype(F32)
        zs[u] = both.astype(BF16).reshape(2, HR, HC)
        loop(lambda i: z_copy(u, i).start(), 1, LINE)

    def across(u, i):
        ref = grl.at[g, u]
        return wcopy(ref, ref, gp_s.at[u, i], gp_r.at[u, g], lax.rem(g + i, groups) * OWN + o)

    def share(u, v, i):
        ref = unit_mom(u, piece(v), keepc)
        return wcopy(ref, ref, aq_s.at[u, i], aq_r.at[u, v], line_dev(line(i)))

    def l3(u):
        zr[u, qa] = zs[u, :, piece(qa), :]

        def take(i):
            v = line(i)
            wcopy(zr.at[u, v], zr.at[u, v], zs_s.at[u, 0], zs_r.at[u, v], line_dev(v)).wait_recv()

        loop(take, 1, LINE)
        total = zr[u, 0].astype(F32)
        for v in range(1, LINE):
            total = total + zr[u, v].astype(F32)
        owned(u, total)
        loop(lambda i: share(u, qa, i).start(), 1, LINE)

    def half_copy(u, cols):
        ref = unit_mom(u, pl.ds(0, HR), cols)
        return wcopy(ref, ref, ap_s.at[u], ap_r.at[u], pair)

    def l4(u):
        loop(lambda i: share(u, line(i), i).wait_recv(), 1, LINE)
        half_copy(u, keepc).start()

    fans = {0: [(0, 2, 1)], 1: [(1, 0, 0), (2, 1, 1)], 2: [(3, 0, 0), (4, 1, 1)]}

    def fan_ref(u, m, t):
        low = lax.rem(t, 2)
        return mom.at[2, t // 2, low] if u == 0 else mom.at[m, t // 2, low, u - 1]

    def near_copy(u, f, m, c):
        return ncopy(fan_ref(u, m, n), fan_ref(u, m, n), la_s.at[f, 0], la_r.at[f, n], c + 2 * b1)

    def far_copy(u, f, m, c):
        return ncopy(fan_ref(u, m, n), fan_ref(u, m, n), la_s.at[f, 1], la_r.at[f, n], c + 2 * (1 - b1))

    def l5(u):
        if u < 2:
            half_copy(u, awayc).wait_recv()
        else:
            group_loop(lambda i: d2_copy(member(i), i).wait_recv())
        for f, m, c in fans[u]:
            far_copy(u, f, m, c).start()

            @pl.when(b0 != c)
            def _():
                near_copy(u, f, m, c).start()

    def fan_wait(u, f, m):
        for x in (1, 2, 3):
            t = rel(x)
            ncopy(fan_ref(u, m, t), fan_ref(u, m, t), la_s.at[0, 0], la_r.at[f, t], t).wait_recv()

    def vec_copy(buf, ss, rs, i, v):
        return wcopy(buf.at[v], buf.at[v], ss.at[i], rs.at[v], g * OWN + member(i))

    def vec_across(buf, ss, rs, i, v):
        ref = buf.at[OWN + v]
        return wcopy(ref, ref, ss.at[OWN + i], rs.at[OWN + v], lax.rem(g + i, groups) * OWN + o)

    def vec_send(*where):
        group_loop(lambda i: vec_copy(*where, i, o).start())

    def vec_sum(buf, ss, rs):
        group_loop(lambda i: vec_copy(buf, ss, rs, i, member(i)).wait_recv())
        zero = jnp.zeros(buf.shape[1:], F32)
        total = lax.fori_loop(0, OWN, lambda v, t: t + buf[v], zero)
        if groups > 1:
            buf[OWN + g] = total
            group_loop(lambda i: vec_across(buf, ss, rs, i, g).start(), 1, groups)
            group_loop(
                lambda i: vec_across(buf, ss, rs, i, lax.rem(g + i, groups)).wait_recv(), 1, groups
            )
            total = lax.fori_loop(0, groups, lambda v, t: t + buf[OWN + v], zero)
        return total

    def vec_done(buf, ss, rs):
        group_loop(lambda i: vec_copy(buf, ss, rs, i, o).wait_send())
        if groups > 1:
            group_loop(lambda i: vec_across(buf, ss, rs, i, g).wait_send(), 1, groups)

    def over_copy(m):
        return ncopy(eys.at[m], eyr.at[m], g3_s.at[m], g3_r.at[m], n2)

    def chip_sum(m, y, part):
        return gst[m, b0, y, part, :].astype(F32) + gr1[m, y, part, :].astype(F32)

    def early_over(m):
        ncopy(gst.at[m, b0], gr1.at[m], g1_s.at[m], g1_r.at[m], n1).wait_recv()
        eys[m] = chip_sum(m, 1 - b1, slice(None)).astype(BF16)
        start(over_copy(m))

    def pair_copy(m):
        return wcopy(es1.at[m], er1.at[m], g2_s.at[m], g2_r.at[m], pair)

    def early_pair(m):
        over_copy(m).wait_recv()
        es1[m] = (chip_sum(m, b1, away) + eyr[m, away, :].astype(F32)).astype(BF16)
        start(pair_copy(m))

    def e_line(m, i):
        u = line(i)
        return wcopy(zse.at[m, piece(u), :], zre.at[m, qa], ez_s.at[m, i], ez_r.at[m, qa], line_dev(u))

    def early_line(m):
        pair_copy(m).wait_recv()
        total = chip_sum(m, b1, keep) + eyr[m, keep, :].astype(F32) + er1[m].astype(F32)
        zse[m] = total.astype(BF16)
        loop(lambda i: e_line(m, i).start(), 1, LINE)

    def e_across(m, i):
        ref = grp.at[g, m]
        return wcopy(ref, ref, gp_s.at[3 + m, i], gp_r.at[3 + m, g], lax.rem(g + i, groups) * OWN + o)

    def e_swap(m, y):
        ref = mom.at[3 + m, y, b0, pb, piece(qa), :]
        return ncopy(ref, ref, ey_s.at[m], ey_r.at[m], n2)

    def early_sum(m):
        zre[m, qa] = zse[m, piece(qa), :]

        def take(i):
            v = line(i)
            ref = zre.at[m, v]
            wcopy(ref, ref, ez_s.at[m, 0], ez_r.at[m, v], line_dev(v)).wait_recv()

        loop(take, 1, LINE)
        total = zre[m, 0].astype(F32)
        for v in range(1, LINE):
            total = total + zre[m, v].astype(F32)
        if groups > 1:
            grp[g, m] = total.astype(BF16)
            loop(lambda i: e_across(m, i).start(), 1, groups)

            def meet(i):
                v = lax.rem(g + i, groups)
                ref = grp.at[v, m]
                wcopy(ref, ref, gp_s.at[3 + m, i], gp_r.at[3 + m, v], v * OWN + o).wait_recv()

            loop(meet, 1, groups)
            total = lax.fori_loop(
                0, groups, lambda v, t: t + grp[v, m].astype(F32), jnp.zeros_like(total)
            )
        old = mT[3 + m, pl.ds(pl.multiple_of(pb * HR + qa * PR, PR), PR), :]
        mom[3 + m, b1, b0, pb, piece(qa), :] = (total + 0.5 * old).astype(BF16)
        start(e_swap(m, b1))

    def e_share(m, u, i):
        ref = mom.at[3 + m, :, b0, pb, piece(u), :]
        return wcopy(ref, ref, aq_s.at[3 + m, i], aq_r.at[3 + m, u], line_dev(line(i)))

    def early_back(m):
        e_swap(m, 1 - b1).wait_recv()
        loop(lambda i: e_share(m, qa, i).start(), 1, LINE)

    def e_half(m, b):
        ref = mom.at[3 + m, :, b0, b]
        return wcopy(ref, ref, ap_s.at[3 + m], ap_r.at[3 + m], pair)

    def early_half(m):
        loop(lambda i: e_share(m, line(i), i).wait_recv(), 1, LINE)
        start(e_half(m, pb))

    def e_near(m, c):
        ref = mom.at[3 + m, :, c]
        return ncopy(ref, ref, ow_s.at[m], ow_r.at[m], n1)

    def early_near(m):
        e_half(m, 1 - pb).wait_recv()

        @pl.when(b0 != m % 2)
        def _():
            e_near(m, b0).start()

    def vec_early():
        for x in (1, 2, 3):
            arrived(vecs.at[rel(x)], vn_s.at[x], vn_r.at[x], rel(x))
        vecw[o] = ((vecs[0] + vecs[1]) + vecs[2]) + vecs[3]
        vec_send(vecw, vw_s, vw_r)

    plan = {
        ("a", 0): [(early_over, 0)],
        ("a", 1): [(early_over, 1)],
        ("a", 2): [(early_over, 2)],
        ("a", 3): [(lambda m: vec_early(), 0)],
        (0, 1, 0): [(early_pair, 0)],
        (0, 1, 1): [(l2, 0)],
        (0, 2, 0): [(early_pair, 1)],
        (0, 3, 0): [(early_pair, 2), (early_line, 0)],
        (0, 3, 1): [(l3, 0)],
        (1, 0, 0): [(early_line, 1)],
        (1, 1, 0): [(early_line, 2), (early_sum, 0)],
        (1, 1, 1): [(l4, 0), (l2, 1)],
        (1, 2, 0): [(early_sum, 1)],
        (1, 2, 1): [(early_back, 0)],
        (1, 3, 0): [(early_sum, 2), (l5, 0)],
        (1, 3, 1): [(l3, 1)],
    }

    def after(i, key):
        for k in range(NAR):
            point = (key[0], k) + key[1:]
            if point in plan:
                @pl.when(i == k)
                def _():
                    held = len(pending)
                    for fn, arg in plan[point]:
                        fn(arg)
                    del pending[held:]

    dkT[...] = jnp.zeros_like(dkT)
    dvT[...] = jnp.zeros_like(dvT)
    lane = lax.broadcasted_iota(jnp.int32, (TB, CW), 1)
    low_lane = lane < HD

    def backward_v(i, _):
        t = rel(i)
        rr = rows(t, TB)

        @pl.when(i > 0)
        def _():
            for c in range(TB // MID):
                dst = dcr.at[pl.ds(pl.multiple_of(t * TB + c * MID, MID), MID)]
                ncopy(
                    dcst.at[pl.ds(c * MID, MID), mycols], dst, dc_sem.at[i, c], dc_rem.at[i, c], t
                ).wait_recv()

        dcs = (dcr[rr, :].astype(F32) * rln[rr, :]).astype(BF16)
        full = dcs.astype(F32)
        prod = full * ctxn[rr, :]
        delta = (
            jnp.sum(jnp.where(low_lane, prod, 0.0), axis=1, keepdims=True),
            jnp.sum(jnp.where(low_lane, 0.0, prod), axis=1, keepdims=True),
        )
        dcT = full.T.astype(BF16)
        for h in range(2):
            hs = slice(h * HD, (h + 1) * HD)
            top = delta[h].astype(BF16).astype(F32)
            tail = delta[h] - top
            base = (1 - h) * HD
            extra = jnp.where(lane == base, -top, jnp.where(lane == base + 1, -tail, 0.0))
            qp[h, rr, 0:CW] = jnp.where(low_lane == (h == 0), full, extra).astype(BF16)
            dvT[hs, :] += mm(dcT[hs, :], e_ref[h, rr, :])
        after(i, ("a",))
        return 0

    lax.fori_loop(0, NAR, backward_v, 0)
    gT[2 * CW:, :] = dvT[...].astype(BF16)
    l1(0, gT[2 * CW:, :])

    def backward(h):
        hs = slice(h * HD, (h + 1) * HD)
        ks = slice(CW + h * HD, CW + (h + 1) * HD)

        def block(i, _):
            rr = rows(rel(i), TB)
            s_ref[...] = mm(qp[h, rr, 0:CW], vTp[h])
            ds = e_ref[h, rr, :] * s_ref[...].astype(BF16)
            gT[hs, rr] = (mm_nt(kTp[h, hs, :], ds) * 0.125).astype(BF16)
            after(i, (h, 0))
            dkT[hs, :] += mm(qT[hs, rr], ds)
            after(i, (h, 1))
            return 0

        lax.fori_loop(0, NAR, block, 0)
        gT[ks, :] = dkT[hs, :].astype(BF16)
        lhs = jnp.concatenate([gT[hs, :], gT[ks, :]], axis=0)
        if h == 0:
            l1(1, lhs)
        else:
            d1(lhs)

    backward(0)
    backward(1)

    def dx(t):
        return mm(wqkv[...], gT[:, rows(t, TB)])

    both_rows = pl.ds(pl.multiple_of(b1 * 2 * CW, 2 * CW), 2 * CW)
    XB = s_ref.at[:, 0:D]

    def newton_begin(m):
        xin = mom[m].reshape(D, D).astype(F32)
        XB[...] = xin * (1.0 / (jnp.sqrt(jnp.sum(xin * xin)) + 1e-07))

    def newton_step():
        x = XB[...]
        xl = x.astype(BF16)
        a = mm_nt(xl, xl)
        al = a.astype(BF16)
        p = (COEF_B * a + COEF_C * mm(al, al)).astype(BF16)
        XB[...] = COEF_A * x + mm(p, xl)

    def swap(m, k):
        return ncopy(dkT.at[:, k * D:(k + 1) * D], orth.at[m], sw_s.at[k], sw_r.at[k], n1)

    def newton_last(m, k):
        xl = XB[...].astype(BF16)
        xo = XB[both_rows, :]
        a = mm_nt(xo.astype(BF16), xl).astype(BF16)
        y = mm(a, xl)
        z = mm_nt(y.astype(BF16), xl).astype(BF16)
        res = COEF_A * xo + COEF_B * y + COEF_C * mm(z, xl)
        first, second = res[0:CW], res[CW:]
        orth[m] = jnp.where(b0 == 0, first, second)
        dkT[:, k * D:(k + 1) * D] = jnp.where(b0 == 0, second, first)
        start(swap(m, k))

    def dx2_copy(c):
        cols = slice(c * MID, (c + 1) * MID)
        return ncopy(dxs2.at[:, cols], dxr2.at[:, cols], dx2_s.at[c], dx2_r.at[c], n2)

    dxs[1][...] = dx(n3).astype(BF16)
    start(ncopy(dxs[1], dxr1.at[1], dx1_s.at[1], dx1_r.at[1], n1))
    dxs[0][...] = dx(n1).astype(BF16)
    start(ncopy(dxs[0], dxr1.at[0], dx1_s.at[0], dx1_r.at[0], n1))
    early_back(1)
    over = dx(n2)
    early_half(0)
    one = jnp.ones((8, LEN), BF16)
    upper_rows = lax.broadcasted_iota(jnp.int32, (8, CW), 0) < 4
    lv[o] = jnp.where(upper_rows, mm_nt(one, gT[0:CW, :]), mm_nt(one, gT[2 * CW:, :]))
    ncopy(dxs[1], dxr1.at[1], dx1_s.at[1], dx1_r.at[1], n1).wait_recv()
    dxs2[...] = (over + dxr1[1].astype(F32)).astype(BF16)
    start(dx2_copy(0))
    early_back(2)
    l4(1)
    dxo = dx(n).T
    for k in range(NAR):
        cols = slice(k * CW, (k + 1) * CW)
        ograd[:, cols] = dxo[:, cols] + win_f[k]
    d2()
    early_near(0)
    early_half(1)

    @pl.when(b0 == 0)
    def _():
        e_near(0, 1).wait_recv()

    @pl.when(b0 == 1)
    def _():
        fan_wait(0, 0, 2)

    newton_begin(3 - b0)
    newton_step()
    early_half(2)
    l5(1)
    early_near(1)
    vec_send(lv, lv_s, lv_r)
    newton_step()
    l5(2)
    start(dx2_copy(1))
    early_near(2)
    newton_last(3 - b0, 1)

    e_near(2 - b0, 1 - b0).wait_recv()
    newton_begin(5 - b0)
    newton_step()
    newton_step()
    newton_last(5 - b0, 2)
    fan_wait(1, 1 + b0, b0)
    fan_wait(2, 3 + b0, b0)
    newton_begin(b0)
    l_mom = pltpu.make_async_copy(mom.at[:, b1, b0], omom_h, loc_sem.at[8])
    l_mom.start()
    newton_step()
    newton_step()
    newton_last(b0, 0)

    ncopy(dxs[0], dxr1.at[0], dx1_s.at[0], dx1_r.at[0], n1).wait_recv()
    for c in (0, 1):
        dx2_copy(c).wait_recv()
    ograd[...] = ograd[...] + (dxr1[0].astype(F32) + dxr2[...].astype(F32)).T
    l_ograd = pltpu.make_async_copy(ograd, ograd_h, loc_sem.at[7])
    l_ograd.start()

    swap(2 + b0, 1).wait_recv()
    swap(4 + b0, 2).wait_recv()
    swap(1 - b0, 0).wait_recv()
    l_orth = pltpu.make_async_copy(orth, oorth_h, loc_sem.at[9])
    l_orth.start()

    ovec[...] = vec_sum(vecw, vw_s, vw_r)
    late = vec_sum(lv, lv_s, lv_r)
    ovec2[0:1, :] = late[0:1]
    ovec2[1:2, :] = late[4:5]
    ovec2[2:3, :] = ovec[6:7, mycols]
    ovec2[3:8, :] = jnp.zeros((5, CW), F32)

    for m in range(3):
        pending.extend((pair_copy(m), over_copy(m), e_swap(m, b1)))
        if m < 2:
            pending.append(half_copy(m, keepc))
        for f, k, c in fans[m]:
            pending.append(far_copy(m, f, k, c))

            @pl.when(b0 != c)
            def _():
                near_copy(m, f, k, c).wait_send()

        @pl.when(b0 != m % 2)
        def _():
            e_near(m, b0).wait_send()

    for c in pending:
        c.wait_send()
    vec_done(vecw, vw_s, vw_r)
    vec_done(lv, lv_s, lv_r)
    group_loop(lambda i: d1_copy(i).wait_send())
    group_loop(lambda i: d2_copy(o, i).wait_send())
    for k in range(3):
        if k < 2:
            loop(lambda i: z_copy(k, i).wait_send(), 1, LINE)
            loop(lambda i: share(k, qa, i).wait_send(), 1, LINE)
        loop(lambda i: e_line(k, i).wait_send(), 1, LINE)
        loop(lambda i: e_share(k, qa, i).wait_send(), 1, LINE)
        if groups > 1:
            loop(lambda i: across(k, i).wait_send(), 1, groups)
            loop(lambda i: e_across(k, i).wait_send(), 1, groups)
    l_otok.wait()
    l_ograd.wait()
    l_mom.wait()
    l_orth.wait()


def run_layer(wide, tokens, cotangent, seg, pad, gen, in_w, out_w, in_m, out_m, shared, split):
    any_ = pl.BlockSpec(memory_space=pl.ANY)
    vm = pl.BlockSpec(memory_space=pltpu.VMEM)
    V = pltpu.VMEM
    dma = lambda *s: pltpu.SemaphoreType.DMA(s)
    one = pltpu.SemaphoreType.DMA
    groups = wide // OWN
    vslots = OWN + (groups if groups > 1 else 0)
    scratch = [
        V((LEN, D), BF16), V((TB, D), BF16), V((NAR, 16, CW), F32),
        V((4, D, CW), F32), V((2, CW, D), F32), V((6, CW, D), F32),
        V((3 * CW, D), BF16), V((D, 3 * CW), BF16),
        V((D, D), BF16), V((2, D, D), BF16), V((2, CW, CW), F32),
        V((2, LEN, 2 * CW), BF16), V((2, 2 * CW, LEN), BF16), V((2, CW, LEN), BF16), V((CW, LEN), BF16),
        V((LEN, CW), F32), V((TB, LEN), F32), V((2, LEN, LEN), BF16),
        V((LEN, CW), F32), V((LEN, CW), BF16), V((TB, D), BF16),
        V((TB, D), BF16), V((TB, D), BF16), V((TB, D), BF16), V((TB, D), BF16), V((TB, D), BF16),
        V((TB, D), BF16), V((LEN, CW), BF16),
        V((NAR, 8, D), F32), V((vslots, 8, D), F32), V((CW, LEN), F32), V((CW, LEN), F32), V((3 * CW, LEN), BF16),
        V((3, 2, 2, CW, D), BF16), V((3, 2, CW, D), BF16), V((3, CW, D), BF16), V((3, CW, D), BF16),
        V((3, HR, D), BF16), V((3, HR, D), BF16), V((3, HR, D), BF16), V((3, LINE, PR, D), BF16), V((3, CW, HC), BF16),
        V((2, 2, HR, HC), BF16), V((2, LINE, 2, PR, HC), BF16), V((2, HR, D), BF16), V((OWN, 2, PR, HC), BF16),
        V((vslots, 8, CW), F32),
        V((6, 2, 2, 2, HR, D), BF16),
        V((groups, 3, PR, D) if groups > 1 else (1, 1, PR, D), BF16),
        V((groups, 3, 2, PR, HC) if groups > 1 else (1, 1, 1, PR, HC), BF16),
        V((2, D, TB), BF16), V((D, TB), BF16),
        dma(10), dma(4), dma(4), dma(2), dma(2), dma(4), dma(4), dma(3, 2), dma(3, 2), dma(1, 2), dma(1, 2),
        dma(4), dma(4), dma(4, TB // MID), dma(4, TB // MID), dma(4), dma(4), dma(vslots), dma(vslots),
        dma(vslots), dma(vslots),
        dma(3), dma(3), dma(3), dma(3), dma(3), dma(3), dma(3), dma(3), dma(3, LINE), dma(3, LINE),
        dma(OWN), dma(OWN), dma(OWN), dma(OWN),
        dma(6, groups), dma(6, groups),
        dma(6, LINE), dma(6, LINE), dma(6), dma(6),
        dma(3), dma(3), dma(3, LINE), dma(3, LINE), dma(3), dma(3), dma(5, 2), dma(5, 4), dma(3), dma(3),
        dma(2), dma(2), dma(2), dma(2),
    ]
    return pl.pallas_call(
        functools.partial(layer_kernel, wide),
        out_shape=[
            jax.ShapeDtypeStruct((TB, D), BF16),
            jax.ShapeDtypeStruct((TB, D), F32),
            jax.ShapeDtypeStruct((6, 2, HR, D), BF16),
            jax.ShapeDtypeStruct((6, CW, D), F32),
            jax.ShapeDtypeStruct((8, D), F32),
            jax.ShapeDtypeStruct((8, CW), F32),
        ],
        in_specs=[any_, any_, vm, vm, vm, any_, any_, any_, any_, vm, vm],
        out_specs=[any_, any_, any_, any_, vm, vm],
        scratch_shapes=scratch,
        compiler_params=pltpu.CompilerParams(
            collective_id=0, has_side_effects=True, vmem_limit_bytes=62 * MB
        ),
        name="layer",
    )(tokens, cotangent, seg, pad, gen, in_w, out_w, in_m, out_m, shared, split)


def muon_step(weights, orthogonal):
    return weights - 0.2 * (0.2 * math.sqrt(D) * orthogonal + 0.01 * weights)


def adam_step(values, moment_one, moment_two, gradient):
    moment_one = 0.9 * moment_one + 0.1 * gradient
    moment_two = 0.999 * moment_two + 0.001 * gradient * gradient
    step_ratio = (
        moment_one / (1.0 - 0.9**STEP) / (jnp.sqrt(moment_two / (1.0 - 0.999**STEP)) + 1e-08)
    )
    return (moment_one, moment_two, values - 0.3 * (step_ratio + 0.01 * values))


def blend(average, weights):
    return 0.6 * average + 0.4 * weights


def update_kernel(
    otok, ograd, mom, orth, in_w, out_w, in_a, out_a, vec, vec2,
    sv, s1, s2, sa, pv, p1, p2, pa,
    tok_o, grad_o, inm_o, outm_o, inw_o, outw_o, inl_o, outl_o, ina_o, outa_o,
    s1_o, s2_o, sv_o, sa_o, p1_o, p2_o, pv_o, pa_o,
    mom_b, orth_b, inw_b, outw_b, ina_b, outa_b,
    inm_v, outm_v, inw_v, outw_v, inl_v, outl_v, ina_v, outa_v, grad_v, tok_v, thru, rsem, wsem,
):
    whole = [
        pltpu.make_async_copy(ograd, grad_v, thru.at[0]),
        pltpu.make_async_copy(otok, tok_v, thru.at[1]),
    ]
    back = [
        pltpu.make_async_copy(grad_v, grad_o, thru.at[2]),
        pltpu.make_async_copy(tok_v, tok_o, thru.at[3]),
    ]
    reads, writes = [], []
    for k in range(6):
        j, inner = (k, True) if k < 4 else (k - 4, False)
        srcs = (mom.at[k], orth.at[k], (in_w if inner else out_w).at[j], (in_a if inner else out_a).at[j])
        dsts = (
            mom_b.at[k], orth_b.at[k], (inw_b if inner else outw_b).at[j], (ina_b if inner else outa_b).at[j],
        )
        reads.append([pltpu.make_async_copy(s, d, rsem.at[k, i]) for i, (s, d) in enumerate(zip(srcs, dsts))])
        bufs = (inm_v, inw_v, inl_v, ina_v) if inner else (outm_v, outw_v, outl_v, outa_v)
        outs = (inm_o, inw_o, inl_o, ina_o) if inner else (outm_o, outw_o, outl_o, outa_o)
        writes.append(
            [pltpu.make_async_copy(s.at[j], d.at[j], wsem.at[k, i]) for i, (s, d) in enumerate(zip(bufs, outs))]
        )
    for c in reads[0]:
        c.start()
    for c in reads[1]:
        c.start()
    for c in whole:
        c.start()
    for k in range(2, 6):
        for c in reads[k]:
            c.start()
    s1_o[...], s2_o[...], shared_new = adam_step(sv[...], s1[...], s2[...], vec[0:6, :])
    sv_o[...] = shared_new
    sa_o[...] = blend(sa[...], shared_new)
    p1_o[...], p2_o[...], split_new = adam_step(pv[...], p1[...], p2[...], vec2[0:3, :])
    pv_o[...] = split_new
    pa_o[...] = blend(pa[...], split_new)
    for k in range(6):
        if k in (1, 2):
            whole[k - 1].wait()
            back[k - 1].start()
        for c in reads[k]:
            c.wait()
        if k < 4:
            inm_v[k] = mom_b[k].reshape(CW, D).astype(F32).T
            new = muon_step(inw_b[k], orth_b[k].T)
            inw_v[k] = new
            inl_v[k] = new.astype(BF16)
            ina_v[k] = blend(ina_b[k], new)
        else:
            j = k - 4
            outm_v[j] = mom_b[k].reshape(CW, D).astype(F32)
            new = muon_step(outw_b[j], orth_b[k])
            outw_v[j] = new
            outl_v[j] = new.astype(BF16)
            outa_v[j] = blend(outa_b[j], new)
        for c in writes[k]:
            c.start()
    for c in back:
        c.wait()
    for k in range(6):
        for c in writes[k]:
            c.wait()


def run_update(*args):
    vm = pl.BlockSpec(memory_space=pltpu.VMEM)
    any_ = pl.BlockSpec(memory_space=pl.ANY)
    S = jax.ShapeDtypeStruct
    V = pltpu.VMEM
    inner, outer = (4, D, CW), (2, CW, D)
    return pl.pallas_call(
        update_kernel,
        out_shape=[
            S((TB, D), BF16), S((TB, D), F32), S(inner, F32), S(outer, F32), S(inner, F32), S(outer, F32),
            S(inner, BF16), S(outer, BF16), S(inner, F32), S(outer, F32),
        ]
        + [S((6, D), F32)] * 4
        + [S((3, CW), F32)] * 4,
        in_specs=[any_] * 8 + [vm] * 10,
        out_specs=[any_] * 10 + [vm] * 8,
        scratch_shapes=[
            V((6, 2, HR, D), BF16), V((6, CW, D), F32), V(inner, F32), V(outer, F32), V(inner, F32), V(outer, F32),
            V(inner, F32), V(outer, F32), V(inner, F32), V(outer, F32), V(inner, BF16), V(outer, BF16),
            V(inner, F32), V(outer, F32), V((TB, D), F32), V((TB, D), BF16),
            pltpu.SemaphoreType.DMA((4,)), pltpu.SemaphoreType.DMA((6, 4)), pltpu.SemaphoreType.DMA((6, 4)),
        ],
        compiler_params=pltpu.CompilerParams(vmem_limit_bytes=60 * MB),
        name="update",
    )(*args)


def body(
    wide, tokens, cotangent, segments, padding, generative, in_weights, out_weights, in_momenta,
    out_momenta, in_average, out_average, shared_values, shared_moment1, shared_moment2,
    shared_average, split_values, split_moment1, split_moment2, split_average,
):
    flags = [v.reshape(TB // CW, CW) for v in (segments, padding, generative)]
    otok, ograd, mom, orth, vec, vec2 = run_layer(
        wide, tokens, cotangent, *flags, in_weights, out_weights, in_momenta, out_momenta,
        shared_values, split_values,
    )
    return tuple(
        run_update(
            otok, ograd, mom, orth, in_weights, out_weights, in_average, out_average, vec, vec2,
            shared_values, shared_moment1, shared_moment2, shared_average,
            split_values, split_moment1, split_moment2, split_average,
        )
    )


def solution(mesh):
    rows = P(("wide", "narrow"), None)
    flat = P(("wide", "narrow"))
    cols = P(None, None, "narrow")
    outs = P(None, "narrow", None)
    vec = P(None, "narrow")
    return jax.shard_map(
        functools.partial(body, mesh.shape["wide"]),
        mesh=mesh,
        in_specs=(
            rows, rows, flat, flat, flat, cols, outs, cols, outs, cols, outs,
            P(), P(), P(), P(), vec, vec, vec, vec,
        ),
        out_specs=(
            rows, rows, cols, outs, cols, outs, cols, outs, cols, outs,
            P(), P(), P(), P(), vec, vec, vec, vec,
        ),
        check_vma=False,
    )
```

```python
import functools
import math

import jax
import jax.numpy as jnp
from jax import lax
from jax.experimental import pallas as pl
from jax.experimental.pallas import tpu as pltpu
from jax.sharding import PartitionSpec as P

D = 512
HD = 64
LEN = 2048
NS_ITERS = 3
STEP = 10
NAR = 4
TB = LEN // NAR
CW = D // NAR
OWN = 8
LINE = OWN // 2
HR = CW // 2
HC = D // 2
PR = CW // OWN
MID = 256

F32 = jnp.float32
BF16 = jnp.bfloat16
MESH = pl.DeviceIdType.MESH

COEF_A = 3.4445
COEF_B = -4.775
COEF_C = 2.0315
NEG = -1e30
MB = 2**20


def mm(a, b):
    return jnp.dot(a, b, preferred_element_type=F32)


def mm_nt(a, b):
    return lax.dot_general(a, b, (((1,), (1,)), ((), ())), preferred_element_type=F32)


def mm_tn(a, b):
    return lax.dot_general(a, b, (((0,), (0,)), ((), ())), preferred_element_type=F32)


def layer_kernel(wide, *refs):
    (
        tok_h, cot_h, seg_i, pad_i, gen_i, win_h, wout_h, min_h, mout_h, shared, split,
        otok_h, ograd_h, omom_h, oorth_h, ovec, ovec2,
        tok, cot, pay, win_f, wout_f, mT, wqkvT, wqkv, wup, wod, bcol,
        qp, kTp, vTp, qT, rdn, s_ref, e_ref, ctxn, ctx_s, ctxf,
        hr, act, du, dr2r, dr1r, dcst, dcr, vecs, vecw, dkT, dvT, gT,
        gst, gr1, eys, eyr, es1, er1, zse, zre, lr1, zs, zr, zd, zdr, lv, mom, grp, grl,
        dxr1, dxr2,
        loc_sem, ag_s, ag_r, rly_s, rly_r, pay_s, pay_r, wg_s, wg_r, wr_s, wr_r,
        ctx_sem, ctx_rem, dc_sem, dc_rem, vn_s, vn_r, vw_s, vw_r, lv_s, lv_r,
        g1_s, g1_r, g2_s, g2_r, g3_s, g3_r, l1_s, l1_r, zs_s, zs_r, zd_s, zd_r, ad_s, ad_r, gp_s, gp_r,
        aq_s, aq_r, ap_s, ap_r, ow_s, ow_r, ez_s, ez_r, ey_s, ey_r, la_s, la_r, sw_s, sw_r, dx1_s, dx1_r, dx2_s, dx2_r,
    ) = refs
    n = lax.axis_index("narrow")
    w = lax.axis_index("wide")
    groups = wide // OWN
    g = w // OWN if groups > 1 else 0
    o = lax.rem(w, OWN) if groups > 1 else w
    b0 = lax.rem(n, 2)
    b1 = n // 2

    def rel(x):
        return lax.rem(b0 + x % 2, 2) + 2 * lax.rem(b1 + x // 2, 2)

    n1, n2, n3 = rel(1), rel(2), rel(3)

    def rows(t, size):
        return pl.ds(pl.multiple_of(t * size, size), size)

    def ncopy(src, dst, ssem, rsem, t):
        return pltpu.make_async_remote_copy(
            src_ref=src, dst_ref=dst, send_sem=ssem, recv_sem=rsem,
            device_id={"narrow": t}, device_id_type=MESH,
        )

    def wcopy(src, dst, ssem, rsem, u):
        return pltpu.make_async_remote_copy(
            src_ref=src, dst_ref=dst, send_sem=ssem, recv_sem=rsem,
            device_id={"wide": u}, device_id_type=MESH,
        )

    pending = []

    def start(copy):
        copy.start()
        pending.append(copy)
        return copy

    own = rows(n, TB)
    ograd = s_ref.at[:, 3 * D:4 * D]
    ograd_b = hr
    rln = rdn
    otok = cot
    dxs, dxs2 = (act, du), dr2r

    l_tok = pltpu.make_async_copy(tok_h, tok.at[own], loc_sem.at[0])
    l_win = pltpu.make_async_copy(win_h, win_f, loc_sem.at[1])
    l_wout = pltpu.make_async_copy(wout_h, wout_f, loc_sem.at[2])
    l_cot = pltpu.make_async_copy(cot_h, cot, loc_sem.at[3])
    l_min = pltpu.make_async_copy(min_h, win_f, loc_sem.at[4])
    l_mout = pltpu.make_async_copy(mout_h, mT.at[pl.ds(4, 2)], loc_sem.at[5])
    for c in (l_tok, l_win, l_wout, l_cot, l_mout):
        c.start()

    barrier = pltpu.get_barrier_semaphore()
    for x in (1, 2, 3):
        pl.semaphore_signal(barrier, inc=1, device_id={"narrow": rel(x)}, device_id_type=MESH)

    def greet(i, c):
        pl.semaphore_signal(
            barrier, inc=1, device_id={"wide": g * OWN + lax.rem(o + i, OWN)}, device_id_type=MESH
        )
        return c

    lax.fori_loop(1, OWN, greet, 0)

    def greet_group(i, c):
        pl.semaphore_signal(
            barrier, inc=1, device_id={"wide": lax.rem(g + i, groups) * OWN + o}, device_id_type=MESH
        )
        return c

    if groups > 1:
        lax.fori_loop(1, groups, greet_group, 0)
    seg = seg_i[...]
    closed = jnp.logical_or(pad_i[...] != 0, gen_i[...] != 0)
    pay[n] = jnp.concatenate(
        [
            seg.astype(F32), jnp.where(closed, -1, seg).astype(F32),
            split[2:3, :], jnp.zeros((7, CW), F32),
        ],
        axis=0,
    )
    l_tok.wait()
    pl.semaphore_wait(barrier, 3 + (OWN - 1) + (groups - 1))

    half = TB // 2

    def ag_rows(t, c):
        return tok.at[pl.ds(pl.multiple_of(t * TB + c * half, half), half)]

    for x in (1, 2, 3):
        start(ncopy(pay.at[n], pay.at[n], pay_s.at[x], pay_r.at[x], rel(x)))
    for c in (0, 1):
        start(ncopy(ag_rows(n, c), ag_rows(n, c), ag_s.at[2 + c], ag_r.at[2 + c], n2))
    for c in (0, 1):
        start(ncopy(ag_rows(n, c), ag_rows(n, c), ag_s.at[c], ag_r.at[c], n1))

    def arrived(slot, sem_s, sem_r, t):
        ncopy(slot, slot, sem_s, sem_r, t).wait_recv()

    l_win.wait()
    for k in range(3):
        piece = win_f[k]
        wqkvT[k * CW:(k + 1) * CW, :] = piece.T.astype(BF16)
        wqkv[:, k * CW:(k + 1) * CW] = piece.astype(BF16)
    mycols = pl.ds(pl.multiple_of(n * CW, CW), CW)
    wup[:, mycols] = win_f[3].astype(BF16)
    l_min.start()
    l_wout.wait()
    for k in range(2):
        wod[k, mycols, :] = wout_f[k].astype(BF16)

    def wg_list(sems, semr, x, t, target):
        cols = pl.ds(pl.multiple_of(t * CW, CW), CW)
        return [
            ncopy(wod.at[:, cols, :], wod.at[:, cols, :], sems.at[x, 0], semr.at[x, 0], target),
            ncopy(wup.at[:, cols], wup.at[:, cols], sems.at[x, 1], semr.at[x, 1], target),
        ]

    bcol[0] = jnp.broadcast_to(split[0:1, :], (CW, CW)).T
    bcol[1] = jnp.broadcast_to(split[1:2, :], (CW, CW)).T

    def project(t, c):
        rr = pl.ds(pl.multiple_of(t * TB + c * half, half), half)
        tb = tok[rr, :]
        qk = mm(tb, wqkv[:, 0:2 * CW])
        q = (qk[:, :CW] + split[0:1, :]).astype(BF16)
        k = qk[:, CW:].astype(BF16)
        q8 = q.astype(F32) * 0.125
        prod = q8 * k.astype(F32)
        low = lax.broadcasted_iota(jnp.int32, (half, CW), 1) < HD
        d0 = jnp.sum(jnp.where(low, prod, 0.0), axis=1, keepdims=True)
        d1 = jnp.sum(jnp.where(low, 0.0, prod), axis=1, keepdims=True)
        rdn[rr, :] = jnp.where(low, d0, d1)
        lane1 = lax.broadcasted_iota(jnp.int32, (CW, CW), 1).astype(F32)
        lowj = lane1 < HD
        for j in range(half // CW):
            seg = jnp.broadcast_to(pay[t, pl.ds(c * (half // CW) + j, 1), :], (CW, CW)).T
            part = q8[j * CW:(j + 1) * CW, :]
            hot = lambda base: jnp.where(seg == lane1 + base, 1.0, 0.0)
            rj = pl.ds(pl.multiple_of(t * TB + c * half + j * CW, CW), CW)
            qp[0, rj, 0:CW] = jnp.where(lowj, part, hot(-float(HD))).astype(BF16)
            qp[1, rj, 0:CW] = jnp.where(lowj, hot(0.0), part).astype(BF16)
            rest = hot(float(HD)).astype(BF16)
            qp[0, rj, CW:] = rest
            qp[1, rj, CW:] = rest
        tT = mm_nt(wqkvT[...], tb)
        bq = jnp.concatenate([bcol[0]] * (half // CW), axis=1)
        bv = jnp.concatenate([bcol[1]] * (half // CW), axis=1)
        qT[:, rr] = ((tT[0:CW] + bq).astype(BF16).astype(F32) * 0.125).astype(BF16)
        kT = tT[CW:2 * CW].astype(BF16)
        vT = (tT[2 * CW:] + bv).astype(BF16)
        code = jnp.concatenate(
            [pay[t, pl.ds(4 + c * (half // CW) + j, 1), :] for j in range(half // CW)], axis=1
        )
        rowi = lax.broadcasted_iota(jnp.int32, (HD, half), 0).astype(F32)
        keep = lambda base: jnp.where(code == rowi + base, 0.0, NEG).astype(BF16)
        first, second, third = keep(0.0), keep(float(HD)), keep(float(2 * HD))
        ones = jnp.ones((HD, half), BF16)
        kTp[0, 0:HD, rr] = kT[0:HD]
        kTp[0, HD:CW, rr] = first
        kTp[1, 0:HD, rr] = first
        kTp[1, HD:CW, rr] = kT[HD:]
        vTp[0, 0:HD, rr] = vT[0:HD]
        vTp[0, HD:, rr] = ones
        vTp[1, 0:HD, rr] = ones
        vTp[1, HD:, rr] = vT[HD:]
        for h in range(2):
            kTp[h, CW:CW + HD, rr] = second
            kTp[h, CW + HD:, rr] = third

    def relayed(c):
        return ncopy(ag_rows(n2, c), ag_rows(n2, c), rly_s.at[c], rly_r.at[c], n1)

    def project_step(i, _):
        @pl.when(i == 2)
        def _():
            arrived(pay.at[n1], pay_s.at[1], pay_r.at[1], n1)
            arrived(ag_rows(n1, 0), ag_s.at[0], ag_r.at[0], n1)
            l_min.wait()
            for k in range(4):
                mT[k] = win_f[k].T

        @pl.when(i == 3)
        def _():
            arrived(ag_rows(n1, 1), ag_s.at[1], ag_r.at[1], n1)

        @pl.when(i == 4)
        def _():
            arrived(pay.at[n2], pay_s.at[2], pay_r.at[2], n2)
            arrived(pay.at[n3], pay_s.at[3], pay_r.at[3], n3)
            arrived(ag_rows(n2, 0), ag_s.at[2], ag_r.at[2], n2)
            relayed(0).start()

        @pl.when(i == 5)
        def _():
            arrived(ag_rows(n3, 0), rly_s.at[0], rly_r.at[0], n1)

        @pl.when(i == 6)
        def _():
            arrived(ag_rows(n2, 1), ag_s.at[3], ag_r.at[3], n2)
            relayed(1).start()
            for x in (2, 1):
                for c in wg_list(wg_s, wg_r, x, n, rel(x)):
                    c.start()

        @pl.when(i == 7)
        def _():
            arrived(ag_rows(n3, 1), rly_s.at[1], rly_r.at[1], n1)

        far = i // 4
        x = (1 - far) * (i // 2) + far * (2 + lax.rem(i, 2))
        c = (1 - far) * lax.rem(i, 2) + far * (i // 2 - 2)
        project(rel(x), c)
        return 0

    lax.fori_loop(0, 2 * NAR, project_step, 0)
    for x in (2, 1):
        pending.extend(wg_list(wg_s, wg_r, x, n, rel(x)))
    pending.extend((relayed(0), relayed(1)))

    eye = lax.broadcasted_iota(jnp.int32, (CW, CW), 0) == lax.broadcasted_iota(jnp.int32, (CW, CW), 1)

    def ctx_copy(x, t):
        return ncopy(
            ctx_s.at[rows(t, TB)], ctxf.at[:, mycols], ctx_sem.at[x], ctx_rem.at[x], t
        )

    def attend(i, _):
        hi = 1 - i // 2
        lo = lax.rem((i + 1) // 2, 2)
        t = lax.rem(b0 + lo, 2) + 2 * lax.rem(b1 + hi, 2)
        rr = rows(t, TB)
        parts = []
        for h in range(2):
            s_ref[...] = mm(qp[h, rr, :], kTp[h])
            for j in range(TB // CW):
                cc = pl.ds(pl.multiple_of(t * TB + j * CW, CW), CW)
                diag = rdn[cc, h * HD:h * HD + 1]
                sub = pl.ds(j * CW, CW)
                s_ref[sub, cc] = jnp.where(eye, diag, s_ref[sub, cc])
            s = s_ref[...]
            top = jnp.max(s, axis=1, keepdims=True)
            e = jnp.exp(s - top).astype(BF16)
            e_ref[h, rr, :] = e
            parts.append(mm_nt(vTp[0, 0:HD + 16, :] if h == 0 else vTp[1, HD - 16:, :], e))
        num = jnp.concatenate([parts[0][:HD], parts[1][16:]], axis=0)
        den = jnp.concatenate(
            [
                jnp.broadcast_to(1.0 / parts[0][HD:HD + 1], (HD, TB)),
                jnp.broadcast_to(1.0 / parts[1][0:1], (HD, TB)),
            ],
            axis=0,
        )
        cn = (num * den).T
        ctxn[rr, :] = cn
        rln[rr, :] = den.T
        ctx_s[rr, :] = cn.astype(BF16)

        @pl.when(i < 3)
        def _():
            x = lo + 2 * hi
            ctx_copy(x, t).start()

        @pl.when(i == 2)
        def _():
            for c in wg_list(wg_s, wg_r, 2, n2, n2):
                c.wait_recv()
            for c in wg_list(wr_s, wr_r, 0, n2, n1):
                c.start()

        return 0

    lax.fori_loop(0, NAR, attend, 0)
    pending.extend(wg_list(wr_s, wr_r, 0, n2, n1))
    for x in (1, 2, 3):
        pending.append(ctx_copy(x, rel(x)))
    ctxf[:, mycols] = ctx_s[own, :]
    for c in wg_list(wg_s, wg_r, 1, n1, n1):
        c.wait_recv()
    for c in wg_list(wr_s, wr_r, 0, n3, n1):
        c.wait_recv()
    l_cot.wait()
    l_mout.wait()
    for x in (2, 3, 1):
        cols = pl.ds(pl.multiple_of(rel(x) * CW, CW), CW)
        ncopy(ctx_s.at[own], ctxf.at[:, cols], ctx_sem.at[x], ctx_rem.at[x], rel(x)).wait_recv()

    up_bias = jnp.concatenate([pay[t, 8:9, :] for t in range(NAR)], axis=1)
    vecs[n] = jnp.zeros((8, D), F32)

    def dc_copy(x, c, t, me):
        rr = pl.ds(c * MID, MID)
        cols = pl.ds(pl.multiple_of(t * CW, CW), CW)
        dst = dcr.at[pl.ds(pl.multiple_of(me * TB + c * MID, MID), MID)]
        return ncopy(dcst.at[rr, cols], dst, dc_sem.at[x, c], dc_rem.at[x, c], t)

    def middle(c, _):
        rr = pl.ds(pl.multiple_of(c * MID, MID), MID)
        ga1, be1, ga2, be2, ba, bd = (shared[k:k + 1, :] for k in range(6))
        x0 = tok[pl.ds(pl.multiple_of(n * TB + c * MID, MID), MID), :].astype(F32)
        r1 = x0 + (mm(ctxf[rr, :], wod[0]) + ba)
        c1 = r1 - jnp.mean(r1, axis=1, keepdims=True)
        s1 = lax.rsqrt(jnp.mean(c1 * c1, axis=1, keepdims=True) + 1e-05)
        x1 = c1 * s1
        hidden = x1 * ga1 + be1
        low = hidden.astype(BF16)
        hr[rr, :] = low
        upper = mm(low, wup[...]) + up_bias
        cdf = 0.5 * (1.0 + lax.erf(upper * (1.0 / math.sqrt(2.0))))
        pdf = jnp.exp(-0.5 * upper * upper) * (1.0 / math.sqrt(2.0 * math.pi))
        slope = cdf + upper * pdf
        a = (upper * cdf).astype(BF16)
        act[rr, :] = a
        r2 = hidden + (mm(a, wod[1]) + bd)
        c2 = r2 - jnp.mean(r2, axis=1, keepdims=True)
        s2 = lax.rsqrt(jnp.mean(c2 * c2, axis=1, keepdims=True) + 1e-05)
        x2 = c2 * s2
        dy = cot[rr, :].astype(F32)
        otok[rr, :] = (x2 * ga2 + be2).astype(BF16)
        dn = dy * ga2
        dr2 = s2 * (
            dn - jnp.mean(dn, axis=1, keepdims=True) - x2 * jnp.mean(dn * x2, axis=1, keepdims=True)
        )
        d2 = dr2.astype(BF16)
        dr2r[rr, :] = d2
        dup = (mm_nt(d2, wod[1]) * slope).astype(BF16)
        du[rr, :] = dup
        dh = dr2 + mm_nt(dup, wup[...])
        en = dh * ga1
        d1f = s1 * (
            en - jnp.mean(en, axis=1, keepdims=True) - x1 * jnp.mean(en * x1, axis=1, keepdims=True)
        )
        for k in range(NAR):
            win_f[k, rr, :] = d1f[:, k * CW:(k + 1) * CW]
        d1 = d1f.astype(BF16)
        dr1r[rr, :] = d1
        dcst[rr, :] = mm_nt(d1, wod[0]).astype(BF16)
        add = lambda v: jnp.sum(v, axis=0, keepdims=True)
        vecs[n] += jnp.concatenate(
            [
                add(dh * x1), add(dh), add(dy * x2), add(dy), add(d1f), add(dr2),
                add(dup.astype(F32)), jnp.zeros((1, D), F32),
            ],
            axis=0,
        )
        for k in range(TB // MID):
            @pl.when(c == k)
            def _():
                for x in (2, 3, 1):
                    dc_copy(x, k, rel(x), n).start()

        dcr[pl.ds(pl.multiple_of(n * TB + c * MID, MID), MID), :] = dcst[rr, mycols]
        return 0

    lax.fori_loop(0, TB // MID, middle, 0)
    for x in (1, 2, 3):
        for c in range(TB // MID):
            pending.append(dc_copy(x, c, rel(x), n))
    l_otok = pltpu.make_async_copy(otok, otok_h, loc_sem.at[6])
    l_otok.start()
    for x in (1, 2, 3):
        start(ncopy(vecs.at[n], vecs.at[n], vn_s.at[x], vn_r.at[x], rel(x)))

    for k, (left, right) in enumerate(((du, hr), (ctxf, dr1r), (act, dr2r))):
        grad = mm_tn(left[...], right[...]).astype(BF16)
        for t in range(NAR):
            gst[k, t % 2, t // 2] = grad[t * CW:(t + 1) * CW]
        ncopy(gst.at[k, 1 - b0], gr1.at[k], g1_s.at[k], g1_r.at[k], n1).start()

    def loop(fn, first, count):
        def go(i, c):
            fn(i)
            return c

        lax.fori_loop(first, count, go, 0)

    def group_loop(fn, first=1, count=OWN):
        loop(fn, first, count)

    def member(i):
        return lax.rem(o + i, OWN)

    pb = lax.rem(o, 2)
    qa = o // 2
    pair = g * OWN + 2 * qa + (1 - pb)

    def line(i):
        return lax.rem(qa + i, LINE)

    def line_dev(u):
        return g * OWN + 2 * u + pb

    keep = pl.ds(pl.multiple_of(pb * HR, HR), HR)
    away = pl.ds(pl.multiple_of((1 - pb) * HR, HR), HR)

    keepc = pl.ds(pl.multiple_of(pb * HC, HC), HC)
    awayc = pl.ds(pl.multiple_of((1 - pb) * HC, HC), HC)

    def piece(v):
        return pl.ds(pl.multiple_of(v * PR, PR), PR)

    def unit_rows(u):
        return pl.ds(u * CW, CW)

    def unit_mom(u, part, cols):
        if u == 0:
            return mom.at[2, b1, b0, :, part, cols]
        return mom.at[pl.ds(0, 2), b1, b0, u - 1, part, cols]

    def l1_copy(u):
        return wcopy(dr1r.at[unit_rows(u), awayc], lr1.at[u], l1_s.at[u], l1_r.at[u], pair)

    def l1(u, lhs):
        dr1r[unit_rows(u), :] = mm(lhs, tok[...]).astype(BF16)
        start(l1_copy(u))

    def z_copy(u, i):
        v = line(i)
        return wcopy(zs.at[u, :, piece(v), :], zr.at[u, qa], zs_s.at[u, i], zs_r.at[u, qa], line_dev(v))

    def owned(u, total):
        if groups > 1:
            grl[g, u] = total.astype(BF16)
            loop(lambda i: across(u, i).start(), 1, groups)

            def meet(i):
                v = lax.rem(g + i, groups)
                ref = grl.at[v, u]
                wcopy(ref, ref, gp_s.at[u, i], gp_r.at[u, v], v * OWN + o).wait_recv()

            loop(meet, 1, groups)
            total = lax.fori_loop(
                0, groups, lambda v, t: t + grl[v, u].astype(F32), jnp.zeros_like(total)
            )
        for k in range(2):
            m, first = (2, k * HR) if u == 0 else (k, (u - 1) * HR)
            old = mT[m, pl.ds(pl.multiple_of(first + qa * PR, PR), PR), keepc]
            new = (total[k] + 0.5 * old).astype(BF16)
            if u == 0:
                mom[2, b1, b0, k, piece(qa), keepc] = new
            else:
                mom[k, b1, b0, u - 1, piece(qa), keepc] = new

    def half_cols(b):
        return pl.ds(pl.multiple_of(b * HC, HC), HC)

    def d1_copy(i):
        v = member(i)
        src = zd.at[:, piece(v // 2), half_cols(lax.rem(v, 2))]
        return wcopy(src, zdr.at[o], zd_s.at[i], zd_r.at[o], g * OWN + v)

    def d1(lhs):
        zd[...] = mm(lhs, tok[...]).astype(BF16).reshape(2, HR, D)
        group_loop(lambda i: d1_copy(i).start())

    def d2_copy(v, i):
        ref = unit_mom(2, piece(v // 2), half_cols(lax.rem(v, 2)))
        return wcopy(ref, ref, ad_s.at[i], ad_r.at[v], g * OWN + member(i))

    def d2():
        zdr[o] = zd[:, piece(qa), keepc]

        def take(i):
            v = member(i)
            wcopy(zdr.at[v], zdr.at[v], zd_s.at[0], zd_r.at[v], g * OWN + v).wait_recv()

        group_loop(take)
        total = zdr[0].astype(F32)
        for v in range(1, OWN):
            total = total + zdr[v].astype(F32)
        owned(2, total)
        group_loop(lambda i: d2_copy(o, i).start())

    def l2(u):
        l1_copy(u).wait_recv()
        both = dr1r[unit_rows(u), keepc].astype(F32) + lr1[u].astype(F32)
        zs[u] = both.astype(BF16).reshape(2, HR, HC)
        loop(lambda i: z_copy(u, i).start(), 1, LINE)

    def across(u, i):
        ref = grl.at[g, u]
        return wcopy(ref, ref, gp_s.at[u, i], gp_r.at[u, g], lax.rem(g + i, groups) * OWN + o)

    def share(u, v, i):
        ref = unit_mom(u, piece(v), keepc)
        return wcopy(ref, ref, aq_s.at[u, i], aq_r.at[u, v], line_dev(line(i)))

    def l3(u):
        zr[u, qa] = zs[u, :, piece(qa), :]

        def take(i):
            v = line(i)
            wcopy(zr.at[u, v], zr.at[u, v], zs_s.at[u, 0], zs_r.at[u, v], line_dev(v)).wait_recv()

        loop(take, 1, LINE)
        total = zr[u, 0].astype(F32)
        for v in range(1, LINE):
            total = total + zr[u, v].astype(F32)
        owned(u, total)
        loop(lambda i: share(u, qa, i).start(), 1, LINE)

    def half_copy(u, cols):
        ref = unit_mom(u, pl.ds(0, HR), cols)
        return wcopy(ref, ref, ap_s.at[u], ap_r.at[u], pair)

    def l4(u):
        loop(lambda i: share(u, line(i), i).wait_recv(), 1, LINE)
        half_copy(u, keepc).start()

    fans = {0: [(0, 2, 1)], 1: [(1, 0, 0), (2, 1, 1)], 2: [(3, 0, 0), (4, 1, 1)]}

    def fan_ref(u, m, t):
        low = lax.rem(t, 2)
        return mom.at[2, t // 2, low] if u == 0 else mom.at[m, t // 2, low, u - 1]

    def near_copy(u, f, m, c):
        return ncopy(fan_ref(u, m, n), fan_ref(u, m, n), la_s.at[f, 0], la_r.at[f, n], c + 2 * b1)

    def far_copy(u, f, m, c):
        return ncopy(fan_ref(u, m, n), fan_ref(u, m, n), la_s.at[f, 1], la_r.at[f, n], c + 2 * (1 - b1))

    def l5(u):
        if u < 2:
            half_copy(u, awayc).wait_recv()
        else:
            group_loop(lambda i: d2_copy(member(i), i).wait_recv())
        for f, m, c in fans[u]:
            far_copy(u, f, m, c).start()

            @pl.when(b0 != c)
            def _():
                near_copy(u, f, m, c).start()

    def fan_wait(u, f, m):
        for x in (1, 2, 3):
            t = rel(x)
            ncopy(fan_ref(u, m, t), fan_ref(u, m, t), la_s.at[0, 0], la_r.at[f, t], t).wait_recv()

    def vec_copy(buf, ss, rs, i, v):
        return wcopy(buf.at[v], buf.at[v], ss.at[i], rs.at[v], g * OWN + member(i))

    def vec_across(buf, ss, rs, i, v):
        ref = buf.at[OWN + v]
        return wcopy(ref, ref, ss.at[OWN + i], rs.at[OWN + v], lax.rem(g + i, groups) * OWN + o)

    def vec_send(*where):
        group_loop(lambda i: vec_copy(*where, i, o).start())

    def vec_sum(buf, ss, rs):
        group_loop(lambda i: vec_copy(buf, ss, rs, i, member(i)).wait_recv())
        zero = jnp.zeros(buf.shape[1:], F32)
        total = lax.fori_loop(0, OWN, lambda v, t: t + buf[v], zero)
        if groups > 1:
            buf[OWN + g] = total
            group_loop(lambda i: vec_across(buf, ss, rs, i, g).start(), 1, groups)
            group_loop(
                lambda i: vec_across(buf, ss, rs, i, lax.rem(g + i, groups)).wait_recv(), 1, groups
            )
            total = lax.fori_loop(0, groups, lambda v, t: t + buf[OWN + v], zero)
        return total

    def vec_done(buf, ss, rs):
        group_loop(lambda i: vec_copy(buf, ss, rs, i, o).wait_send())
        if groups > 1:
            group_loop(lambda i: vec_across(buf, ss, rs, i, g).wait_send(), 1, groups)

    def over_copy(m):
        return ncopy(eys.at[m], eyr.at[m], g3_s.at[m], g3_r.at[m], n2)

    def chip_sum(m, y, part):
        return gst[m, b0, y, part, :].astype(F32) + gr1[m, y, part, :].astype(F32)

    def early_over(m):
        ncopy(gst.at[m, b0], gr1.at[m], g1_s.at[m], g1_r.at[m], n1).wait_recv()
        eys[m] = chip_sum(m, 1 - b1, slice(None)).astype(BF16)
        start(over_copy(m))

    def pair_copy(m):
        return wcopy(es1.at[m], er1.at[m], g2_s.at[m], g2_r.at[m], pair)

    def early_pair(m):
        over_copy(m).wait_recv()
        es1[m] = (chip_sum(m, b1, away) + eyr[m, away, :].astype(F32)).astype(BF16)
        start(pair_copy(m))

    def e_line(m, i):
        u = line(i)
        return wcopy(zse.at[m, piece(u), :], zre.at[m, qa], ez_s.at[m, i], ez_r.at[m, qa], line_dev(u))

    def early_line(m):
        pair_copy(m).wait_recv()
        total = chip_sum(m, b1, keep) + eyr[m, keep, :].astype(F32) + er1[m].astype(F32)
        zse[m] = total.astype(BF16)
        loop(lambda i: e_line(m, i).start(), 1, LINE)

    def e_across(m, i):
        ref = grp.at[g, m]
        return wcopy(ref, ref, gp_s.at[3 + m, i], gp_r.at[3 + m, g], lax.rem(g + i, groups) * OWN + o)

    def e_swap(m, y):
        ref = mom.at[3 + m, y, b0, pb, piece(qa), :]
        return ncopy(ref, ref, ey_s.at[m], ey_r.at[m], n2)

    def early_sum(m):
        zre[m, qa] = zse[m, piece(qa), :]

        def take(i):
            v = line(i)
            ref = zre.at[m, v]
            wcopy(ref, ref, ez_s.at[m, 0], ez_r.at[m, v], line_dev(v)).wait_recv()

        loop(take, 1, LINE)
        total = zre[m, 0].astype(F32)
        for v in range(1, LINE):
            total = total + zre[m, v].astype(F32)
        if groups > 1:
            grp[g, m] = total.astype(BF16)
            loop(lambda i: e_across(m, i).start(), 1, groups)

            def meet(i):
                v = lax.rem(g + i, groups)
                ref = grp.at[v, m]
                wcopy(ref, ref, gp_s.at[3 + m, i], gp_r.at[3 + m, v], v * OWN + o).wait_recv()

            loop(meet, 1, groups)
            total = lax.fori_loop(
                0, groups, lambda v, t: t + grp[v, m].astype(F32), jnp.zeros_like(total)
            )
        old = mT[3 + m, pl.ds(pl.multiple_of(pb * HR + qa * PR, PR), PR), :]
        mom[3 + m, b1, b0, pb, piece(qa), :] = (total + 0.5 * old).astype(BF16)
        start(e_swap(m, b1))

    def e_share(m, u, i):
        ref = mom.at[3 + m, :, b0, pb, piece(u), :]
        return wcopy(ref, ref, aq_s.at[3 + m, i], aq_r.at[3 + m, u], line_dev(line(i)))

    def early_back(m):
        e_swap(m, 1 - b1).wait_recv()
        loop(lambda i: e_share(m, qa, i).start(), 1, LINE)

    def e_half(m, b):
        ref = mom.at[3 + m, :, b0, b]
        return wcopy(ref, ref, ap_s.at[3 + m], ap_r.at[3 + m], pair)

    def early_half(m):
        loop(lambda i: e_share(m, line(i), i).wait_recv(), 1, LINE)
        start(e_half(m, pb))

    def e_near(m, c):
        ref = mom.at[3 + m, :, c]
        return ncopy(ref, ref, ow_s.at[m], ow_r.at[m], n1)

    def early_near(m):
        e_half(m, 1 - pb).wait_recv()

        @pl.when(b0 != m % 2)
        def _():
            e_near(m, b0).start()

    def vec_early():
        for x in (1, 2, 3):
            arrived(vecs.at[rel(x)], vn_s.at[x], vn_r.at[x], rel(x))
        vecw[o] = ((vecs[0] + vecs[1]) + vecs[2]) + vecs[3]
        vec_send(vecw, vw_s, vw_r)

    plan = {
        ("a", 0): [(early_over, 0)],
        ("a", 1): [(early_over, 1)],
        ("a", 2): [(early_over, 2)],
        (0, 1, 0): [(early_pair, 0)],
        (0, 1, 1): [(l2, 0)],
        (0, 2, 0): [(early_pair, 1)],
        (0, 3, 0): [(early_pair, 2), (early_line, 0)],
        (0, 3, 1): [(l3, 0)],
        (1, 0, 0): [(early_line, 1)],
        (1, 1, 0): [(early_line, 2), (early_sum, 0)],
        (1, 1, 1): [(l4, 0), (l2, 1)],
        (1, 2, 0): [(early_sum, 1)],
        (1, 2, 1): [(early_back, 0)],
        (1, 3, 0): [(early_sum, 2), (l5, 0)],
        (1, 3, 1): [(l3, 1)],
    }

    def after(i, key):
        for k in range(NAR):
            point = (key[0], k) + key[1:]
            if point in plan:
                @pl.when(i == k)
                def _():
                    held = len(pending)
                    for fn, arg in plan[point]:
                        fn(arg)
                    del pending[held:]

    dkT[...] = jnp.zeros_like(dkT)
    dvT[...] = jnp.zeros_like(dvT)
    lane = lax.broadcasted_iota(jnp.int32, (TB, CW), 1)
    low_lane = lane < HD

    def backward_v(i, _):
        t = rel(i)
        rr = rows(t, TB)

        @pl.when(i > 0)
        def _():
            for c in range(TB // MID):
                dst = dcr.at[pl.ds(pl.multiple_of(t * TB + c * MID, MID), MID)]
                ncopy(
                    dcst.at[pl.ds(c * MID, MID), mycols], dst, dc_sem.at[i, c], dc_rem.at[i, c], t
                ).wait_recv()

        dcs = (dcr[rr, :].astype(F32) * rln[rr, :]).astype(BF16)
        full = dcs.astype(F32)
        prod = full * ctxn[rr, :]
        delta = (
            jnp.sum(jnp.where(low_lane, prod, 0.0), axis=1, keepdims=True),
            jnp.sum(jnp.where(low_lane, 0.0, prod), axis=1, keepdims=True),
        )
        dcT = full.T.astype(BF16)
        for h in range(2):
            hs = slice(h * HD, (h + 1) * HD)
            top = delta[h].astype(BF16).astype(F32)
            tail = delta[h] - top
            base = (1 - h) * HD
            extra = jnp.where(lane == base, -top, jnp.where(lane == base + 1, -tail, 0.0))
            qp[h, rr, 0:CW] = jnp.where(low_lane == (h == 0), full, extra).astype(BF16)
            dvT[hs, :] += mm(dcT[hs, :], e_ref[h, rr, :])
        after(i, ("a",))
        return 0

    lax.fori_loop(0, NAR, backward_v, 0)
    gT[2 * CW:, :] = dvT[...].astype(BF16)
    l1(0, gT[2 * CW:, :])
    for k in range(3):
        ncopy(gst.at[k, 1 - b0], gr1.at[k], g1_s.at[k], g1_r.at[k], n1).wait_send()

    def backward(h):
        hs = slice(h * HD, (h + 1) * HD)
        ks = slice(CW + h * HD, CW + (h + 1) * HD)

        def block(i, _):
            rr = rows(rel(i), TB)
            s_ref[...] = mm(qp[h, rr, 0:CW], vTp[h])
            ds = e_ref[h, rr, :] * s_ref[...].astype(BF16)
            gT[hs, rr] = (mm_nt(kTp[h, hs, :], ds) * 0.125).astype(BF16)
            after(i, (h, 0))
            dkT[hs, :] += mm(qT[hs, rr], ds)
            after(i, (h, 1))
            return 0

        lax.fori_loop(0, NAR, block, 0)
        gT[ks, :] = dkT[hs, :].astype(BF16)
        lhs = jnp.concatenate([gT[hs, :], gT[ks, :]], axis=0)
        if h == 0:
            l1(1, lhs)
        else:
            d1(lhs)

    backward(0)
    backward(1)

    def dx(t):
        return mm(wqkv[...], gT[:, rows(t, TB)])

    both_rows = pl.ds(pl.multiple_of(b1 * 2 * CW, 2 * CW), 2 * CW)
    XB = s_ref.at[:, 0:D]

    def newton_begin(m):
        xin = mom[m].reshape(D, D).astype(F32)
        XB[...] = xin * (1.0 / (jnp.sqrt(jnp.sum(xin * xin)) + 1e-07))

    def newton_step():
        x = XB[...]
        xl = x.astype(BF16)
        a = mm_nt(xl, xl)
        al = a.astype(BF16)
        p = (COEF_B * a + COEF_C * mm(al, al)).astype(BF16)
        XB[...] = COEF_A * x + mm(p, xl)

    def orth(m):
        return gst.at[m // 2, lax.rem(m, 2), 0]

    def swap(m, k):
        return ncopy(gst.at[k, 0, 1], orth(m), sw_s.at[k], sw_r.at[k], n1)

    def newton_last(m, k):
        xl = XB[...].astype(BF16)
        xo = XB[both_rows, :]
        a = mm_nt(xo.astype(BF16), xl).astype(BF16)
        y = mm(a, xl)
        z = mm_nt(y.astype(BF16), xl).astype(BF16)
        res = COEF_A * xo + COEF_B * y + COEF_C * mm(z, xl)
        first, second = res[0:CW], res[CW:]
        gst[m // 2, lax.rem(m, 2), 0] = jnp.where(b0 == 0, first, second).astype(BF16)
        gst[k, 0, 1] = jnp.where(b0 == 0, second, first).astype(BF16)
        start(swap(m, k))

    def dx2_copy(c):
        cols = slice(c * MID, (c + 1) * MID)
        return ncopy(dxs2.at[:, cols], dxr2.at[:, cols], dx2_s.at[c], dx2_r.at[c], n2)

    dxs[1][...] = dx(n3).astype(BF16)
    start(ncopy(dxs[1], dxr1.at[1], dx1_s.at[1], dx1_r.at[1], n1))
    dxs[0][...] = dx(n1).astype(BF16)
    start(ncopy(dxs[0], dxr1.at[0], dx1_s.at[0], dx1_r.at[0], n1))
    early_back(1)
    over = dx(n2)
    one = jnp.ones((8, LEN), BF16)
    upper_rows = lax.broadcasted_iota(jnp.int32, (8, CW), 0) < 4
    lv[o] = jnp.where(upper_rows, mm_nt(one, gT[0:CW, :]), mm_nt(one, gT[2 * CW:, :]))
    ncopy(dxs[1], dxr1.at[1], dx1_s.at[1], dx1_r.at[1], n1).wait_recv()
    dxs2[...] = (over + dxr1[1].astype(F32)).astype(BF16)
    start(dx2_copy(0))
    early_half(0)
    l4(1)
    dxo = dx(n).T
    for k in range(NAR):
        cols = slice(k * CW, (k + 1) * CW)
        ograd[:, cols] = dxo[:, cols] + win_f[k]
    d2()
    settled = pending[:]
    pending.clear()
    early_back(2)
    early_near(0)

    @pl.when(b0 == 0)
    def _():
        e_near(0, 1).wait_recv()

    @pl.when(b0 == 1)
    def _():
        fan_wait(0, 0, 2)

    newton_begin(3 - b0)
    newton_step()
    early_half(1)
    l5(1)
    newton_step()
    vec_early()
    vec_send(lv, lv_s, lv_r)
    newton_last(3 - b0, 1)
    l5(2)
    early_near(1)
    early_half(2)

    def fans_wait():
        fan_wait(1, 1 + b0, b0)
        fan_wait(2, 3 + b0, b0)

    for c in settled:
        c.wait_send()
    for k in range(3):
        loop(lambda i: e_line(k, i).wait_send(), 1, LINE)
        if k < 2:
            loop(lambda i: z_copy(k, i).wait_send(), 1, LINE)
            loop(lambda i: share(k, qa, i).wait_send(), 1, LINE)
    group_loop(lambda i: d1_copy(i).wait_send())

    @pl.when(b0 == 0)
    def _():
        fans_wait()

    @pl.when(b0 == 1)
    def _():
        e_near(1, 0).wait_recv()

    start(dx2_copy(1))
    newton_begin(4 * b0)
    newton_step()
    newton_step()
    newton_last(4 * b0, 2)
    early_near(2)
    l_mom = pltpu.make_async_copy(mom.at[:, b1, b0], omom_h, loc_sem.at[8])
    l_mom.start()
    ovec[...] = vec_sum(vecw, vw_s, vw_r)
    late = vec_sum(lv, lv_s, lv_r)
    ovec2[0:1, :] = late[0:1]
    ovec2[1:2, :] = late[4:5]
    ovec2[2:3, :] = ovec[6:7, mycols]
    ovec2[3:8, :] = jnp.zeros((5, CW), F32)

    @pl.when(b0 == 0)
    def _():
        e_near(2, 1).wait_recv()

    @pl.when(b0 == 1)
    def _():
        fans_wait()

    newton_begin(5 - 4 * b0)
    newton_step()
    newton_step()
    newton_last(5 - 4 * b0, 0)

    ncopy(dxs[0], dxr1.at[0], dx1_s.at[0], dx1_r.at[0], n1).wait_recv()
    for c in (0, 1):
        dx2_copy(c).wait_recv()
    ograd_b[...] = (ograd[...] + (dxr1[0].astype(F32) + dxr2[...].astype(F32)).T).astype(BF16)
    l_ograd = pltpu.make_async_copy(ograd_b, ograd_h, loc_sem.at[7])
    l_ograd.start()
    swap(2 + b0, 1).wait_recv()
    swap(4 * (1 - b0), 2).wait_recv()
    swap(1 + 4 * b0, 0).wait_recv()
    l_orth = pltpu.make_async_copy(gst.at[:, :, 0], oorth_h, loc_sem.at[9])
    l_orth.start()

    for m in range(3):
        pending.extend((pair_copy(m), over_copy(m), e_swap(m, b1)))
        if m < 2:
            pending.append(half_copy(m, keepc))
        for f, k, c in fans[m]:
            pending.append(far_copy(m, f, k, c))

            @pl.when(b0 != c)
            def _():
                near_copy(m, f, k, c).wait_send()

        @pl.when(b0 != m % 2)
        def _():
            e_near(m, b0).wait_send()

    for c in pending:
        c.wait_send()
    vec_done(vecw, vw_s, vw_r)
    vec_done(lv, lv_s, lv_r)
    group_loop(lambda i: d2_copy(o, i).wait_send())
    for k in range(3):
        loop(lambda i: e_share(k, qa, i).wait_send(), 1, LINE)
        if groups > 1:
            loop(lambda i: across(k, i).wait_send(), 1, groups)
            loop(lambda i: e_across(k, i).wait_send(), 1, groups)
    l_otok.wait()
    l_ograd.wait()
    l_mom.wait()
    l_orth.wait()


def run_layer(wide, tokens, cotangent, seg, pad, gen, in_w, out_w, in_m, out_m, shared, split):
    any_ = pl.BlockSpec(memory_space=pl.ANY)
    vm = pl.BlockSpec(memory_space=pltpu.VMEM)
    V = pltpu.VMEM
    dma = lambda *s: pltpu.SemaphoreType.DMA(s)
    one = pltpu.SemaphoreType.DMA
    groups = wide // OWN
    vslots = OWN + (groups if groups > 1 else 0)
    scratch = [
        V((LEN, D), BF16), V((TB, D), BF16), V((NAR, 16, CW), F32),
        V((4, D, CW), F32), V((2, CW, D), F32), V((6, CW, D), F32),
        V((3 * CW, D), BF16), V((D, 3 * CW), BF16),
        V((D, D), BF16), V((2, D, D), BF16), V((2, CW, CW), F32),
        V((2, LEN, 2 * CW), BF16), V((2, 2 * CW, LEN), BF16), V((2, CW, LEN), BF16), V((CW, LEN), BF16),
        V((LEN, CW), F32), V((TB, LEN), F32), V((2, LEN, LEN), BF16),
        V((LEN, CW), F32), V((LEN, CW), BF16), V((TB, D), BF16),
        V((TB, D), BF16), V((TB, D), BF16), V((TB, D), BF16), V((TB, D), BF16), V((TB, D), BF16),
        V((TB, D), BF16), V((LEN, CW), BF16),
        V((NAR, 8, D), F32), V((vslots, 8, D), F32), V((CW, LEN), F32), V((CW, LEN), F32), V((3 * CW, LEN), BF16),
        V((3, 2, 2, CW, D), BF16), V((3, 2, CW, D), BF16), V((3, CW, D), BF16), V((3, CW, D), BF16),
        V((3, HR, D), BF16), V((3, HR, D), BF16), V((3, HR, D), BF16), V((3, LINE, PR, D), BF16), V((3, CW, HC), BF16),
        V((2, 2, HR, HC), BF16), V((2, LINE, 2, PR, HC), BF16), V((2, HR, D), BF16), V((OWN, 2, PR, HC), BF16),
        V((vslots, 8, CW), F32),
        V((6, 2, 2, 2, HR, D), BF16),
        V((groups, 3, PR, D) if groups > 1 else (1, 1, PR, D), BF16),
        V((groups, 3, 2, PR, HC) if groups > 1 else (1, 1, 1, PR, HC), BF16),
        V((2, D, TB), BF16), V((D, TB), BF16),
        dma(10), dma(4), dma(4), dma(2), dma(2), dma(4), dma(4), dma(3, 2), dma(3, 2), dma(1, 2), dma(1, 2),
        dma(4), dma(4), dma(4, TB // MID), dma(4, TB // MID), dma(4), dma(4), dma(vslots), dma(vslots),
        dma(vslots), dma(vslots),
        dma(3), dma(3), dma(3), dma(3), dma(3), dma(3), dma(3), dma(3), dma(3, LINE), dma(3, LINE),
        dma(OWN), dma(OWN), dma(OWN), dma(OWN),
        dma(6, groups), dma(6, groups),
        dma(6, LINE), dma(6, LINE), dma(6), dma(6),
        dma(3), dma(3), dma(3, LINE), dma(3, LINE), dma(3), dma(3), dma(5, 2), dma(5, 4), dma(3), dma(3),
        dma(2), dma(2), dma(2), dma(2),
    ]
    return pl.pallas_call(
        functools.partial(layer_kernel, wide),
        out_shape=[
            jax.ShapeDtypeStruct((TB, D), BF16),
            jax.ShapeDtypeStruct((TB, D), BF16),
            jax.ShapeDtypeStruct((6, 2, HR, D), BF16),
            jax.ShapeDtypeStruct((3, 2, CW, D), BF16),
            jax.ShapeDtypeStruct((8, D), F32),
            jax.ShapeDtypeStruct((8, CW), F32),
        ],
        in_specs=[any_, any_, vm, vm, vm, any_, any_, any_, any_, vm, vm],
        out_specs=[any_, any_, any_, any_, vm, vm],
        scratch_shapes=scratch,
        compiler_params=pltpu.CompilerParams(
            collective_id=0, has_side_effects=True, vmem_limit_bytes=62 * MB
        ),
        name="layer",
    )(tokens, cotangent, seg, pad, gen, in_w, out_w, in_m, out_m, shared, split)


def muon_step(weights, orthogonal):
    return weights - 0.2 * (0.2 * math.sqrt(D) * orthogonal + 0.01 * weights)


def adam_step(values, moment_one, moment_two, gradient):
    moment_one = 0.9 * moment_one + 0.1 * gradient
    moment_two = 0.999 * moment_two + 0.001 * gradient * gradient
    step_ratio = (
        moment_one / (1.0 - 0.9**STEP) / (jnp.sqrt(moment_two / (1.0 - 0.999**STEP)) + 1e-08)
    )
    return (moment_one, moment_two, values - 0.3 * (step_ratio + 0.01 * values))


def blend(average, weights):
    return 0.6 * average + 0.4 * weights


def update_kernel(
    otok, ograd, mom, orth, in_w, out_w, in_a, out_a, vec, vec2,
    sv, s1, s2, sa, pv, p1, p2, pa,
    tok_o, grad_o, inm_o, outm_o, inw_o, outw_o, inl_o, outl_o, ina_o, outa_o,
    s1_o, s2_o, sv_o, sa_o, p1_o, p2_o, pv_o, pa_o,
    mom_b, orth_b, inw_b, outw_b, ina_b, outa_b,
    inm_v, outm_v, inw_v, outw_v, inl_v, outl_v, ina_v, outa_v, grad_v, grad_b, tok_v, thru, rsem, wsem,
):
    whole = [
        pltpu.make_async_copy(ograd, grad_b, thru.at[0]),
        pltpu.make_async_copy(otok, tok_v, thru.at[1]),
    ]
    back = [
        pltpu.make_async_copy(grad_v, grad_o, thru.at[2]),
        pltpu.make_async_copy(tok_v, tok_o, thru.at[3]),
    ]
    reads, writes = [], []
    for k in range(6):
        j, inner = (k, True) if k < 4 else (k - 4, False)
        srcs = (mom.at[k], orth.at[k // 2, k % 2], (in_w if inner else out_w).at[j], (in_a if inner else out_a).at[j])
        dsts = (
            mom_b.at[k], orth_b.at[k], (inw_b if inner else outw_b).at[j], (ina_b if inner else outa_b).at[j],
        )
        reads.append([pltpu.make_async_copy(s, d, rsem.at[k, i]) for i, (s, d) in enumerate(zip(srcs, dsts))])
        bufs = (inm_v, inw_v, inl_v, ina_v) if inner else (outm_v, outw_v, outl_v, outa_v)
        outs = (inm_o, inw_o, inl_o, ina_o) if inner else (outm_o, outw_o, outl_o, outa_o)
        writes.append(
            [pltpu.make_async_copy(s.at[j], d.at[j], wsem.at[k, i]) for i, (s, d) in enumerate(zip(bufs, outs))]
        )
    for c in reads[0]:
        c.start()
    for c in reads[1]:
        c.start()
    for c in whole:
        c.start()
    for k in range(2, 6):
        for c in reads[k]:
            c.start()
    s1_o[...], s2_o[...], shared_new = adam_step(sv[...], s1[...], s2[...], vec[0:6, :])
    sv_o[...] = shared_new
    sa_o[...] = blend(sa[...], shared_new)
    p1_o[...], p2_o[...], split_new = adam_step(pv[...], p1[...], p2[...], vec2[0:3, :])
    pv_o[...] = split_new
    pa_o[...] = blend(pa[...], split_new)
    for k in range(6):
        if k in (1, 2):
            whole[k - 1].wait()
            if k == 1:
                grad_v[...] = grad_b[...].astype(F32)
            back[k - 1].start()
        for c in reads[k]:
            c.wait()
        if k < 4:
            inm_v[k] = mom_b[k].reshape(CW, D).astype(F32).T
            new = muon_step(inw_b[k], orth_b[k].astype(F32).T)
            inw_v[k] = new
            inl_v[k] = new.astype(BF16)
            ina_v[k] = blend(ina_b[k], new)
        else:
            j = k - 4
            outm_v[j] = mom_b[k].reshape(CW, D).astype(F32)
            new = muon_step(outw_b[j], orth_b[k].astype(F32))
            outw_v[j] = new
            outl_v[j] = new.astype(BF16)
            outa_v[j] = blend(outa_b[j], new)
        for c in writes[k]:
            c.start()
    for c in back:
        c.wait()
    for k in range(6):
        for c in writes[k]:
            c.wait()


def run_update(*args):
    vm = pl.BlockSpec(memory_space=pltpu.VMEM)
    any_ = pl.BlockSpec(memory_space=pl.ANY)
    S = jax.ShapeDtypeStruct
    V = pltpu.VMEM
    inner, outer = (4, D, CW), (2, CW, D)
    return pl.pallas_call(
        update_kernel,
        out_shape=[
            S((TB, D), BF16), S((TB, D), F32), S(inner, F32), S(outer, F32), S(inner, F32), S(outer, F32),
            S(inner, BF16), S(outer, BF16), S(inner, F32), S(outer, F32),
        ]
        + [S((6, D), F32)] * 4
        + [S((3, CW), F32)] * 4,
        in_specs=[any_] * 8 + [vm] * 10,
        out_specs=[any_] * 10 + [vm] * 8,
        scratch_shapes=[
            V((6, 2, HR, D), BF16), V((6, CW, D), BF16), V(inner, F32), V(outer, F32), V(inner, F32), V(outer, F32),
            V(inner, F32), V(outer, F32), V(inner, F32), V(outer, F32), V(inner, BF16), V(outer, BF16),
            V(inner, F32), V(outer, F32), V((TB, D), F32), V((TB, D), BF16), V((TB, D), BF16),
            pltpu.SemaphoreType.DMA((4,)), pltpu.SemaphoreType.DMA((6, 4)), pltpu.SemaphoreType.DMA((6, 4)),
        ],
        compiler_params=pltpu.CompilerParams(vmem_limit_bytes=60 * MB),
        name="update",
    )(*args)


def body(
    wide, tokens, cotangent, segments, padding, generative, in_weights, out_weights, in_momenta,
    out_momenta, in_average, out_average, shared_values, shared_moment1, shared_moment2,
    shared_average, split_values, split_moment1, split_moment2, split_average,
):
    flags = [v.reshape(TB // CW, CW) for v in (segments, padding, generative)]
    otok, ograd, mom, orth, vec, vec2 = run_layer(
        wide, tokens, cotangent, *flags, in_weights, out_weights, in_momenta, out_momenta,
        shared_values, split_values,
    )
    return tuple(
        run_update(
            otok, ograd, mom, orth, in_weights, out_weights, in_average, out_average, vec, vec2,
            shared_values, shared_moment1, shared_moment2, shared_average,
            split_values, split_moment1, split_moment2, split_average,
        )
    )


def solution(mesh):
    rows = P(("wide", "narrow"), None)
    flat = P(("wide", "narrow"))
    cols = P(None, None, "narrow")
    outs = P(None, "narrow", None)
    vec = P(None, "narrow")
    return jax.shard_map(
        functools.partial(body, mesh.shape["wide"]),
        mesh=mesh,
        in_specs=(
            rows, rows, flat, flat, flat, cols, outs, cols, outs, cols, outs,
            P(), P(), P(), P(), vec, vec, vec, vec,
        ),
        out_specs=(
            rows, rows, cols, outs, cols, outs, cols, outs, cols, outs,
            P(), P(), P(), P(), vec, vec, vec, vec,
        ),
        check_vma=False,
    )
```

```python
import functools
import math

import jax
import jax.numpy as jnp
from jax import lax
from jax.experimental import pallas as pl
from jax.experimental.pallas import tpu as pltpu
from jax.sharding import PartitionSpec as P

D = 512
HD = 64
LEN = 2048
NS_ITERS = 3
STEP = 10
NAR = 4
TB = LEN // NAR
CW = D // NAR
OWN = 8
LINE = OWN // 2
HR = CW // 2
HC = D // 2
PR = CW // OWN
MID = 256

F32 = jnp.float32
BF16 = jnp.bfloat16
MESH = pl.DeviceIdType.MESH

COEF_A = 3.4445
COEF_B = -4.775
COEF_C = 2.0315
NEG = -1e30
MB = 2**20


def mm(a, b):
    return jnp.dot(a, b, preferred_element_type=F32)


def mm_nt(a, b):
    return lax.dot_general(a, b, (((1,), (1,)), ((), ())), preferred_element_type=F32)


def mm_tn(a, b):
    return lax.dot_general(a, b, (((0,), (0,)), ((), ())), preferred_element_type=F32)


def layer_kernel(wide, *refs):
    (
        tok_h, cot_h, seg_i, pad_i, gen_i, win_h, wout_h, min_h, mout_h, shared, split,
        otok_h, ograd_h, omom_h, oorth_h, ovec, ovec2,
        tok, cot, pay, win_f, wout_f, mT, wqkvT, wqkv, wup, wod, bcol,
        qp, kTp, vTp, qT, rdn, s_ref, e_ref, tops_n, ctxn, ctx_s, ctxf,
        hr, act, du, dr2r, dr1r, dcst, dcr, vecs, vecw, dkT, dvT, gT,
        gst, gr1, eys, eyr, es1, er1, zse, zre, lr1, zs, zr, zd, zdr, lv, mom, grp, grl,
        dxr1, dxr2,
        loc_sem, ag_s, ag_r, rly_s, rly_r, pay_s, pay_r, wg_s, wg_r, wr_s, wr_r,
        ctx_sem, ctx_rem, dc_sem, dc_rem, vn_s, vn_r, vw_s, vw_r, lv_s, lv_r,
        g1_s, g1_r, g2_s, g2_r, g3_s, g3_r, l1_s, l1_r, zs_s, zs_r, zd_s, zd_r, ad_s, ad_r, gp_s, gp_r,
        aq_s, aq_r, ap_s, ap_r, ow_s, ow_r, ez_s, ez_r, ey_s, ey_r, la_s, la_r, sw_s, sw_r, dx1_s, dx1_r, dx2_s, dx2_r,
    ) = refs
    n = lax.axis_index("narrow")
    w = lax.axis_index("wide")
    groups = wide // OWN
    g = w // OWN if groups > 1 else 0
    o = lax.rem(w, OWN) if groups > 1 else w
    b0 = lax.rem(n, 2)
    b1 = n // 2

    def rel(x):
        return lax.rem(b0 + x % 2, 2) + 2 * lax.rem(b1 + x // 2, 2)

    n1, n2, n3 = rel(1), rel(2), rel(3)

    def rows(t, size):
        return pl.ds(pl.multiple_of(t * size, size), size)

    def ncopy(src, dst, ssem, rsem, t):
        return pltpu.make_async_remote_copy(
            src_ref=src, dst_ref=dst, send_sem=ssem, recv_sem=rsem,
            device_id={"narrow": t}, device_id_type=MESH,
        )

    def wcopy(src, dst, ssem, rsem, u):
        return pltpu.make_async_remote_copy(
            src_ref=src, dst_ref=dst, send_sem=ssem, recv_sem=rsem,
            device_id={"wide": u}, device_id_type=MESH,
        )

    pending = []

    def start(copy):
        copy.start()
        pending.append(copy)
        return copy

    own = rows(n, TB)
    ograd = s_ref.at[:, 3 * D:4 * D]
    ograd_b = hr
    rln = rdn
    otok = cot
    dxs, dxs2 = (act, du), dr2r

    l_tok = pltpu.make_async_copy(tok_h, tok.at[own], loc_sem.at[0])
    l_win = pltpu.make_async_copy(win_h, win_f, loc_sem.at[1])
    l_wout = pltpu.make_async_copy(wout_h, wout_f, loc_sem.at[2])
    l_cot = pltpu.make_async_copy(cot_h, cot, loc_sem.at[3])
    l_min = pltpu.make_async_copy(min_h, win_f, loc_sem.at[4])
    l_mout = pltpu.make_async_copy(mout_h, mT.at[pl.ds(4, 2)], loc_sem.at[5])
    for c in (l_tok, l_win, l_wout, l_cot, l_mout):
        c.start()

    barrier = pltpu.get_barrier_semaphore()
    for x in (1, 2, 3):
        pl.semaphore_signal(barrier, inc=1, device_id={"narrow": rel(x)}, device_id_type=MESH)

    def greet(i, c):
        pl.semaphore_signal(
            barrier, inc=1, device_id={"wide": g * OWN + lax.rem(o + i, OWN)}, device_id_type=MESH
        )
        return c

    lax.fori_loop(1, OWN, greet, 0)

    def greet_group(i, c):
        pl.semaphore_signal(
            barrier, inc=1, device_id={"wide": lax.rem(g + i, groups) * OWN + o}, device_id_type=MESH
        )
        return c

    if groups > 1:
        lax.fori_loop(1, groups, greet_group, 0)
    seg = seg_i[...]
    closed = jnp.logical_or(pad_i[...] != 0, gen_i[...] != 0)
    pay[n] = jnp.concatenate(
        [
            seg.astype(F32), jnp.where(closed, -1, seg).astype(F32),
            split[2:3, :], jnp.zeros((7, CW), F32),
        ],
        axis=0,
    )
    l_tok.wait()
    pl.semaphore_wait(barrier, 3 + (OWN - 1) + (groups - 1))

    half = TB // 2

    def ag_rows(t, c):
        return tok.at[pl.ds(pl.multiple_of(t * TB + c * half, half), half)]

    for x in (1, 2, 3):
        start(ncopy(pay.at[n], pay.at[n], pay_s.at[x], pay_r.at[x], rel(x)))
    for c in (0, 1):
        start(ncopy(ag_rows(n, c), ag_rows(n, c), ag_s.at[2 + c], ag_r.at[2 + c], n2))
    for c in (0, 1):
        start(ncopy(ag_rows(n, c), ag_rows(n, c), ag_s.at[c], ag_r.at[c], n1))

    def arrived(slot, sem_s, sem_r, t):
        ncopy(slot, slot, sem_s, sem_r, t).wait_recv()

    l_win.wait()
    for k in range(3):
        piece = win_f[k]
        wqkvT[k * CW:(k + 1) * CW, :] = piece.T.astype(BF16)
        wqkv[:, k * CW:(k + 1) * CW] = piece.astype(BF16)
    mycols = pl.ds(pl.multiple_of(n * CW, CW), CW)
    wup[:, mycols] = win_f[3].astype(BF16)
    l_min.start()
    l_wout.wait()
    for k in range(2):
        wod[k, mycols, :] = wout_f[k].astype(BF16)

    def wg_list(sems, semr, x, t, target):
        cols = pl.ds(pl.multiple_of(t * CW, CW), CW)
        return [
            ncopy(wod.at[:, cols, :], wod.at[:, cols, :], sems.at[x, 0], semr.at[x, 0], target),
            ncopy(wup.at[:, cols], wup.at[:, cols], sems.at[x, 1], semr.at[x, 1], target),
        ]

    bcol[0] = jnp.broadcast_to(split[0:1, :], (CW, CW)).T
    bcol[1] = jnp.broadcast_to(split[1:2, :], (CW, CW)).T

    def project(t, c):
        rr = pl.ds(pl.multiple_of(t * TB + c * half, half), half)
        tb = tok[rr, :]
        qk = mm(tb, wqkv[:, 0:2 * CW])
        q = (qk[:, :CW] + split[0:1, :]).astype(BF16)
        k = qk[:, CW:].astype(BF16)
        q8 = q.astype(F32) * 0.125
        prod = q8 * k.astype(F32)
        low = lax.broadcasted_iota(jnp.int32, (half, CW), 1) < HD
        d0 = jnp.sum(jnp.where(low, prod, 0.0), axis=1, keepdims=True)
        d1 = jnp.sum(jnp.where(low, 0.0, prod), axis=1, keepdims=True)
        rdn[rr, :] = jnp.where(low, d0, d1)
        lane1 = lax.broadcasted_iota(jnp.int32, (CW, CW), 1).astype(F32)
        lowj = lane1 < HD
        for j in range(half // CW):
            seg = jnp.broadcast_to(pay[t, pl.ds(c * (half // CW) + j, 1), :], (CW, CW)).T
            part = q8[j * CW:(j + 1) * CW, :]
            hot = lambda base: jnp.where(seg == lane1 + base, 1.0, 0.0)
            rj = pl.ds(pl.multiple_of(t * TB + c * half + j * CW, CW), CW)
            qp[0, rj, 0:CW] = jnp.where(lowj, part, hot(-float(HD))).astype(BF16)
            qp[1, rj, 0:CW] = jnp.where(lowj, hot(0.0), part).astype(BF16)
            rest = hot(float(HD)).astype(BF16)
            qp[0, rj, CW:] = rest
            qp[1, rj, CW:] = rest
        tT = mm_nt(wqkvT[...], tb)
        bq = jnp.concatenate([bcol[0]] * (half // CW), axis=1)
        bv = jnp.concatenate([bcol[1]] * (half // CW), axis=1)
        qT[:, rr] = ((tT[0:CW] + bq).astype(BF16).astype(F32) * 0.125).astype(BF16)
        kT = tT[CW:2 * CW].astype(BF16)
        vT = (tT[2 * CW:] + bv).astype(BF16)
        code = jnp.concatenate(
            [pay[t, pl.ds(4 + c * (half // CW) + j, 1), :] for j in range(half // CW)], axis=1
        )
        rowi = lax.broadcasted_iota(jnp.int32, (HD, half), 0).astype(F32)
        keep = lambda base: jnp.where(code == rowi + base, 0.0, NEG).astype(BF16)
        first, second, third = keep(0.0), keep(float(HD)), keep(float(2 * HD))
        ones = jnp.ones((HD, half), BF16)
        kTp[0, 0:HD, rr] = kT[0:HD]
        kTp[0, HD:CW, rr] = first
        kTp[1, 0:HD, rr] = first
        kTp[1, HD:CW, rr] = kT[HD:]
        vTp[0, 0:HD, rr] = vT[0:HD]
        vTp[0, HD:, rr] = ones
        vTp[1, 0:HD, rr] = ones
        vTp[1, HD:, rr] = vT[HD:]
        for h in range(2):
            kTp[h, CW:CW + HD, rr] = second
            kTp[h, CW + HD:, rr] = third

    def relayed(c):
        return ncopy(ag_rows(n2, c), ag_rows(n2, c), rly_s.at[c], rly_r.at[c], n1)

    def project_step(i, _):
        @pl.when(i == 2)
        def _():
            arrived(pay.at[n1], pay_s.at[1], pay_r.at[1], n1)
            arrived(ag_rows(n1, 0), ag_s.at[0], ag_r.at[0], n1)
            l_min.wait()
            for k in range(4):
                mT[k] = win_f[k].T

        @pl.when(i == 3)
        def _():
            arrived(ag_rows(n1, 1), ag_s.at[1], ag_r.at[1], n1)

        @pl.when(i == 4)
        def _():
            arrived(pay.at[n2], pay_s.at[2], pay_r.at[2], n2)
            arrived(pay.at[n3], pay_s.at[3], pay_r.at[3], n3)
            arrived(ag_rows(n2, 0), ag_s.at[2], ag_r.at[2], n2)
            relayed(0).start()

        @pl.when(i == 5)
        def _():
            arrived(ag_rows(n3, 0), rly_s.at[0], rly_r.at[0], n1)

        @pl.when(i == 6)
        def _():
            arrived(ag_rows(n2, 1), ag_s.at[3], ag_r.at[3], n2)
            relayed(1).start()
            for x in (2, 1):
                for c in wg_list(wg_s, wg_r, x, n, rel(x)):
                    c.start()

        @pl.when(i == 7)
        def _():
            arrived(ag_rows(n3, 1), rly_s.at[1], rly_r.at[1], n1)

        far = i // 4
        x = (1 - far) * (i // 2) + far * (2 + lax.rem(i, 2))
        c = (1 - far) * lax.rem(i, 2) + far * (i // 2 - 2)
        project(rel(x), c)
        return 0

    lax.fori_loop(0, NAR, project_step, 0)

    eye = lax.broadcasted_iota(jnp.int32, (CW, CW), 0) == lax.broadcasted_iota(jnp.int32, (CW, CW), 1)
    sh = s_ref.at[:, 0:2 * TB]
    near_keys = rows(b1, 2 * TB)
    far_keys = rows(1 - b1, 2 * TB)
    lane_low = lax.broadcasted_iota(jnp.int32, (TB, CW), 1) < HD

    def v_rows(h):
        return slice(0, HD + 16) if h == 0 else slice(HD - 16, CW)

    def both_heads(parts):
        num = jnp.concatenate([parts[0][:HD], parts[1][16:]], axis=0)
        den = jnp.concatenate(
            [
                jnp.broadcast_to(parts[0][HD:HD + 1], (HD, TB)),
                jnp.broadcast_to(parts[1][0:1], (HD, TB)),
            ],
            axis=0,
        )
        return num.T, den.T

    def attend_near(x, _):
        t = rel(x)
        rr = rows(t, TB)
        low = lax.rem(t, 2)
        parts, tops = [], []
        for h in range(2):
            sh[...] = mm(qp[h, rr, :], kTp[h, :, near_keys])
            for j in range(TB // CW):
                diag = rdn[pl.ds(pl.multiple_of(t * TB + j * CW, CW), CW), h * HD:h * HD + 1]
                cc = pl.ds(pl.multiple_of(low * TB + j * CW, CW), CW)
                sub = pl.ds(j * CW, CW)
                s_ref[sub, cc] = jnp.where(eye, diag, s_ref[sub, cc])
            sv = sh[...]
            top = jnp.max(sv, axis=1, keepdims=True)
            e = jnp.exp(sv - top).astype(BF16)
            e_ref[h, rr, near_keys] = e
            parts.append(mm_nt(vTp[h, v_rows(h), near_keys], e))
            tops.append(top)
        num, den = both_heads(parts)
        ctxn[rr, :] = num
        rln[rr, :] = den
        tops_n[low] = jnp.where(lane_low, tops[0], tops[1])
        return 0

    lax.fori_loop(0, 2, attend_near, 0)
    lax.fori_loop(NAR, 2 * NAR, project_step, 0)
    for x in (2, 1):
        pending.extend(wg_list(wg_s, wg_r, x, n, rel(x)))
    pending.extend((relayed(0), relayed(1)))

    def ctx_copy(x, t):
        return ncopy(
            ctx_s.at[rows(t, TB)], ctxf.at[:, mycols], ctx_sem.at[x], ctx_rem.at[x], t
        )

    def attend_far(i, _):
        t = rel(2 + i)
        rr = rows(t, TB)
        parts = []
        for h in range(2):
            s_ref[...] = mm(qp[h, rr, :], kTp[h])
            for j in range(TB // CW):
                cc = pl.ds(pl.multiple_of(t * TB + j * CW, CW), CW)
                diag = rdn[cc, h * HD:h * HD + 1]
                sub = pl.ds(j * CW, CW)
                s_ref[sub, cc] = jnp.where(eye, diag, s_ref[sub, cc])
            sv = s_ref[...]
            top = jnp.max(sv, axis=1, keepdims=True)
            e = jnp.exp(sv - top).astype(BF16)
            e_ref[h, rr, :] = e
            parts.append(mm_nt(vTp[h, v_rows(h), :], e))
        num, den = both_heads(parts)
        inv = 1.0 / den
        cn = num * inv
        ctxn[rr, :] = cn
        rln[rr, :] = inv
        ctx_s[rr, :] = cn.astype(BF16)
        ctx_copy(2 + i, t).start()
        return 0

    def attend_rest(i, _):
        t = rel(1 - i)

        @pl.when(i == 1)
        def _():
            for c in wg_list(wg_s, wg_r, 2, n2, n2):
                c.wait_recv()
            for c in wg_list(wr_s, wr_r, 0, n2, n1):
                c.start()

        rr = rows(t, TB)
        low = lax.rem(t, 2)
        parts, shrink = [], []
        for h in range(2):
            sh[...] = mm(qp[h, rr, :], kTp[h, :, far_keys])
            sv = sh[...]
            old = tops_n[low, :, h * HD:h * HD + 1]
            top = jnp.maximum(jnp.max(sv, axis=1, keepdims=True), old)
            less = jnp.exp(old - top)
            e = jnp.exp(sv - top).astype(BF16)
            e_ref[h, rr, far_keys] = e
            e_ref[h, rr, near_keys] = (e_ref[h, rr, near_keys].astype(F32) * less).astype(BF16)
            parts.append(mm_nt(vTp[h, v_rows(h), far_keys], e))
            shrink.append(less)
        num, den = both_heads(parts)
        less = jnp.where(lane_low, shrink[0], shrink[1])
        inv = 1.0 / (rln[rr, :] * less + den)
        cn = (ctxn[rr, :] * less + num) * inv
        ctxn[rr, :] = cn
        rln[rr, :] = inv
        ctx_s[rr, :] = cn.astype(BF16)

        @pl.when(i == 0)
        def _():
            ctx_copy(1, t).start()

        return 0

    lax.fori_loop(0, 2, attend_far, 0)
    lax.fori_loop(0, 2, attend_rest, 0)
    pending.extend(wg_list(wr_s, wr_r, 0, n2, n1))
    for x in (1, 2, 3):
        pending.append(ctx_copy(x, rel(x)))
    ctxf[:, mycols] = ctx_s[own, :]
    for c in wg_list(wg_s, wg_r, 1, n1, n1):
        c.wait_recv()
    for c in wg_list(wr_s, wr_r, 0, n3, n1):
        c.wait_recv()
    l_cot.wait()
    l_mout.wait()
    for x in (2, 3, 1):
        cols = pl.ds(pl.multiple_of(rel(x) * CW, CW), CW)
        ncopy(ctx_s.at[own], ctxf.at[:, cols], ctx_sem.at[x], ctx_rem.at[x], rel(x)).wait_recv()

    up_bias = jnp.concatenate([pay[t, 8:9, :] for t in range(NAR)], axis=1)
    vecs[n] = jnp.zeros((8, D), F32)

    def dc_copy(x, c, t, me):
        rr = pl.ds(c * MID, MID)
        cols = pl.ds(pl.multiple_of(t * CW, CW), CW)
        dst = dcr.at[pl.ds(pl.multiple_of(me * TB + c * MID, MID), MID)]
        return ncopy(dcst.at[rr, cols], dst, dc_sem.at[x, c], dc_rem.at[x, c], t)

    def middle(c, _):
        rr = pl.ds(pl.multiple_of(c * MID, MID), MID)
        ga1, be1, ga2, be2, ba, bd = (shared[k:k + 1, :] for k in range(6))
        x0 = tok[pl.ds(pl.multiple_of(n * TB + c * MID, MID), MID), :].astype(F32)
        r1 = x0 + (mm(ctxf[rr, :], wod[0]) + ba)
        c1 = r1 - jnp.mean(r1, axis=1, keepdims=True)
        s1 = lax.rsqrt(jnp.mean(c1 * c1, axis=1, keepdims=True) + 1e-05)
        x1 = c1 * s1
        hidden = x1 * ga1 + be1
        low = hidden.astype(BF16)
        hr[rr, :] = low
        upper = mm(low, wup[...]) + up_bias
        cdf = 0.5 * (1.0 + lax.erf(upper * (1.0 / math.sqrt(2.0))))
        pdf = jnp.exp(-0.5 * upper * upper) * (1.0 / math.sqrt(2.0 * math.pi))
        slope = cdf + upper * pdf
        a = (upper * cdf).astype(BF16)
        act[rr, :] = a
        r2 = hidden + (mm(a, wod[1]) + bd)
        c2 = r2 - jnp.mean(r2, axis=1, keepdims=True)
        s2 = lax.rsqrt(jnp.mean(c2 * c2, axis=1, keepdims=True) + 1e-05)
        x2 = c2 * s2
        dy = cot[rr, :].astype(F32)
        otok[rr, :] = (x2 * ga2 + be2).astype(BF16)
        dn = dy * ga2
        dr2 = s2 * (
            dn - jnp.mean(dn, axis=1, keepdims=True) - x2 * jnp.mean(dn * x2, axis=1, keepdims=True)
        )
        d2 = dr2.astype(BF16)
        dr2r[rr, :] = d2
        dup = (mm_nt(d2, wod[1]) * slope).astype(BF16)
        du[rr, :] = dup
        dh = dr2 + mm_nt(dup, wup[...])
        en = dh * ga1
        d1f = s1 * (
            en - jnp.mean(en, axis=1, keepdims=True) - x1 * jnp.mean(en * x1, axis=1, keepdims=True)
        )
        for k in range(NAR):
            win_f[k, rr, :] = d1f[:, k * CW:(k + 1) * CW]
        d1 = d1f.astype(BF16)
        dr1r[rr, :] = d1
        dcst[rr, :] = mm_nt(d1, wod[0]).astype(BF16)
        add = lambda v: jnp.sum(v, axis=0, keepdims=True)
        vecs[n] += jnp.concatenate(
            [
                add(dh * x1), add(dh), add(dy * x2), add(dy), add(d1f), add(dr2),
                add(dup.astype(F32)), jnp.zeros((1, D), F32),
            ],
            axis=0,
        )
        for k in range(TB // MID):
            @pl.when(c == k)
            def _():
                for x in (2, 3, 1):
                    dc_copy(x, k, rel(x), n).start()

        dcr[pl.ds(pl.multiple_of(n * TB + c * MID, MID), MID), :] = dcst[rr, mycols]
        return 0

    lax.fori_loop(0, TB // MID, middle, 0)
    for x in (1, 2, 3):
        for c in range(TB // MID):
            pending.append(dc_copy(x, c, rel(x), n))
    l_otok = pltpu.make_async_copy(otok, otok_h, loc_sem.at[6])
    l_otok.start()
    for x in (1, 2, 3):
        start(ncopy(vecs.at[n], vecs.at[n], vn_s.at[x], vn_r.at[x], rel(x)))

    for k, (left, right) in enumerate(((du, hr), (ctxf, dr1r), (act, dr2r))):
        grad = mm_tn(left[...], right[...]).astype(BF16)
        for t in range(NAR):
            gst[k, t % 2, t // 2] = grad[t * CW:(t + 1) * CW]
        ncopy(gst.at[k, 1 - b0], gr1.at[k], g1_s.at[k], g1_r.at[k], n1).start()

    def loop(fn, first, count):
        def go(i, c):
            fn(i)
            return c

        lax.fori_loop(first, count, go, 0)

    def group_loop(fn, first=1, count=OWN):
        loop(fn, first, count)

    def member(i):
        return lax.rem(o + i, OWN)

    pb = lax.rem(o, 2)
    qa = o // 2
    pair = g * OWN + 2 * qa + (1 - pb)

    def line(i):
        return lax.rem(qa + i, LINE)

    def line_dev(u):
        return g * OWN + 2 * u + pb

    keep = pl.ds(pl.multiple_of(pb * HR, HR), HR)
    away = pl.ds(pl.multiple_of((1 - pb) * HR, HR), HR)

    keepc = pl.ds(pl.multiple_of(pb * HC, HC), HC)
    awayc = pl.ds(pl.multiple_of((1 - pb) * HC, HC), HC)

    def piece(v):
        return pl.ds(pl.multiple_of(v * PR, PR), PR)

    def unit_rows(u):
        return pl.ds(u * CW, CW)

    def unit_mom(u, part, cols):
        if u == 0:
            return mom.at[2, b1, b0, :, part, cols]
        return mom.at[pl.ds(0, 2), b1, b0, u - 1, part, cols]

    def l1_copy(u):
        return wcopy(dr1r.at[unit_rows(u), awayc], lr1.at[u], l1_s.at[u], l1_r.at[u], pair)

    def l1(u, lhs):
        dr1r[unit_rows(u), :] = mm(lhs, tok[...]).astype(BF16)
        start(l1_copy(u))

    def z_copy(u, i):
        v = line(i)
        return wcopy(zs.at[u, :, piece(v), :], zr.at[u, qa], zs_s.at[u, i], zs_r.at[u, qa], line_dev(v))

    def owned(u, total):
        if groups > 1:
            grl[g, u] = total.astype(BF16)
            loop(lambda i: across(u, i).start(), 1, groups)

            def meet(i):
                v = lax.rem(g + i, groups)
                ref = grl.at[v, u]
                wcopy(ref, ref, gp_s.at[u, i], gp_r.at[u, v], v * OWN + o).wait_recv()

            loop(meet, 1, groups)
            total = lax.fori_loop(
                0, groups, lambda v, t: t + grl[v, u].astype(F32), jnp.zeros_like(total)
            )
        for k in range(2):
            m, first = (2, k * HR) if u == 0 else (k, (u - 1) * HR)
            old = mT[m, pl.ds(pl.multiple_of(first + qa * PR, PR), PR), keepc]
            new = (total[k] + 0.5 * old).astype(BF16)
            if u == 0:
                mom[2, b1, b0, k, piece(qa), keepc] = new
            else:
                mom[k, b1, b0, u - 1, piece(qa), keepc] = new

    def half_cols(b):
        return pl.ds(pl.multiple_of(b * HC, HC), HC)

    def d1_copy(i):
        v = member(i)
        src = zd.at[:, piece(v // 2), half_cols(lax.rem(v, 2))]
        return wcopy(src, zdr.at[o], zd_s.at[i], zd_r.at[o], g * OWN + v)

    def d1(lhs):
        zd[...] = mm(lhs, tok[...]).astype(BF16).reshape(2, HR, D)
        group_loop(lambda i: d1_copy(i).start())

    def d2_copy(v, i):
        ref = unit_mom(2, piece(v // 2), half_cols(lax.rem(v, 2)))
        return wcopy(ref, ref, ad_s.at[i], ad_r.at[v], g * OWN + member(i))

    def d2():
        zdr[o] = zd[:, piece(qa), keepc]

        def take(i):
            v = member(i)
            wcopy(zdr.at[v], zdr.at[v], zd_s.at[0], zd_r.at[v], g * OWN + v).wait_recv()

        group_loop(take)
        total = zdr[0].astype(F32)
        for v in range(1, OWN):
            total = total + zdr[v].astype(F32)
        owned(2, total)
        group_loop(lambda i: d2_copy(o, i).start())

    def l2(u):
        l1_copy(u).wait_recv()
        both = dr1r[unit_rows(u), keepc].astype(F32) + lr1[u].astype(F32)
        zs[u] = both.astype(BF16).reshape(2, HR, HC)
        loop(lambda i: z_copy(u, i).start(), 1, LINE)

    def across(u, i):
        ref = grl.at[g, u]
        return wcopy(ref, ref, gp_s.at[u, i], gp_r.at[u, g], lax.rem(g + i, groups) * OWN + o)

    def share(u, v, i):
        ref = unit_mom(u, piece(v), keepc)
        return wcopy(ref, ref, aq_s.at[u, i], aq_r.at[u, v], line_dev(line(i)))

    def l3(u):
        zr[u, qa] = zs[u, :, piece(qa), :]

        def take(i):
            v = line(i)
            wcopy(zr.at[u, v], zr.at[u, v], zs_s.at[u, 0], zs_r.at[u, v], line_dev(v)).wait_recv()

        loop(take, 1, LINE)
        total = zr[u, 0].astype(F32)
        for v in range(1, LINE):
            total = total + zr[u, v].astype(F32)
        owned(u, total)
        loop(lambda i: share(u, qa, i).start(), 1, LINE)

    def half_copy(u, cols):
        ref = unit_mom(u, pl.ds(0, HR), cols)
        return wcopy(ref, ref, ap_s.at[u], ap_r.at[u], pair)

    def l4(u):
        loop(lambda i: share(u, line(i), i).wait_recv(), 1, LINE)
        half_copy(u, keepc).start()

    fans = {0: [(0, 2, 1)], 1: [(1, 0, 0), (2, 1, 1)], 2: [(3, 0, 0), (4, 1, 1)]}

    def fan_ref(u, m, t):
        low = lax.rem(t, 2)
        return mom.at[2, t // 2, low] if u == 0 else mom.at[m, t // 2, low, u - 1]

    def near_copy(u, f, m, c):
        return ncopy(fan_ref(u, m, n), fan_ref(u, m, n), la_s.at[f, 0], la_r.at[f, n], c + 2 * b1)

    def far_copy(u, f, m, c):
        return ncopy(fan_ref(u, m, n), fan_ref(u, m, n), la_s.at[f, 1], la_r.at[f, n], c + 2 * (1 - b1))

    def l5(u):
        if u < 2:
            half_copy(u, awayc).wait_recv()
        else:
            group_loop(lambda i: d2_copy(member(i), i).wait_recv())
        for f, m, c in fans[u]:
            far_copy(u, f, m, c).start()

            @pl.when(b0 != c)
            def _():
                near_copy(u, f, m, c).start()

    def fan_wait(u, f, m):
        for x in (1, 2, 3):
            t = rel(x)
            ncopy(fan_ref(u, m, t), fan_ref(u, m, t), la_s.at[0, 0], la_r.at[f, t], t).wait_recv()

    def vec_copy(buf, ss, rs, i, v):
        return wcopy(buf.at[v], buf.at[v], ss.at[i], rs.at[v], g * OWN + member(i))

    def vec_across(buf, ss, rs, i, v):
        ref = buf.at[OWN + v]
        return wcopy(ref, ref, ss.at[OWN + i], rs.at[OWN + v], lax.rem(g + i, groups) * OWN + o)

    def vec_send(*where):
        group_loop(lambda i: vec_copy(*where, i, o).start())

    def vec_sum(buf, ss, rs):
        group_loop(lambda i: vec_copy(buf, ss, rs, i, member(i)).wait_recv())
        zero = jnp.zeros(buf.shape[1:], F32)
        total = lax.fori_loop(0, OWN, lambda v, t: t + buf[v], zero)
        if groups > 1:
            buf[OWN + g] = total
            group_loop(lambda i: vec_across(buf, ss, rs, i, g).start(), 1, groups)
            group_loop(
                lambda i: vec_across(buf, ss, rs, i, lax.rem(g + i, groups)).wait_recv(), 1, groups
            )
            total = lax.fori_loop(0, groups, lambda v, t: t + buf[OWN + v], zero)
        return total

    def vec_done(buf, ss, rs):
        group_loop(lambda i: vec_copy(buf, ss, rs, i, o).wait_send())
        if groups > 1:
            group_loop(lambda i: vec_across(buf, ss, rs, i, g).wait_send(), 1, groups)

    def over_copy(m):
        return ncopy(eys.at[m], eyr.at[m], g3_s.at[m], g3_r.at[m], n2)

    def chip_sum(m, y, part):
        return gst[m, b0, y, part, :].astype(F32) + gr1[m, y, part, :].astype(F32)

    def early_over(m):
        ncopy(gst.at[m, b0], gr1.at[m], g1_s.at[m], g1_r.at[m], n1).wait_recv()
        eys[m] = chip_sum(m, 1 - b1, slice(None)).astype(BF16)
        start(over_copy(m))

    def pair_copy(m):
        return wcopy(es1.at[m], er1.at[m], g2_s.at[m], g2_r.at[m], pair)

    def early_pair(m):
        over_copy(m).wait_recv()
        es1[m] = (chip_sum(m, b1, away) + eyr[m, away, :].astype(F32)).astype(BF16)
        start(pair_copy(m))

    def e_line(m, i):
        u = line(i)
        return wcopy(zse.at[m, piece(u), :], zre.at[m, qa], ez_s.at[m, i], ez_r.at[m, qa], line_dev(u))

    def early_line(m):
        pair_copy(m).wait_recv()
        total = chip_sum(m, b1, keep) + eyr[m, keep, :].astype(F32) + er1[m].astype(F32)
        zse[m] = total.astype(BF16)
        loop(lambda i: e_line(m, i).start(), 1, LINE)

    def e_across(m, i):
        ref = grp.at[g, m]
        return wcopy(ref, ref, gp_s.at[3 + m, i], gp_r.at[3 + m, g], lax.rem(g + i, groups) * OWN + o)

    def e_swap(m, y):
        ref = mom.at[3 + m, y, b0, pb, piece(qa), :]
        return ncopy(ref, ref, ey_s.at[m], ey_r.at[m], n2)

    def early_sum(m):
        zre[m, qa] = zse[m, piece(qa), :]

        def take(i):
            v = line(i)
            ref = zre.at[m, v]
            wcopy(ref, ref, ez_s.at[m, 0], ez_r.at[m, v], line_dev(v)).wait_recv()

        loop(take, 1, LINE)
        total = zre[m, 0].astype(F32)
        for v in range(1, LINE):
            total = total + zre[m, v].astype(F32)
        if groups > 1:
            grp[g, m] = total.astype(BF16)
            loop(lambda i: e_across(m, i).start(), 1, groups)

            def meet(i):
                v = lax.rem(g + i, groups)
                ref = grp.at[v, m]
                wcopy(ref, ref, gp_s.at[3 + m, i], gp_r.at[3 + m, v], v * OWN + o).wait_recv()

            loop(meet, 1, groups)
            total = lax.fori_loop(
                0, groups, lambda v, t: t + grp[v, m].astype(F32), jnp.zeros_like(total)
            )
        old = mT[3 + m, pl.ds(pl.multiple_of(pb * HR + qa * PR, PR), PR), :]
        mom[3 + m, b1, b0, pb, piece(qa), :] = (total + 0.5 * old).astype(BF16)
        start(e_swap(m, b1))

    def e_share(m, u, i):
        ref = mom.at[3 + m, :, b0, pb, piece(u), :]
        return wcopy(ref, ref, aq_s.at[3 + m, i], aq_r.at[3 + m, u], line_dev(line(i)))

    def early_back(m):
        e_swap(m, 1 - b1).wait_recv()
        loop(lambda i: e_share(m, qa, i).start(), 1, LINE)

    def e_half(m, b):
        ref = mom.at[3 + m, :, b0, b]
        return wcopy(ref, ref, ap_s.at[3 + m], ap_r.at[3 + m], pair)

    def early_half(m):
        loop(lambda i: e_share(m, line(i), i).wait_recv(), 1, LINE)
        start(e_half(m, pb))

    def e_near(m, c):
        ref = mom.at[3 + m, :, c]
        return ncopy(ref, ref, ow_s.at[m], ow_r.at[m], n1)

    def early_near(m):
        e_half(m, 1 - pb).wait_recv()

        @pl.when(b0 != m % 2)
        def _():
            e_near(m, b0).start()

    def vec_early():
        for x in (1, 2, 3):
            arrived(vecs.at[rel(x)], vn_s.at[x], vn_r.at[x], rel(x))
        vecw[o] = ((vecs[0] + vecs[1]) + vecs[2]) + vecs[3]
        vec_send(vecw, vw_s, vw_r)

    plan = {
        ("a", 0): [(early_over, 0)],
        ("a", 1): [(early_over, 1)],
        ("a", 2): [(early_over, 2)],
        (0, 1, 0): [(early_pair, 0)],
        (0, 1, 1): [(l2, 0)],
        (0, 2, 0): [(early_pair, 1)],
        (0, 3, 0): [(early_pair, 2), (early_line, 0)],
        (0, 3, 1): [(l3, 0)],
        (1, 0, 0): [(early_line, 1)],
        (1, 1, 0): [(early_line, 2), (early_sum, 0)],
        (1, 1, 1): [(l4, 0), (l2, 1)],
        (1, 2, 0): [(early_sum, 1)],
        (1, 2, 1): [(early_back, 0)],
        (1, 3, 0): [(early_sum, 2), (l5, 0)],
        (1, 3, 1): [(l3, 1)],
    }

    def after(i, key):
        for k in range(NAR):
            point = (key[0], k) + key[1:]
            if point in plan:
                @pl.when(i == k)
                def _():
                    held = len(pending)
                    for fn, arg in plan[point]:
                        fn(arg)
                    del pending[held:]

    dkT[...] = jnp.zeros_like(dkT)
    dvT[...] = jnp.zeros_like(dvT)
    lane = lax.broadcasted_iota(jnp.int32, (TB, CW), 1)
    low_lane = lane < HD

    def backward_v(i, _):
        t = rel(i)
        rr = rows(t, TB)

        @pl.when(i > 0)
        def _():
            for c in range(TB // MID):
                dst = dcr.at[pl.ds(pl.multiple_of(t * TB + c * MID, MID), MID)]
                ncopy(
                    dcst.at[pl.ds(c * MID, MID), mycols], dst, dc_sem.at[i, c], dc_rem.at[i, c], t
                ).wait_recv()

        dcs = (dcr[rr, :].astype(F32) * rln[rr, :]).astype(BF16)
        full = dcs.astype(F32)
        prod = full * ctxn[rr, :]
        delta = (
            jnp.sum(jnp.where(low_lane, prod, 0.0), axis=1, keepdims=True),
            jnp.sum(jnp.where(low_lane, 0.0, prod), axis=1, keepdims=True),
        )
        dcT = full.T.astype(BF16)
        for h in range(2):
            hs = slice(h * HD, (h + 1) * HD)
            top = delta[h].astype(BF16).astype(F32)
            tail = delta[h] - top
            base = (1 - h) * HD
            extra = jnp.where(lane == base, -top, jnp.where(lane == base + 1, -tail, 0.0))
            qp[h, rr, 0:CW] = jnp.where(low_lane == (h == 0), full, extra).astype(BF16)
            dvT[hs, :] += mm(dcT[hs, :], e_ref[h, rr, :])
        after(i, ("a",))
        return 0

    lax.fori_loop(0, NAR, backward_v, 0)
    gT[2 * CW:, :] = dvT[...].astype(BF16)
    l1(0, gT[2 * CW:, :])
    for k in range(3):
        ncopy(gst.at[k, 1 - b0], gr1.at[k], g1_s.at[k], g1_r.at[k], n1).wait_send()

    def backward(h):
        hs = slice(h * HD, (h + 1) * HD)
        ks = slice(CW + h * HD, CW + (h + 1) * HD)

        def block(i, _):
            rr = rows(rel(i), TB)
            s_ref[...] = mm(qp[h, rr, 0:CW], vTp[h])
            ds = e_ref[h, rr, :] * s_ref[...].astype(BF16)
            gT[hs, rr] = (mm_nt(kTp[h, hs, :], ds) * 0.125).astype(BF16)
            after(i, (h, 0))
            dkT[hs, :] += mm(qT[hs, rr], ds)
            after(i, (h, 1))
            return 0

        lax.fori_loop(0, NAR, block, 0)
        gT[ks, :] = dkT[hs, :].astype(BF16)
        lhs = jnp.concatenate([gT[hs, :], gT[ks, :]], axis=0)
        if h == 0:
            l1(1, lhs)
        else:
            d1(lhs)

    backward(0)
    backward(1)

    def dx(t):
        return mm(wqkv[...], gT[:, rows(t, TB)])

    both_rows = pl.ds(pl.multiple_of(b1 * 2 * CW, 2 * CW), 2 * CW)
    XB = s_ref.at[:, 0:D]

    def newton_begin(m):
        xin = mom[m].reshape(D, D).astype(F32)
        XB[...] = xin * (1.0 / (jnp.sqrt(jnp.sum(xin * xin)) + 1e-07))

    def newton_step():
        x = XB[...]
        xl = x.astype(BF16)
        a = mm_nt(xl, xl)
        al = a.astype(BF16)
        p = (COEF_B * a + COEF_C * mm(al, al)).astype(BF16)
        XB[...] = COEF_A * x + mm(p, xl)

    def orth(m):
        return gst.at[m // 2, lax.rem(m, 2), 0]

    def swap(m, k):
        return ncopy(gst.at[k, 0, 1], orth(m), sw_s.at[k], sw_r.at[k], n1)

    def newton_last(m, k):
        xl = XB[...].astype(BF16)
        xo = XB[both_rows, :]
        a = mm_nt(xo.astype(BF16), xl).astype(BF16)
        y = mm(a, xl)
        z = mm_nt(y.astype(BF16), xl).astype(BF16)
        res = COEF_A * xo + COEF_B * y + COEF_C * mm(z, xl)
        first, second = res[0:CW], res[CW:]
        gst[m // 2, lax.rem(m, 2), 0] = jnp.where(b0 == 0, first, second).astype(BF16)
        gst[k, 0, 1] = jnp.where(b0 == 0, second, first).astype(BF16)
        start(swap(m, k))

    def dx2_copy(c):
        cols = slice(c * MID, (c + 1) * MID)
        return ncopy(dxs2.at[:, cols], dxr2.at[:, cols], dx2_s.at[c], dx2_r.at[c], n2)

    dxs[1][...] = dx(n3).astype(BF16)
    start(ncopy(dxs[1], dxr1.at[1], dx1_s.at[1], dx1_r.at[1], n1))
    dxs[0][...] = dx(n1).astype(BF16)
    start(ncopy(dxs[0], dxr1.at[0], dx1_s.at[0], dx1_r.at[0], n1))
    early_back(1)
    over = dx(n2)
    one = jnp.ones((8, LEN), BF16)
    upper_rows = lax.broadcasted_iota(jnp.int32, (8, CW), 0) < 4
    lv[o] = jnp.where(upper_rows, mm_nt(one, gT[0:CW, :]), mm_nt(one, gT[2 * CW:, :]))
    ncopy(dxs[1], dxr1.at[1], dx1_s.at[1], dx1_r.at[1], n1).wait_recv()
    dxs2[...] = (over + dxr1[1].astype(F32)).astype(BF16)
    start(dx2_copy(0))
    early_half(0)
    l4(1)
    dxo = dx(n).T
    for k in range(NAR):
        cols = slice(k * CW, (k + 1) * CW)
        ograd[:, cols] = dxo[:, cols] + win_f[k]
    d2()
    settled = pending[:]
    pending.clear()
    early_back(2)
    early_near(0)

    @pl.when(b0 == 0)
    def _():
        e_near(0, 1).wait_recv()

    @pl.when(b0 == 1)
    def _():
        fan_wait(0, 0, 2)

    newton_begin(3 - b0)
    newton_step()
    early_half(1)
    l5(1)
    newton_step()
    vec_early()
    vec_send(lv, lv_s, lv_r)
    newton_last(3 - b0, 1)
    l5(2)
    early_near(1)
    early_half(2)

    def fans_wait():
        fan_wait(1, 1 + b0, b0)
        fan_wait(2, 3 + b0, b0)

    for c in settled:
        c.wait_send()
    for k in range(3):
        loop(lambda i: e_line(k, i).wait_send(), 1, LINE)
        if k < 2:
            loop(lambda i: z_copy(k, i).wait_send(), 1, LINE)
            loop(lambda i: share(k, qa, i).wait_send(), 1, LINE)
    group_loop(lambda i: d1_copy(i).wait_send())

    @pl.when(b0 == 0)
    def _():
        fans_wait()

    @pl.when(b0 == 1)
    def _():
        e_near(1, 0).wait_recv()

    start(dx2_copy(1))
    newton_begin(4 * b0)
    newton_step()
    newton_step()
    newton_last(4 * b0, 2)
    early_near(2)
    l_mom = pltpu.make_async_copy(mom.at[:, b1, b0], omom_h, loc_sem.at[8])
    l_mom.start()
    ovec[...] = vec_sum(vecw, vw_s, vw_r)
    late = vec_sum(lv, lv_s, lv_r)
    ovec2[0:1, :] = late[0:1]
    ovec2[1:2, :] = late[4:5]
    ovec2[2:3, :] = ovec[6:7, mycols]
    ovec2[3:8, :] = jnp.zeros((5, CW), F32)

    @pl.when(b0 == 0)
    def _():
        e_near(2, 1).wait_recv()

    @pl.when(b0 == 1)
    def _():
        fans_wait()

    newton_begin(5 - 4 * b0)
    newton_step()
    newton_step()
    newton_last(5 - 4 * b0, 0)

    ncopy(dxs[0], dxr1.at[0], dx1_s.at[0], dx1_r.at[0], n1).wait_recv()
    for c in (0, 1):
        dx2_copy(c).wait_recv()
    ograd_b[...] = (ograd[...] + (dxr1[0].astype(F32) + dxr2[...].astype(F32)).T).astype(BF16)
    l_ograd = pltpu.make_async_copy(ograd_b, ograd_h, loc_sem.at[7])
    l_ograd.start()
    swap(2 + b0, 1).wait_recv()
    swap(4 * (1 - b0), 2).wait_recv()
    swap(1 + 4 * b0, 0).wait_recv()
    l_orth = pltpu.make_async_copy(gst.at[:, :, 0], oorth_h, loc_sem.at[9])
    l_orth.start()

    for m in range(3):
        pending.extend((pair_copy(m), over_copy(m), e_swap(m, b1)))
        if m < 2:
            pending.append(half_copy(m, keepc))
        for f, k, c in fans[m]:
            pending.append(far_copy(m, f, k, c))

            @pl.when(b0 != c)
            def _():
                near_copy(m, f, k, c).wait_send()

        @pl.when(b0 != m % 2)
        def _():
            e_near(m, b0).wait_send()

    for c in pending:
        c.wait_send()
    vec_done(vecw, vw_s, vw_r)
    vec_done(lv, lv_s, lv_r)
    group_loop(lambda i: d2_copy(o, i).wait_send())
    for k in range(3):
        loop(lambda i: e_share(k, qa, i).wait_send(), 1, LINE)
        if groups > 1:
            loop(lambda i: across(k, i).wait_send(), 1, groups)
            loop(lambda i: e_across(k, i).wait_send(), 1, groups)
    l_otok.wait()
    l_ograd.wait()
    l_mom.wait()
    l_orth.wait()


def run_layer(wide, tokens, cotangent, seg, pad, gen, in_w, out_w, in_m, out_m, shared, split):
    any_ = pl.BlockSpec(memory_space=pl.ANY)
    vm = pl.BlockSpec(memory_space=pltpu.VMEM)
    V = pltpu.VMEM
    dma = lambda *s: pltpu.SemaphoreType.DMA(s)
    one = pltpu.SemaphoreType.DMA
    groups = wide // OWN
    vslots = OWN + (groups if groups > 1 else 0)
    scratch = [
        V((LEN, D), BF16), V((TB, D), BF16), V((NAR, 16, CW), F32),
        V((4, D, CW), F32), V((2, CW, D), F32), V((6, CW, D), F32),
        V((3 * CW, D), BF16), V((D, 3 * CW), BF16),
        V((D, D), BF16), V((2, D, D), BF16), V((2, CW, CW), F32),
        V((2, LEN, 2 * CW), BF16), V((2, 2 * CW, LEN), BF16), V((2, CW, LEN), BF16), V((CW, LEN), BF16),
        V((LEN, CW), F32), V((TB, LEN), F32), V((2, LEN, LEN), BF16), V((2, TB, CW), F32),
        V((LEN, CW), F32), V((LEN, CW), BF16), V((TB, D), BF16),
        V((TB, D), BF16), V((TB, D), BF16), V((TB, D), BF16), V((TB, D), BF16), V((TB, D), BF16),
        V((TB, D), BF16), V((LEN, CW), BF16),
        V((NAR, 8, D), F32), V((vslots, 8, D), F32), V((CW, LEN), F32), V((CW, LEN), F32), V((3 * CW, LEN), BF16),
        V((3, 2, 2, CW, D), BF16), V((3, 2, CW, D), BF16), V((3, CW, D), BF16), V((3, CW, D), BF16),
        V((3, HR, D), BF16), V((3, HR, D), BF16), V((3, HR, D), BF16), V((3, LINE, PR, D), BF16), V((3, CW, HC), BF16),
        V((2, 2, HR, HC), BF16), V((2, LINE, 2, PR, HC), BF16), V((2, HR, D), BF16), V((OWN, 2, PR, HC), BF16),
        V((vslots, 8, CW), F32),
        V((6, 2, 2, 2, HR, D), BF16),
        V((groups, 3, PR, D) if groups > 1 else (1, 1, PR, D), BF16),
        V((groups, 3, 2, PR, HC) if groups > 1 else (1, 1, 1, PR, HC), BF16),
        V((2, D, TB), BF16), V((D, TB), BF16),
        dma(10), dma(4), dma(4), dma(2), dma(2), dma(4), dma(4), dma(3, 2), dma(3, 2), dma(1, 2), dma(1, 2),
        dma(4), dma(4), dma(4, TB // MID), dma(4, TB // MID), dma(4), dma(4), dma(vslots), dma(vslots),
        dma(vslots), dma(vslots),
        dma(3), dma(3), dma(3), dma(3), dma(3), dma(3), dma(3), dma(3), dma(3, LINE), dma(3, LINE),
        dma(OWN), dma(OWN), dma(OWN), dma(OWN),
        dma(6, groups), dma(6, groups),
        dma(6, LINE), dma(6, LINE), dma(6), dma(6),
        dma(3), dma(3), dma(3, LINE), dma(3, LINE), dma(3), dma(3), dma(5, 2), dma(5, 4), dma(3), dma(3),
        dma(2), dma(2), dma(2), dma(2),
    ]
    return pl.pallas_call(
        functools.partial(layer_kernel, wide),
        out_shape=[
            jax.ShapeDtypeStruct((TB, D), BF16),
            jax.ShapeDtypeStruct((TB, D), BF16),
            jax.ShapeDtypeStruct((6, 2, HR, D), BF16),
            jax.ShapeDtypeStruct((3, 2, CW, D), BF16),
            jax.ShapeDtypeStruct((8, D), F32),
            jax.ShapeDtypeStruct((8, CW), F32),
        ],
        in_specs=[any_, any_, vm, vm, vm, any_, any_, any_, any_, vm, vm],
        out_specs=[any_, any_, any_, any_, vm, vm],
        scratch_shapes=scratch,
        compiler_params=pltpu.CompilerParams(
            collective_id=0, has_side_effects=True, vmem_limit_bytes=62 * MB
        ),
        name="layer",
    )(tokens, cotangent, seg, pad, gen, in_w, out_w, in_m, out_m, shared, split)


def muon_step(weights, orthogonal):
    return weights - 0.2 * (0.2 * math.sqrt(D) * orthogonal + 0.01 * weights)


def adam_step(values, moment_one, moment_two, gradient):
    moment_one = 0.9 * moment_one + 0.1 * gradient
    moment_two = 0.999 * moment_two + 0.001 * gradient * gradient
    step_ratio = (
        moment_one / (1.0 - 0.9**STEP) / (jnp.sqrt(moment_two / (1.0 - 0.999**STEP)) + 1e-08)
    )
    return (moment_one, moment_two, values - 0.3 * (step_ratio + 0.01 * values))


def blend(average, weights):
    return 0.6 * average + 0.4 * weights


def update_kernel(
    otok, ograd, mom, orth, in_w, out_w, in_a, out_a, vec, vec2,
    sv, s1, s2, sa, pv, p1, p2, pa,
    tok_o, grad_o, inm_o, outm_o, inw_o, outw_o, inl_o, outl_o, ina_o, outa_o,
    s1_o, s2_o, sv_o, sa_o, p1_o, p2_o, pv_o, pa_o,
    mom_b, orth_b, inw_b, outw_b, ina_b, outa_b,
    inm_v, outm_v, inw_v, outw_v, inl_v, outl_v, ina_v, outa_v, grad_v, grad_b, tok_v, thru, rsem, wsem,
):
    whole = [
        pltpu.make_async_copy(ograd, grad_b, thru.at[0]),
        pltpu.make_async_copy(otok, tok_v, thru.at[1]),
    ]
    back = [
        pltpu.make_async_copy(grad_v, grad_o, thru.at[2]),
        pltpu.make_async_copy(tok_v, tok_o, thru.at[3]),
    ]
    reads, writes = [], []
    for k in range(6):
        j, inner = (k, True) if k < 4 else (k - 4, False)
        srcs = (mom.at[k], orth.at[k // 2, k % 2], (in_w if inner else out_w).at[j], (in_a if inner else out_a).at[j])
        dsts = (
            mom_b.at[k], orth_b.at[k], (inw_b if inner else outw_b).at[j], (ina_b if inner else outa_b).at[j],
        )
        reads.append([pltpu.make_async_copy(s, d, rsem.at[k, i]) for i, (s, d) in enumerate(zip(srcs, dsts))])
        bufs = (inm_v, inw_v, inl_v, ina_v) if inner else (outm_v, outw_v, outl_v, outa_v)
        outs = (inm_o, inw_o, inl_o, ina_o) if inner else (outm_o, outw_o, outl_o, outa_o)
        writes.append(
            [pltpu.make_async_copy(s.at[j], d.at[j], wsem.at[k, i]) for i, (s, d) in enumerate(zip(bufs, outs))]
        )
    for c in reads[0]:
        c.start()
    for c in reads[1]:
        c.start()
    for c in whole:
        c.start()
    for k in range(2, 6):
        for c in reads[k]:
            c.start()
    s1_o[...], s2_o[...], shared_new = adam_step(sv[...], s1[...], s2[...], vec[0:6, :])
    sv_o[...] = shared_new
    sa_o[...] = blend(sa[...], shared_new)
    p1_o[...], p2_o[...], split_new = adam_step(pv[...], p1[...], p2[...], vec2[0:3, :])
    pv_o[...] = split_new
    pa_o[...] = blend(pa[...], split_new)
    for k in range(6):
        if k in (1, 2):
            whole[k - 1].wait()
            if k == 1:
                grad_v[...] = grad_b[...].astype(F32)
            back[k - 1].start()
        for c in reads[k]:
            c.wait()
        if k < 4:
            inm_v[k] = mom_b[k].reshape(CW, D).astype(F32).T
            new = muon_step(inw_b[k], orth_b[k].astype(F32).T)
            inw_v[k] = new
            inl_v[k] = new.astype(BF16)
            ina_v[k] = blend(ina_b[k], new)
        else:
            j = k - 4
            outm_v[j] = mom_b[k].reshape(CW, D).astype(F32)
            new = muon_step(outw_b[j], orth_b[k].astype(F32))
            outw_v[j] = new
            outl_v[j] = new.astype(BF16)
            outa_v[j] = blend(outa_b[j], new)
        for c in writes[k]:
            c.start()
    for c in back:
        c.wait()
    for k in range(6):
        for c in writes[k]:
            c.wait()


def run_update(*args):
    vm = pl.BlockSpec(memory_space=pltpu.VMEM)
    any_ = pl.BlockSpec(memory_space=pl.ANY)
    S = jax.ShapeDtypeStruct
    V = pltpu.VMEM
    inner, outer = (4, D, CW), (2, CW, D)
    return pl.pallas_call(
        update_kernel,
        out_shape=[
            S((TB, D), BF16), S((TB, D), F32), S(inner, F32), S(outer, F32), S(inner, F32), S(outer, F32),
            S(inner, BF16), S(outer, BF16), S(inner, F32), S(outer, F32),
        ]
        + [S((6, D), F32)] * 4
        + [S((3, CW), F32)] * 4,
        in_specs=[any_] * 8 + [vm] * 10,
        out_specs=[any_] * 10 + [vm] * 8,
        scratch_shapes=[
            V((6, 2, HR, D), BF16), V((6, CW, D), BF16), V(inner, F32), V(outer, F32), V(inner, F32), V(outer, F32),
            V(inner, F32), V(outer, F32), V(inner, F32), V(outer, F32), V(inner, BF16), V(outer, BF16),
            V(inner, F32), V(outer, F32), V((TB, D), F32), V((TB, D), BF16), V((TB, D), BF16),
            pltpu.SemaphoreType.DMA((4,)), pltpu.SemaphoreType.DMA((6, 4)), pltpu.SemaphoreType.DMA((6, 4)),
        ],
        compiler_params=pltpu.CompilerParams(vmem_limit_bytes=60 * MB),
        name="update",
    )(*args)


def body(
    wide, tokens, cotangent, segments, padding, generative, in_weights, out_weights, in_momenta,
    out_momenta, in_average, out_average, shared_values, shared_moment1, shared_moment2,
    shared_average, split_values, split_moment1, split_moment2, split_average,
):
    flags = [v.reshape(TB // CW, CW) for v in (segments, padding, generative)]
    otok, ograd, mom, orth, vec, vec2 = run_layer(
        wide, tokens, cotangent, *flags, in_weights, out_weights, in_momenta, out_momenta,
        shared_values, split_values,
    )
    return tuple(
        run_update(
            otok, ograd, mom, orth, in_weights, out_weights, in_average, out_average, vec, vec2,
            shared_values, shared_moment1, shared_moment2, shared_average,
            split_values, split_moment1, split_moment2, split_average,
        )
    )


def solution(mesh):
    rows = P(("wide", "narrow"), None)
    flat = P(("wide", "narrow"))
    cols = P(None, None, "narrow")
    outs = P(None, "narrow", None)
    vec = P(None, "narrow")
    return jax.shard_map(
        functools.partial(body, mesh.shape["wide"]),
        mesh=mesh,
        in_specs=(
            rows, rows, flat, flat, flat, cols, outs, cols, outs, cols, outs,
            P(), P(), P(), P(), vec, vec, vec, vec,
        ),
        out_specs=(
            rows, rows, cols, outs, cols, outs, cols, outs, cols, outs,
            P(), P(), P(), P(), vec, vec, vec, vec,
        ),
        check_vma=False,
    )
```

```python
import functools
import math

import jax
import jax.numpy as jnp
from jax import lax
from jax.experimental import pallas as pl
from jax.experimental.pallas import tpu as pltpu
from jax.sharding import PartitionSpec as P

D = 512
HD = 64
LEN = 2048
NS_ITERS = 3
STEP = 10
NAR = 4
TB = LEN // NAR
CW = D // NAR
OWN = 8
LINE = OWN // 2
HR = CW // 2
HC = D // 2
PR = CW // OWN
MID = 256

F32 = jnp.float32
BF16 = jnp.bfloat16
MESH = pl.DeviceIdType.MESH

COEF_A = 3.4445
COEF_B = -4.775
COEF_C = 2.0315
NEG = -1e30
MB = 2**20


def mm(a, b):
    return jnp.dot(a, b, preferred_element_type=F32)


def mm_nt(a, b):
    return lax.dot_general(a, b, (((1,), (1,)), ((), ())), preferred_element_type=F32)


def mm_tn(a, b):
    return lax.dot_general(a, b, (((0,), (0,)), ((), ())), preferred_element_type=F32)


def layer_kernel(wide, *refs):
    (
        tok_h, cot_h, seg_i, pad_i, gen_i, win_h, wout_h, min_h, mout_h, shared, split,
        otok_h, ograd_h, omom_h, oorth_h, ovec, ovec2,
        tok, cot, pay, win_f, wout_f, mT, wqkvT, wqkv, wup, wod, bcol,
        qp, kTp, vTp, qT, rdn, s_ref, e_ref, tops_n, ctxn, ctx_s, ctxf,
        hr, act, du, dr2r, dr1r, dcst, dcr, vecs, vecw, dkT, dvT, gT,
        gst, gr1, eys, eyr, es1, er1, zse, zre, lr1, zs, zr, zd, zdr, lv, mom, grp, grl,
        dxr1, dxr2,
        loc_sem, ag_s, ag_r, rly_s, rly_r, pay_s, pay_r, wg_s, wg_r, wr_s, wr_r,
        ctx_sem, ctx_rem, dc_sem, dc_rem, vn_s, vn_r, vw_s, vw_r, lv_s, lv_r,
        g1_s, g1_r, g2_s, g2_r, g3_s, g3_r, l1_s, l1_r, zs_s, zs_r, zd_s, zd_r, ad_s, ad_r, gp_s, gp_r,
        aq_s, aq_r, ap_s, ap_r, ow_s, ow_r, ez_s, ez_r, ey_s, ey_r, la_s, la_r, sw_s, sw_r, dx1_s, dx1_r, dx2_s, dx2_r,
    ) = refs
    n = lax.axis_index("narrow")
    w = lax.axis_index("wide")
    groups = wide // OWN
    g = w // OWN if groups > 1 else 0
    o = lax.rem(w, OWN) if groups > 1 else w
    b0 = lax.rem(n, 2)
    b1 = n // 2

    def rel(x):
        return lax.rem(b0 + x % 2, 2) + 2 * lax.rem(b1 + x // 2, 2)

    n1, n2, n3 = rel(1), rel(2), rel(3)

    def rows(t, size):
        return pl.ds(pl.multiple_of(t * size, size), size)

    def ncopy(src, dst, ssem, rsem, t):
        return pltpu.make_async_remote_copy(
            src_ref=src, dst_ref=dst, send_sem=ssem, recv_sem=rsem,
            device_id={"narrow": t}, device_id_type=MESH,
        )

    def wcopy(src, dst, ssem, rsem, u):
        return pltpu.make_async_remote_copy(
            src_ref=src, dst_ref=dst, send_sem=ssem, recv_sem=rsem,
            device_id={"wide": u}, device_id_type=MESH,
        )

    pending = []

    def start(copy):
        copy.start()
        pending.append(copy)
        return copy

    own = rows(n, TB)
    ograd = s_ref.at[:, 3 * D:4 * D]
    ograd_b = hr
    rln = rdn
    otok = cot
    dxs, dxs2 = (act, du), dr2r

    l_tok = pltpu.make_async_copy(tok_h, tok.at[own], loc_sem.at[0])
    l_win = pltpu.make_async_copy(win_h, win_f, loc_sem.at[1])
    l_wout = pltpu.make_async_copy(wout_h, wout_f, loc_sem.at[2])
    l_cot = pltpu.make_async_copy(cot_h, cot, loc_sem.at[3])
    l_min = pltpu.make_async_copy(min_h, win_f, loc_sem.at[4])
    l_mout = pltpu.make_async_copy(mout_h, mT.at[pl.ds(4, 2)], loc_sem.at[5])
    for c in (l_tok, l_win, l_wout, l_cot, l_mout):
        c.start()

    barrier = pltpu.get_barrier_semaphore()
    for x in (1, 2, 3):
        pl.semaphore_signal(barrier, inc=1, device_id={"narrow": rel(x)}, device_id_type=MESH)

    def greet(i, c):
        pl.semaphore_signal(
            barrier, inc=1, device_id={"wide": g * OWN + lax.rem(o + i, OWN)}, device_id_type=MESH
        )
        return c

    lax.fori_loop(1, OWN, greet, 0)

    def greet_group(i, c):
        pl.semaphore_signal(
            barrier, inc=1, device_id={"wide": lax.rem(g + i, groups) * OWN + o}, device_id_type=MESH
        )
        return c

    if groups > 1:
        lax.fori_loop(1, groups, greet_group, 0)
    seg = seg_i[...]
    closed = jnp.logical_or(pad_i[...] != 0, gen_i[...] != 0)
    pay[n] = jnp.concatenate(
        [
            seg.astype(F32), jnp.where(closed, -1, seg).astype(F32),
            split[2:3, :], jnp.zeros((7, CW), F32),
        ],
        axis=0,
    )
    l_tok.wait()
    pl.semaphore_wait(barrier, 3 + (OWN - 1) + (groups - 1))

    half = TB // 2

    def ag_rows(t, c):
        return tok.at[pl.ds(pl.multiple_of(t * TB + c * half, half), half)]

    for x in (1, 2, 3):
        start(ncopy(pay.at[n], pay.at[n], pay_s.at[x], pay_r.at[x], rel(x)))
    for c in (0, 1):
        start(ncopy(ag_rows(n, c), ag_rows(n, c), ag_s.at[2 + c], ag_r.at[2 + c], n2))
    for c in (0, 1):
        start(ncopy(ag_rows(n, c), ag_rows(n, c), ag_s.at[c], ag_r.at[c], n1))

    def arrived(slot, sem_s, sem_r, t):
        ncopy(slot, slot, sem_s, sem_r, t).wait_recv()

    l_win.wait()
    for k in range(3):
        piece = win_f[k]
        wqkvT[k * CW:(k + 1) * CW, :] = piece.T.astype(BF16)
        wqkv[:, k * CW:(k + 1) * CW] = piece.astype(BF16)
    mycols = pl.ds(pl.multiple_of(n * CW, CW), CW)
    wup[:, mycols] = win_f[3].astype(BF16)
    l_min.start()
    l_wout.wait()
    for k in range(2):
        wod[k, mycols, :] = wout_f[k].astype(BF16)

    def wg_list(sems, semr, x, t, target):
        cols = pl.ds(pl.multiple_of(t * CW, CW), CW)
        return [
            ncopy(wod.at[:, cols, :], wod.at[:, cols, :], sems.at[x, 0], semr.at[x, 0], target),
            ncopy(wup.at[:, cols], wup.at[:, cols], sems.at[x, 1], semr.at[x, 1], target),
        ]

    bcol[0] = jnp.broadcast_to(split[0:1, :], (CW, CW)).T
    bcol[1] = jnp.broadcast_to(split[1:2, :], (CW, CW)).T

    def project(t, c):
        rr = pl.ds(pl.multiple_of(t * TB + c * half, half), half)
        tb = tok[rr, :]
        qk = mm(tb, wqkv[:, 0:2 * CW])
        q = (qk[:, :CW] + split[0:1, :]).astype(BF16)
        k = qk[:, CW:].astype(BF16)
        q8 = q.astype(F32) * 0.125
        prod = q8 * k.astype(F32)
        low = lax.broadcasted_iota(jnp.int32, (half, CW), 1) < HD
        d0 = jnp.sum(jnp.where(low, prod, 0.0), axis=1, keepdims=True)
        d1 = jnp.sum(jnp.where(low, 0.0, prod), axis=1, keepdims=True)
        rdn[rr, :] = jnp.where(low, d0, d1)
        lane1 = lax.broadcasted_iota(jnp.int32, (CW, CW), 1).astype(F32)
        lowj = lane1 < HD
        for j in range(half // CW):
            seg = jnp.broadcast_to(pay[t, pl.ds(c * (half // CW) + j, 1), :], (CW, CW)).T
            part = q8[j * CW:(j + 1) * CW, :]
            hot = lambda base: jnp.where(seg == lane1 + base, 1.0, 0.0)
            rj = pl.ds(pl.multiple_of(t * TB + c * half + j * CW, CW), CW)
            qp[0, rj, 0:CW] = jnp.where(lowj, part, hot(-float(HD))).astype(BF16)
            qp[1, rj, 0:CW] = jnp.where(lowj, hot(0.0), part).astype(BF16)
            rest = hot(float(HD)).astype(BF16)
            qp[0, rj, CW:] = rest
            qp[1, rj, CW:] = rest
        tT = mm_nt(wqkvT[...], tb)
        bq = jnp.concatenate([bcol[0]] * (half // CW), axis=1)
        bv = jnp.concatenate([bcol[1]] * (half // CW), axis=1)
        qT[:, rr] = ((tT[0:CW] + bq).astype(BF16).astype(F32) * 0.125).astype(BF16)
        kT = tT[CW:2 * CW].astype(BF16)
        vT = (tT[2 * CW:] + bv).astype(BF16)
        code = jnp.concatenate(
            [pay[t, pl.ds(4 + c * (half // CW) + j, 1), :] for j in range(half // CW)], axis=1
        )
        rowi = lax.broadcasted_iota(jnp.int32, (HD, half), 0).astype(F32)
        keep = lambda base: jnp.where(code == rowi + base, 0.0, NEG).astype(BF16)
        first, second, third = keep(0.0), keep(float(HD)), keep(float(2 * HD))
        ones = jnp.ones((HD, half), BF16)
        kTp[0, 0:HD, rr] = kT[0:HD]
        kTp[0, HD:CW, rr] = first
        kTp[1, 0:HD, rr] = first
        kTp[1, HD:CW, rr] = kT[HD:]
        vTp[0, 0:HD, rr] = vT[0:HD]
        vTp[0, HD:, rr] = ones
        vTp[1, 0:HD, rr] = ones
        vTp[1, HD:, rr] = vT[HD:]
        for h in range(2):
            kTp[h, CW:CW + HD, rr] = second
            kTp[h, CW + HD:, rr] = third

    def relayed(c):
        return ncopy(ag_rows(n2, c), ag_rows(n2, c), rly_s.at[c], rly_r.at[c], n1)

    def project_step(i, _):
        @pl.when(i == 2)
        def _():
            arrived(pay.at[n1], pay_s.at[1], pay_r.at[1], n1)
            arrived(ag_rows(n1, 0), ag_s.at[0], ag_r.at[0], n1)
            l_min.wait()
            for k in range(4):
                mT[k] = win_f[k].T

        @pl.when(i == 3)
        def _():
            arrived(ag_rows(n1, 1), ag_s.at[1], ag_r.at[1], n1)

        @pl.when(i == 4)
        def _():
            arrived(pay.at[n2], pay_s.at[2], pay_r.at[2], n2)
            arrived(pay.at[n3], pay_s.at[3], pay_r.at[3], n3)
            arrived(ag_rows(n2, 0), ag_s.at[2], ag_r.at[2], n2)
            relayed(0).start()

        @pl.when(i == 5)
        def _():
            arrived(ag_rows(n3, 0), rly_s.at[0], rly_r.at[0], n1)

        @pl.when(i == 6)
        def _():
            arrived(ag_rows(n2, 1), ag_s.at[3], ag_r.at[3], n2)
            relayed(1).start()
            for x in (2, 1):
                for c in wg_list(wg_s, wg_r, x, n, rel(x)):
                    c.start()

        @pl.when(i == 7)
        def _():
            arrived(ag_rows(n3, 1), rly_s.at[1], rly_r.at[1], n1)

        far = i // 4
        x = (1 - far) * (i // 2) + far * (2 + lax.rem(i, 2))
        c = (1 - far) * lax.rem(i, 2) + far * (i // 2 - 2)
        project(rel(x), c)
        return 0

    lax.fori_loop(0, NAR, project_step, 0)

    eye = lax.broadcasted_iota(jnp.int32, (CW, CW), 0) == lax.broadcasted_iota(jnp.int32, (CW, CW), 1)
    sh = s_ref.at[:, 0:2 * TB]
    near_keys = rows(b1, 2 * TB)
    far_keys = rows(1 - b1, 2 * TB)
    lane_low = lax.broadcasted_iota(jnp.int32, (TB, CW), 1) < HD

    def v_rows(h):
        return slice(0, HD + 16) if h == 0 else slice(HD - 16, CW)

    def both_heads(parts):
        num = jnp.concatenate([parts[0][:HD], parts[1][16:]], axis=0)
        den = jnp.concatenate(
            [
                jnp.broadcast_to(parts[0][HD:HD + 1], (HD, TB)),
                jnp.broadcast_to(parts[1][0:1], (HD, TB)),
            ],
            axis=0,
        )
        return num.T, den.T

    def attend_near(x, _):
        t = rel(x)
        rr = rows(t, TB)
        low = lax.rem(t, 2)
        parts, tops = [], []
        for h in range(2):
            sh[...] = mm(qp[h, rr, :], kTp[h, :, near_keys])
            for j in range(TB // CW):
                diag = rdn[pl.ds(pl.multiple_of(t * TB + j * CW, CW), CW), h * HD:h * HD + 1]
                cc = pl.ds(pl.multiple_of(low * TB + j * CW, CW), CW)
                sub = pl.ds(j * CW, CW)
                s_ref[sub, cc] = jnp.where(eye, diag, s_ref[sub, cc])
            sv = sh[...]
            top = jnp.max(sv, axis=1, keepdims=True)
            e = jnp.exp(sv - top).astype(BF16)
            e_ref[h, rr, near_keys] = e
            parts.append(mm_nt(vTp[h, v_rows(h), near_keys], e))
            tops.append(top)
        num, den = both_heads(parts)
        ctxn[rr, :] = num
        rln[rr, :] = den
        tops_n[low] = jnp.where(lane_low, tops[0], tops[1])
        return 0

    lax.fori_loop(0, 2, attend_near, 0)
    lax.fori_loop(NAR, 2 * NAR, project_step, 0)
    for x in (2, 1):
        pending.extend(wg_list(wg_s, wg_r, x, n, rel(x)))
    pending.extend((relayed(0), relayed(1)))

    def ctx_copy(x, t):
        return ncopy(
            ctx_s.at[rows(t, TB)], ctxf.at[:, mycols], ctx_sem.at[x], ctx_rem.at[x], t
        )

    def attend_far(i, _):
        t = rel(2 + i)
        rr = rows(t, TB)
        parts = []
        for h in range(2):
            s_ref[...] = mm(qp[h, rr, :], kTp[h])
            for j in range(TB // CW):
                cc = pl.ds(pl.multiple_of(t * TB + j * CW, CW), CW)
                diag = rdn[cc, h * HD:h * HD + 1]
                sub = pl.ds(j * CW, CW)
                s_ref[sub, cc] = jnp.where(eye, diag, s_ref[sub, cc])
            sv = s_ref[...]
            top = jnp.max(sv, axis=1, keepdims=True)
            e = jnp.exp(sv - top).astype(BF16)
            e_ref[h, rr, :] = e
            parts.append(mm_nt(vTp[h, v_rows(h), :], e))
        num, den = both_heads(parts)
        inv = 1.0 / den
        cn = num * inv
        ctxn[rr, :] = cn
        rln[rr, :] = inv
        ctx_s[rr, :] = cn.astype(BF16)
        ctx_copy(2 + i, t).start()
        return 0

    def attend_rest(i, _):
        t = rel(1 - i)

        @pl.when(i == 1)
        def _():
            for c in wg_list(wg_s, wg_r, 2, n2, n2):
                c.wait_recv()
            for c in wg_list(wr_s, wr_r, 0, n2, n1):
                c.start()

        rr = rows(t, TB)
        low = lax.rem(t, 2)
        parts, shrink = [], []
        for h in range(2):
            sh[...] = mm(qp[h, rr, :], kTp[h, :, far_keys])
            sv = sh[...]
            old = tops_n[low, :, h * HD:h * HD + 1]
            top = jnp.maximum(jnp.max(sv, axis=1, keepdims=True), old)
            less = jnp.exp(old - top).astype(BF16)
            e = jnp.exp(sv - top).astype(BF16)
            e_ref[h, rr, far_keys] = e
            e_ref[h, rr, near_keys] = e_ref[h, rr, near_keys] * less
            parts.append(mm_nt(vTp[h, v_rows(h), far_keys], e))
            shrink.append(less.astype(F32))
        num, den = both_heads(parts)
        less = jnp.where(lane_low, shrink[0], shrink[1])
        inv = 1.0 / (rln[rr, :] * less + den)
        cn = (ctxn[rr, :] * less + num) * inv
        ctxn[rr, :] = cn
        rln[rr, :] = inv
        ctx_s[rr, :] = cn.astype(BF16)

        @pl.when(i == 0)
        def _():
            ctx_copy(1, t).start()

        return 0

    lax.fori_loop(0, 2, attend_far, 0)
    lax.fori_loop(0, 2, attend_rest, 0)
    pending.extend(wg_list(wr_s, wr_r, 0, n2, n1))
    for x in (1, 2, 3):
        pending.append(ctx_copy(x, rel(x)))
    ctxf[:, mycols] = ctx_s[own, :]
    for c in wg_list(wg_s, wg_r, 1, n1, n1):
        c.wait_recv()
    for c in wg_list(wr_s, wr_r, 0, n3, n1):
        c.wait_recv()
    l_cot.wait()
    l_mout.wait()
    for x in (2, 3, 1):
        cols = pl.ds(pl.multiple_of(rel(x) * CW, CW), CW)
        ncopy(ctx_s.at[own], ctxf.at[:, cols], ctx_sem.at[x], ctx_rem.at[x], rel(x)).wait_recv()

    up_bias = jnp.concatenate([pay[t, 8:9, :] for t in range(NAR)], axis=1)
    vecs[n] = jnp.zeros((8, D), F32)

    def dc_copy(x, c, t, me):
        rr = pl.ds(c * MID, MID)
        cols = pl.ds(pl.multiple_of(t * CW, CW), CW)
        dst = dcr.at[pl.ds(pl.multiple_of(me * TB + c * MID, MID), MID)]
        return ncopy(dcst.at[rr, cols], dst, dc_sem.at[x, c], dc_rem.at[x, c], t)

    def middle(c, _):
        rr = pl.ds(pl.multiple_of(c * MID, MID), MID)
        ga1, be1, ga2, be2, ba, bd = (shared[k:k + 1, :] for k in range(6))
        x0 = tok[pl.ds(pl.multiple_of(n * TB + c * MID, MID), MID), :].astype(F32)
        r1 = x0 + (mm(ctxf[rr, :], wod[0]) + ba)
        c1 = r1 - jnp.mean(r1, axis=1, keepdims=True)
        s1 = lax.rsqrt(jnp.mean(c1 * c1, axis=1, keepdims=True) + 1e-05)
        x1 = c1 * s1
        hidden = x1 * ga1 + be1
        low = hidden.astype(BF16)
        hr[rr, :] = low
        upper = mm(low, wup[...]) + up_bias
        cdf = 0.5 * (1.0 + lax.erf(upper * (1.0 / math.sqrt(2.0))))
        pdf = jnp.exp(-0.5 * upper * upper) * (1.0 / math.sqrt(2.0 * math.pi))
        slope = cdf + upper * pdf
        a = (upper * cdf).astype(BF16)
        act[rr, :] = a
        r2 = hidden + (mm(a, wod[1]) + bd)
        c2 = r2 - jnp.mean(r2, axis=1, keepdims=True)
        s2 = lax.rsqrt(jnp.mean(c2 * c2, axis=1, keepdims=True) + 1e-05)
        x2 = c2 * s2
        dy = cot[rr, :].astype(F32)
        otok[rr, :] = (x2 * ga2 + be2).astype(BF16)
        dn = dy * ga2
        dr2 = s2 * (
            dn - jnp.mean(dn, axis=1, keepdims=True) - x2 * jnp.mean(dn * x2, axis=1, keepdims=True)
        )
        d2 = dr2.astype(BF16)
        dr2r[rr, :] = d2
        dup = (mm_nt(d2, wod[1]) * slope).astype(BF16)
        du[rr, :] = dup
        dh = dr2 + mm_nt(dup, wup[...])
        en = dh * ga1
        d1f = s1 * (
            en - jnp.mean(en, axis=1, keepdims=True) - x1 * jnp.mean(en * x1, axis=1, keepdims=True)
        )
        for k in range(NAR):
            win_f[k, rr, :] = d1f[:, k * CW:(k + 1) * CW]
        d1 = d1f.astype(BF16)
        dr1r[rr, :] = d1
        dcst[rr, :] = mm_nt(d1, wod[0]).astype(BF16)
        add = lambda v: jnp.sum(v, axis=0, keepdims=True)
        vecs[n] += jnp.concatenate(
            [
                add(dh * x1), add(dh), add(dy * x2), add(dy), add(d1f), add(dr2),
                add(dup.astype(F32)), jnp.zeros((1, D), F32),
            ],
            axis=0,
        )
        for k in range(TB // MID):
            @pl.when(c == k)
            def _():
                for x in (2, 3, 1):
                    dc_copy(x, k, rel(x), n).start()

        dcr[pl.ds(pl.multiple_of(n * TB + c * MID, MID), MID), :] = dcst[rr, mycols]
        return 0

    lax.fori_loop(0, TB // MID, middle, 0)
    for x in (1, 2, 3):
        for c in range(TB // MID):
            pending.append(dc_copy(x, c, rel(x), n))
    l_otok = pltpu.make_async_copy(otok, otok_h, loc_sem.at[6])
    l_otok.start()
    for x in (1, 2, 3):
        start(ncopy(vecs.at[n], vecs.at[n], vn_s.at[x], vn_r.at[x], rel(x)))

    for k, (left, right) in enumerate(((du, hr), (ctxf, dr1r), (act, dr2r))):
        grad = mm_tn(left[...], right[...]).astype(BF16)
        for t in range(NAR):
            gst[k, t % 2, t // 2] = grad[t * CW:(t + 1) * CW]
        ncopy(gst.at[k, 1 - b0], gr1.at[k], g1_s.at[k], g1_r.at[k], n1).start()

    def loop(fn, first, count):
        def go(i, c):
            fn(i)
            return c

        lax.fori_loop(first, count, go, 0)

    def group_loop(fn, first=1, count=OWN):
        loop(fn, first, count)

    def member(i):
        return lax.rem(o + i, OWN)

    pb = lax.rem(o, 2)
    qa = o // 2
    pair = g * OWN + 2 * qa + (1 - pb)

    def line(i):
        return lax.rem(qa + i, LINE)

    def line_dev(u):
        return g * OWN + 2 * u + pb

    keep = pl.ds(pl.multiple_of(pb * HR, HR), HR)
    away = pl.ds(pl.multiple_of((1 - pb) * HR, HR), HR)

    keepc = pl.ds(pl.multiple_of(pb * HC, HC), HC)
    awayc = pl.ds(pl.multiple_of((1 - pb) * HC, HC), HC)

    def piece(v):
        return pl.ds(pl.multiple_of(v * PR, PR), PR)

    def unit_rows(u):
        return pl.ds(u * CW, CW)

    def unit_mom(u, part, cols):
        if u == 0:
            return mom.at[2, b1, b0, :, part, cols]
        return mom.at[pl.ds(0, 2), b1, b0, u - 1, part, cols]

    def l1_copy(u):
        return wcopy(dr1r.at[unit_rows(u), awayc], lr1.at[u], l1_s.at[u], l1_r.at[u], pair)

    def l1(u, lhs):
        dr1r[unit_rows(u), :] = mm(lhs, tok[...]).astype(BF16)
        start(l1_copy(u))

    def z_copy(u, i):
        v = line(i)
        return wcopy(zs.at[u, :, piece(v), :], zr.at[u, qa], zs_s.at[u, i], zs_r.at[u, qa], line_dev(v))

    def owned(u, total):
        if groups > 1:
            grl[g, u] = total.astype(BF16)
            loop(lambda i: across(u, i).start(), 1, groups)

            def meet(i):
                v = lax.rem(g + i, groups)
                ref = grl.at[v, u]
                wcopy(ref, ref, gp_s.at[u, i], gp_r.at[u, v], v * OWN + o).wait_recv()

            loop(meet, 1, groups)
            total = lax.fori_loop(
                0, groups, lambda v, t: t + grl[v, u].astype(F32), jnp.zeros_like(total)
            )
        for k in range(2):
            m, first = (2, k * HR) if u == 0 else (k, (u - 1) * HR)
            old = mT[m, pl.ds(pl.multiple_of(first + qa * PR, PR), PR), keepc]
            new = (total[k] + 0.5 * old).astype(BF16)
            if u == 0:
                mom[2, b1, b0, k, piece(qa), keepc] = new
            else:
                mom[k, b1, b0, u - 1, piece(qa), keepc] = new

    def half_cols(b):
        return pl.ds(pl.multiple_of(b * HC, HC), HC)

    def d1_copy(i):
        v = member(i)
        src = zd.at[:, piece(v // 2), half_cols(lax.rem(v, 2))]
        return wcopy(src, zdr.at[o], zd_s.at[i], zd_r.at[o], g * OWN + v)

    def d1(lhs):
        zd[...] = mm(lhs, tok[...]).astype(BF16).reshape(2, HR, D)
        group_loop(lambda i: d1_copy(i).start())

    def d2_copy(v, i):
        ref = unit_mom(2, piece(v // 2), half_cols(lax.rem(v, 2)))
        return wcopy(ref, ref, ad_s.at[i], ad_r.at[v], g * OWN + member(i))

    def d2():
        zdr[o] = zd[:, piece(qa), keepc]

        def take(i):
            v = member(i)
            wcopy(zdr.at[v], zdr.at[v], zd_s.at[0], zd_r.at[v], g * OWN + v).wait_recv()

        group_loop(take)
        total = zdr[0].astype(F32)
        for v in range(1, OWN):
            total = total + zdr[v].astype(F32)
        owned(2, total)
        group_loop(lambda i: d2_copy(o, i).start())

    def l2(u):
        l1_copy(u).wait_recv()
        both = dr1r[unit_rows(u), keepc].astype(F32) + lr1[u].astype(F32)
        zs[u] = both.astype(BF16).reshape(2, HR, HC)
        loop(lambda i: z_copy(u, i).start(), 1, LINE)

    def across(u, i):
        ref = grl.at[g, u]
        return wcopy(ref, ref, gp_s.at[u, i], gp_r.at[u, g], lax.rem(g + i, groups) * OWN + o)

    def share(u, v, i):
        ref = unit_mom(u, piece(v), keepc)
        return wcopy(ref, ref, aq_s.at[u, i], aq_r.at[u, v], line_dev(line(i)))

    def l3(u):
        zr[u, qa] = zs[u, :, piece(qa), :]

        def take(i):
            v = line(i)
            wcopy(zr.at[u, v], zr.at[u, v], zs_s.at[u, 0], zs_r.at[u, v], line_dev(v)).wait_recv()

        loop(take, 1, LINE)
        total = zr[u, 0].astype(F32)
        for v in range(1, LINE):
            total = total + zr[u, v].astype(F32)
        owned(u, total)
        loop(lambda i: share(u, qa, i).start(), 1, LINE)

    def half_copy(u, cols):
        ref = unit_mom(u, pl.ds(0, HR), cols)
        return wcopy(ref, ref, ap_s.at[u], ap_r.at[u], pair)

    def l4(u):
        loop(lambda i: share(u, line(i), i).wait_recv(), 1, LINE)
        half_copy(u, keepc).start()

    fans = {0: [(0, 2, 1)], 1: [(1, 0, 0), (2, 1, 1)], 2: [(3, 0, 0), (4, 1, 1)]}

    def fan_ref(u, m, t):
        low = lax.rem(t, 2)
        return mom.at[2, t // 2, low] if u == 0 else mom.at[m, t // 2, low, u - 1]

    def near_copy(u, f, m, c):
        return ncopy(fan_ref(u, m, n), fan_ref(u, m, n), la_s.at[f, 0], la_r.at[f, n], c + 2 * b1)

    def far_copy(u, f, m, c):
        return ncopy(fan_ref(u, m, n), fan_ref(u, m, n), la_s.at[f, 1], la_r.at[f, n], c + 2 * (1 - b1))

    def l5(u):
        if u < 2:
            half_copy(u, awayc).wait_recv()
        else:
            group_loop(lambda i: d2_copy(member(i), i).wait_recv())
        for f, m, c in fans[u]:
            far_copy(u, f, m, c).start()

            @pl.when(b0 != c)
            def _():
                near_copy(u, f, m, c).start()

    def fan_wait(u, f, m):
        for x in (1, 2, 3):
            t = rel(x)
            ncopy(fan_ref(u, m, t), fan_ref(u, m, t), la_s.at[0, 0], la_r.at[f, t], t).wait_recv()

    def vec_copy(buf, ss, rs, i, v):
        return wcopy(buf.at[v], buf.at[v], ss.at[i], rs.at[v], g * OWN + member(i))

    def vec_across(buf, ss, rs, i, v):
        ref = buf.at[OWN + v]
        return wcopy(ref, ref, ss.at[OWN + i], rs.at[OWN + v], lax.rem(g + i, groups) * OWN + o)

    def vec_send(*where):
        group_loop(lambda i: vec_copy(*where, i, o).start())

    def vec_sum(buf, ss, rs):
        group_loop(lambda i: vec_copy(buf, ss, rs, i, member(i)).wait_recv())
        zero = jnp.zeros(buf.shape[1:], F32)
        total = lax.fori_loop(0, OWN, lambda v, t: t + buf[v], zero)
        if groups > 1:
            buf[OWN + g] = total
            group_loop(lambda i: vec_across(buf, ss, rs, i, g).start(), 1, groups)
            group_loop(
                lambda i: vec_across(buf, ss, rs, i, lax.rem(g + i, groups)).wait_recv(), 1, groups
            )
            total = lax.fori_loop(0, groups, lambda v, t: t + buf[OWN + v], zero)
        return total

    def vec_done(buf, ss, rs):
        group_loop(lambda i: vec_copy(buf, ss, rs, i, o).wait_send())
        if groups > 1:
            group_loop(lambda i: vec_across(buf, ss, rs, i, g).wait_send(), 1, groups)

    def over_copy(m):
        return ncopy(eys.at[m], eyr.at[m], g3_s.at[m], g3_r.at[m], n2)

    def chip_sum(m, y, part):
        return gst[m, b0, y, part, :].astype(F32) + gr1[m, y, part, :].astype(F32)

    def early_over(m):
        ncopy(gst.at[m, b0], gr1.at[m], g1_s.at[m], g1_r.at[m], n1).wait_recv()
        eys[m] = chip_sum(m, 1 - b1, slice(None)).astype(BF16)
        start(over_copy(m))

    def pair_copy(m):
        return wcopy(es1.at[m], er1.at[m], g2_s.at[m], g2_r.at[m], pair)

    def early_pair(m):
        over_copy(m).wait_recv()
        es1[m] = (chip_sum(m, b1, away) + eyr[m, away, :].astype(F32)).astype(BF16)
        start(pair_copy(m))

    def e_line(m, i):
        u = line(i)
        return wcopy(zse.at[m, piece(u), :], zre.at[m, qa], ez_s.at[m, i], ez_r.at[m, qa], line_dev(u))

    def early_line(m):
        pair_copy(m).wait_recv()
        total = chip_sum(m, b1, keep) + eyr[m, keep, :].astype(F32) + er1[m].astype(F32)
        zse[m] = total.astype(BF16)
        loop(lambda i: e_line(m, i).start(), 1, LINE)

    def e_across(m, i):
        ref = grp.at[g, m]
        return wcopy(ref, ref, gp_s.at[3 + m, i], gp_r.at[3 + m, g], lax.rem(g + i, groups) * OWN + o)

    def e_swap(m, y):
        ref = mom.at[3 + m, y, b0, pb, piece(qa), :]
        return ncopy(ref, ref, ey_s.at[m], ey_r.at[m], n2)

    def early_sum(m):
        zre[m, qa] = zse[m, piece(qa), :]

        def take(i):
            v = line(i)
            ref = zre.at[m, v]
            wcopy(ref, ref, ez_s.at[m, 0], ez_r.at[m, v], line_dev(v)).wait_recv()

        loop(take, 1, LINE)
        total = zre[m, 0].astype(F32)
        for v in range(1, LINE):
            total = total + zre[m, v].astype(F32)
        if groups > 1:
            grp[g, m] = total.astype(BF16)
            loop(lambda i: e_across(m, i).start(), 1, groups)

            def meet(i):
                v = lax.rem(g + i, groups)
                ref = grp.at[v, m]
                wcopy(ref, ref, gp_s.at[3 + m, i], gp_r.at[3 + m, v], v * OWN + o).wait_recv()

            loop(meet, 1, groups)
            total = lax.fori_loop(
                0, groups, lambda v, t: t + grp[v, m].astype(F32), jnp.zeros_like(total)
            )
        old = mT[3 + m, pl.ds(pl.multiple_of(pb * HR + qa * PR, PR), PR), :]
        mom[3 + m, b1, b0, pb, piece(qa), :] = (total + 0.5 * old).astype(BF16)
        start(e_swap(m, b1))

    def e_share(m, u, i):
        ref = mom.at[3 + m, :, b0, pb, piece(u), :]
        return wcopy(ref, ref, aq_s.at[3 + m, i], aq_r.at[3 + m, u], line_dev(line(i)))

    def early_back(m):
        e_swap(m, 1 - b1).wait_recv()
        loop(lambda i: e_share(m, qa, i).start(), 1, LINE)

    def e_half(m, b):
        ref = mom.at[3 + m, :, b0, b]
        return wcopy(ref, ref, ap_s.at[3 + m], ap_r.at[3 + m], pair)

    def early_half(m):
        loop(lambda i: e_share(m, line(i), i).wait_recv(), 1, LINE)
        start(e_half(m, pb))

    def e_near(m, c):
        ref = mom.at[3 + m, :, c]
        return ncopy(ref, ref, ow_s.at[m], ow_r.at[m], n1)

    def early_near(m):
        e_half(m, 1 - pb).wait_recv()

        @pl.when(b0 != m % 2)
        def _():
            e_near(m, b0).start()

    def vec_early():
        for x in (1, 2, 3):
            arrived(vecs.at[rel(x)], vn_s.at[x], vn_r.at[x], rel(x))
        vecw[o] = ((vecs[0] + vecs[1]) + vecs[2]) + vecs[3]
        vec_send(vecw, vw_s, vw_r)

    plan = {
        ("a", 0): [(early_over, 0)],
        ("a", 1): [(early_over, 1)],
        ("a", 2): [(early_over, 2)],
        (0, 1, 0): [(early_pair, 0)],
        (0, 1, 1): [(l2, 0)],
        (0, 2, 0): [(early_pair, 1)],
        (0, 3, 0): [(early_pair, 2), (early_line, 0)],
        (0, 3, 1): [(l3, 0)],
        (1, 0, 0): [(early_line, 1)],
        (1, 1, 0): [(early_line, 2), (early_sum, 0)],
        (1, 1, 1): [(l4, 0), (l2, 1)],
        (1, 2, 0): [(early_sum, 1)],
        (1, 2, 1): [(early_back, 0)],
        (1, 3, 0): [(early_sum, 2), (l5, 0)],
        (1, 3, 1): [(l3, 1)],
    }

    def after(i, key):
        for k in range(NAR):
            point = (key[0], k) + key[1:]
            if point in plan:
                @pl.when(i == k)
                def _():
                    held = len(pending)
                    for fn, arg in plan[point]:
                        fn(arg)
                    del pending[held:]

    dkT[...] = jnp.zeros_like(dkT)
    dvT[...] = jnp.zeros_like(dvT)
    lane = lax.broadcasted_iota(jnp.int32, (TB, CW), 1)
    low_lane = lane < HD

    def backward_v(i, _):
        t = rel(i)
        rr = rows(t, TB)

        @pl.when(i > 0)
        def _():
            for c in range(TB // MID):
                dst = dcr.at[pl.ds(pl.multiple_of(t * TB + c * MID, MID), MID)]
                ncopy(
                    dcst.at[pl.ds(c * MID, MID), mycols], dst, dc_sem.at[i, c], dc_rem.at[i, c], t
                ).wait_recv()

        dcs = (dcr[rr, :].astype(F32) * rln[rr, :]).astype(BF16)
        full = dcs.astype(F32)
        prod = full * ctxn[rr, :]
        delta = (
            jnp.sum(jnp.where(low_lane, prod, 0.0), axis=1, keepdims=True),
            jnp.sum(jnp.where(low_lane, 0.0, prod), axis=1, keepdims=True),
        )
        dcT = full.T.astype(BF16)
        for h in range(2):
            hs = slice(h * HD, (h + 1) * HD)
            top = delta[h].astype(BF16).astype(F32)
            tail = delta[h] - top
            base = (1 - h) * HD
            extra = jnp.where(lane == base, -top, jnp.where(lane == base + 1, -tail, 0.0))
            qp[h, rr, 0:CW] = jnp.where(low_lane == (h == 0), full, extra).astype(BF16)
            dvT[hs, :] += mm(dcT[hs, :], e_ref[h, rr, :])
        after(i, ("a",))
        return 0

    lax.fori_loop(0, NAR, backward_v, 0)
    gT[2 * CW:, :] = dvT[...].astype(BF16)
    l1(0, gT[2 * CW:, :])
    for k in range(3):
        ncopy(gst.at[k, 1 - b0], gr1.at[k], g1_s.at[k], g1_r.at[k], n1).wait_send()

    def backward(h):
        hs = slice(h * HD, (h + 1) * HD)
        ks = slice(CW + h * HD, CW + (h + 1) * HD)

        def block(i, _):
            rr = rows(rel(i), TB)
            s_ref[...] = mm(qp[h, rr, 0:CW], vTp[h])
            ds = e_ref[h, rr, :] * s_ref[...].astype(BF16)
            gT[hs, rr] = (mm_nt(kTp[h, hs, :], ds) * 0.125).astype(BF16)
            after(i, (h, 0))
            dkT[hs, :] += mm(qT[hs, rr], ds)
            after(i, (h, 1))
            return 0

        lax.fori_loop(0, NAR, block, 0)
        gT[ks, :] = dkT[hs, :].astype(BF16)
        lhs = jnp.concatenate([gT[hs, :], gT[ks, :]], axis=0)
        if h == 0:
            l1(1, lhs)
        else:
            d1(lhs)

    backward(0)
    backward(1)

    def dx(t):
        return mm(wqkv[...], gT[:, rows(t, TB)])

    both_rows = pl.ds(pl.multiple_of(b1 * 2 * CW, 2 * CW), 2 * CW)
    XB = s_ref.at[:, 0:D]

    def newton_first(m):
        xl = mom[m].reshape(D, D)
        x = xl.astype(F32)
        inv = 1.0 / (jnp.sqrt(jnp.sum(x * x)) + 1e-07)
        a = mm_nt(xl, xl) * (inv * inv)
        al = a.astype(BF16)
        p = (COEF_B * a + COEF_C * mm(al, al)).astype(BF16)
        XB[...] = (COEF_A * x + mm(p, xl)) * inv

    def newton_step():
        x = XB[...]
        xl = x.astype(BF16)
        a = mm_nt(xl, xl)
        al = a.astype(BF16)
        p = (COEF_B * a + COEF_C * mm(al, al)).astype(BF16)
        XB[...] = COEF_A * x + mm(p, xl)

    def orth(m):
        return gst.at[m // 2, lax.rem(m, 2), 0]

    def swap(m, k):
        return ncopy(gst.at[k, 0, 1], orth(m), sw_s.at[k], sw_r.at[k], n1)

    def newton_last(m, k):
        xl = XB[...].astype(BF16)
        xo = XB[both_rows, :]
        a = mm_nt(xo.astype(BF16), xl).astype(BF16)
        y = mm(a, xl)
        z = mm_nt(y.astype(BF16), xl).astype(BF16)
        res = COEF_A * xo + COEF_B * y + COEF_C * mm(z, xl)
        first, second = res[0:CW], res[CW:]
        gst[m // 2, lax.rem(m, 2), 0] = jnp.where(b0 == 0, first, second).astype(BF16)
        gst[k, 0, 1] = jnp.where(b0 == 0, second, first).astype(BF16)
        start(swap(m, k))

    def dx2_copy(c):
        cols = slice(c * MID, (c + 1) * MID)
        return ncopy(dxs2.at[:, cols], dxr2.at[:, cols], dx2_s.at[c], dx2_r.at[c], n2)

    dxs[1][...] = dx(n3).astype(BF16)
    start(ncopy(dxs[1], dxr1.at[1], dx1_s.at[1], dx1_r.at[1], n1))
    dxs[0][...] = dx(n1).astype(BF16)
    start(ncopy(dxs[0], dxr1.at[0], dx1_s.at[0], dx1_r.at[0], n1))
    early_back(1)
    over = dx(n2)
    one = jnp.ones((8, LEN), BF16)
    upper_rows = lax.broadcasted_iota(jnp.int32, (8, CW), 0) < 4
    lv[o] = jnp.where(upper_rows, mm_nt(one, gT[0:CW, :]), mm_nt(one, gT[2 * CW:, :]))
    ncopy(dxs[1], dxr1.at[1], dx1_s.at[1], dx1_r.at[1], n1).wait_recv()
    dxs2[...] = (over + dxr1[1].astype(F32)).astype(BF16)
    start(dx2_copy(0))
    early_half(0)
    l4(1)
    dxo = dx(n).T
    for k in range(NAR):
        cols = slice(k * CW, (k + 1) * CW)
        ograd[:, cols] = dxo[:, cols] + win_f[k]
    d2()
    settled = pending[:]
    pending.clear()
    early_back(2)
    early_near(0)

    @pl.when(b0 == 0)
    def _():
        e_near(0, 1).wait_recv()

    @pl.when(b0 == 1)
    def _():
        fan_wait(0, 0, 2)

    newton_first(3 - b0)
    early_half(1)
    l5(1)
    newton_step()
    vec_early()
    vec_send(lv, lv_s, lv_r)
    newton_last(3 - b0, 1)
    l5(2)
    early_near(1)
    early_half(2)

    def fans_wait():
        fan_wait(1, 1 + b0, b0)
        fan_wait(2, 3 + b0, b0)

    for c in settled:
        c.wait_send()
    for k in range(3):
        loop(lambda i: e_line(k, i).wait_send(), 1, LINE)
        if k < 2:
            loop(lambda i: z_copy(k, i).wait_send(), 1, LINE)
            loop(lambda i: share(k, qa, i).wait_send(), 1, LINE)
    group_loop(lambda i: d1_copy(i).wait_send())

    @pl.when(b0 == 0)
    def _():
        fans_wait()

    @pl.when(b0 == 1)
    def _():
        e_near(1, 0).wait_recv()

    start(dx2_copy(1))
    newton_first(4 * b0)
    newton_step()
    newton_last(4 * b0, 2)
    early_near(2)
    l_mom = pltpu.make_async_copy(mom.at[:, b1, b0], omom_h, loc_sem.at[8])
    l_mom.start()
    ovec[...] = vec_sum(vecw, vw_s, vw_r)
    late = vec_sum(lv, lv_s, lv_r)
    ovec2[0:1, :] = late[0:1]
    ovec2[1:2, :] = late[4:5]
    ovec2[2:3, :] = ovec[6:7, mycols]
    ovec2[3:8, :] = jnp.zeros((5, CW), F32)

    @pl.when(b0 == 0)
    def _():
        e_near(2, 1).wait_recv()

    @pl.when(b0 == 1)
    def _():
        fans_wait()

    newton_first(5 - 4 * b0)
    newton_step()
    newton_last(5 - 4 * b0, 0)

    ncopy(dxs[0], dxr1.at[0], dx1_s.at[0], dx1_r.at[0], n1).wait_recv()
    for c in (0, 1):
        dx2_copy(c).wait_recv()
    ograd_b[...] = (ograd[...] + (dxr1[0].astype(F32) + dxr2[...].astype(F32)).T).astype(BF16)
    l_ograd = pltpu.make_async_copy(ograd_b, ograd_h, loc_sem.at[7])
    l_ograd.start()
    swap(2 + b0, 1).wait_recv()
    swap(4 * (1 - b0), 2).wait_recv()
    swap(1 + 4 * b0, 0).wait_recv()
    l_orth = pltpu.make_async_copy(gst.at[:, :, 0], oorth_h, loc_sem.at[9])
    l_orth.start()

    for m in range(3):
        pending.extend((pair_copy(m), over_copy(m), e_swap(m, b1)))
        if m < 2:
            pending.append(half_copy(m, keepc))
        for f, k, c in fans[m]:
            pending.append(far_copy(m, f, k, c))

            @pl.when(b0 != c)
            def _():
                near_copy(m, f, k, c).wait_send()

        @pl.when(b0 != m % 2)
        def _():
            e_near(m, b0).wait_send()

    for c in pending:
        c.wait_send()
    vec_done(vecw, vw_s, vw_r)
    vec_done(lv, lv_s, lv_r)
    group_loop(lambda i: d2_copy(o, i).wait_send())
    for k in range(3):
        loop(lambda i: e_share(k, qa, i).wait_send(), 1, LINE)
        if groups > 1:
            loop(lambda i: across(k, i).wait_send(), 1, groups)
            loop(lambda i: e_across(k, i).wait_send(), 1, groups)
    l_otok.wait()
    l_ograd.wait()
    l_mom.wait()
    l_orth.wait()


def run_layer(wide, tokens, cotangent, seg, pad, gen, in_w, out_w, in_m, out_m, shared, split):
    any_ = pl.BlockSpec(memory_space=pl.ANY)
    vm = pl.BlockSpec(memory_space=pltpu.VMEM)
    V = pltpu.VMEM
    dma = lambda *s: pltpu.SemaphoreType.DMA(s)
    one = pltpu.SemaphoreType.DMA
    groups = wide // OWN
    vslots = OWN + (groups if groups > 1 else 0)
    scratch = [
        V((LEN, D), BF16), V((TB, D), BF16), V((NAR, 16, CW), F32),
        V((4, D, CW), F32), V((2, CW, D), F32), V((6, CW, D), F32),
        V((3 * CW, D), BF16), V((D, 3 * CW), BF16),
        V((D, D), BF16), V((2, D, D), BF16), V((2, CW, CW), F32),
        V((2, LEN, 2 * CW), BF16), V((2, 2 * CW, LEN), BF16), V((2, CW, LEN), BF16), V((CW, LEN), BF16),
        V((LEN, CW), F32), V((TB, LEN), F32), V((2, LEN, LEN), BF16), V((2, TB, CW), F32),
        V((LEN, CW), F32), V((LEN, CW), BF16), V((TB, D), BF16),
        V((TB, D), BF16), V((TB, D), BF16), V((TB, D), BF16), V((TB, D), BF16), V((TB, D), BF16),
        V((TB, D), BF16), V((LEN, CW), BF16),
        V((NAR, 8, D), F32), V((vslots, 8, D), F32), V((CW, LEN), F32), V((CW, LEN), F32), V((3 * CW, LEN), BF16),
        V((3, 2, 2, CW, D), BF16), V((3, 2, CW, D), BF16), V((3, CW, D), BF16), V((3, CW, D), BF16),
        V((3, HR, D), BF16), V((3, HR, D), BF16), V((3, HR, D), BF16), V((3, LINE, PR, D), BF16), V((3, CW, HC), BF16),
        V((2, 2, HR, HC), BF16), V((2, LINE, 2, PR, HC), BF16), V((2, HR, D), BF16), V((OWN, 2, PR, HC), BF16),
        V((vslots, 8, CW), F32),
        V((6, 2, 2, 2, HR, D), BF16),
        V((groups, 3, PR, D) if groups > 1 else (1, 1, PR, D), BF16),
        V((groups, 3, 2, PR, HC) if groups > 1 else (1, 1, 1, PR, HC), BF16),
        V((2, D, TB), BF16), V((D, TB), BF16),
        dma(10), dma(4), dma(4), dma(2), dma(2), dma(4), dma(4), dma(3, 2), dma(3, 2), dma(1, 2), dma(1, 2),
        dma(4), dma(4), dma(4, TB // MID), dma(4, TB // MID), dma(4), dma(4), dma(vslots), dma(vslots),
        dma(vslots), dma(vslots),
        dma(3), dma(3), dma(3), dma(3), dma(3), dma(3), dma(3), dma(3), dma(3, LINE), dma(3, LINE),
        dma(OWN), dma(OWN), dma(OWN), dma(OWN),
        dma(6, groups), dma(6, groups),
        dma(6, LINE), dma(6, LINE), dma(6), dma(6),
        dma(3), dma(3), dma(3, LINE), dma(3, LINE), dma(3), dma(3), dma(5, 2), dma(5, 4), dma(3), dma(3),
        dma(2), dma(2), dma(2), dma(2),
    ]
    return pl.pallas_call(
        functools.partial(layer_kernel, wide),
        out_shape=[
            jax.ShapeDtypeStruct((TB, D), BF16),
            jax.ShapeDtypeStruct((TB, D), BF16),
            jax.ShapeDtypeStruct((6, 2, HR, D), BF16),
            jax.ShapeDtypeStruct((3, 2, CW, D), BF16),
            jax.ShapeDtypeStruct((8, D), F32),
            jax.ShapeDtypeStruct((8, CW), F32),
        ],
        in_specs=[any_, any_, vm, vm, vm, any_, any_, any_, any_, vm, vm],
        out_specs=[any_, any_, any_, any_, vm, vm],
        scratch_shapes=scratch,
        compiler_params=pltpu.CompilerParams(
            collective_id=0, has_side_effects=True, vmem_limit_bytes=62 * MB
        ),
        name="layer",
    )(tokens, cotangent, seg, pad, gen, in_w, out_w, in_m, out_m, shared, split)


def muon_step(weights, orthogonal):
    return weights - 0.2 * (0.2 * math.sqrt(D) * orthogonal + 0.01 * weights)


def adam_step(values, moment_one, moment_two, gradient):
    moment_one = 0.9 * moment_one + 0.1 * gradient
    moment_two = 0.999 * moment_two + 0.001 * gradient * gradient
    step_ratio = (
        moment_one / (1.0 - 0.9**STEP) / (jnp.sqrt(moment_two / (1.0 - 0.999**STEP)) + 1e-08)
    )
    return (moment_one, moment_two, values - 0.3 * (step_ratio + 0.01 * values))


def blend(average, weights):
    return 0.6 * average + 0.4 * weights


def update_kernel(
    otok, ograd, mom, orth, in_w, out_w, in_a, out_a, vec, vec2,
    sv, s1, s2, sa, pv, p1, p2, pa,
    tok_o, grad_o, inm_o, outm_o, inw_o, outw_o, inl_o, outl_o, ina_o, outa_o,
    s1_o, s2_o, sv_o, sa_o, p1_o, p2_o, pv_o, pa_o,
    mom_b, orth_b, inw_b, outw_b, ina_b, outa_b,
    inm_v, outm_v, inw_v, outw_v, inl_v, outl_v, ina_v, outa_v, grad_v, grad_b, tok_v, thru, rsem, wsem,
):
    whole = [
        pltpu.make_async_copy(ograd, grad_b, thru.at[0]),
        pltpu.make_async_copy(otok, tok_v, thru.at[1]),
    ]
    back = [
        pltpu.make_async_copy(grad_v, grad_o, thru.at[2]),
        pltpu.make_async_copy(tok_v, tok_o, thru.at[3]),
    ]
    reads, writes = [], []
    for k in range(6):
        j, inner = (k, True) if k < 4 else (k - 4, False)
        srcs = (mom.at[k], orth.at[k // 2, k % 2], (in_w if inner else out_w).at[j], (in_a if inner else out_a).at[j])
        dsts = (
            mom_b.at[k], orth_b.at[k], (inw_b if inner else outw_b).at[j], (ina_b if inner else outa_b).at[j],
        )
        reads.append([pltpu.make_async_copy(s, d, rsem.at[k, i]) for i, (s, d) in enumerate(zip(srcs, dsts))])
        bufs = (inm_v, inw_v, inl_v, ina_v) if inner else (outm_v, outw_v, outl_v, outa_v)
        outs = (inm_o, inw_o, inl_o, ina_o) if inner else (outm_o, outw_o, outl_o, outa_o)
        writes.append(
            [pltpu.make_async_copy(s.at[j], d.at[j], wsem.at[k, i]) for i, (s, d) in enumerate(zip(bufs, outs))]
        )
    for c in reads[0]:
        c.start()
    for c in reads[1]:
        c.start()
    for c in whole:
        c.start()
    for k in range(2, 6):
        for c in reads[k]:
            c.start()
    s1_o[...], s2_o[...], shared_new = adam_step(sv[...], s1[...], s2[...], vec[0:6, :])
    sv_o[...] = shared_new
    sa_o[...] = blend(sa[...], shared_new)
    p1_o[...], p2_o[...], split_new = adam_step(pv[...], p1[...], p2[...], vec2[0:3, :])
    pv_o[...] = split_new
    pa_o[...] = blend(pa[...], split_new)
    for k in range(6):
        if k in (1, 2):
            whole[k - 1].wait()
            if k == 1:
                grad_v[...] = grad_b[...].astype(F32)
            back[k - 1].start()
        for c in reads[k]:
            c.wait()
        if k < 4:
            inm_v[k] = mom_b[k].reshape(CW, D).astype(F32).T
            new = muon_step(inw_b[k], orth_b[k].astype(F32).T)
            inw_v[k] = new
            inl_v[k] = new.astype(BF16)
            ina_v[k] = blend(ina_b[k], new)
        else:
            j = k - 4
            outm_v[j] = mom_b[k].reshape(CW, D).astype(F32)
            new = muon_step(outw_b[j], orth_b[k].astype(F32))
            outw_v[j] = new
            outl_v[j] = new.astype(BF16)
            outa_v[j] = blend(outa_b[j], new)
        for c in writes[k]:
            c.start()
    for c in back:
        c.wait()
    for k in range(6):
        for c in writes[k]:
            c.wait()


def run_update(*args):
    vm = pl.BlockSpec(memory_space=pltpu.VMEM)
    any_ = pl.BlockSpec(memory_space=pl.ANY)
    S = jax.ShapeDtypeStruct
    V = pltpu.VMEM
    inner, outer = (4, D, CW), (2, CW, D)
    return pl.pallas_call(
        update_kernel,
        out_shape=[
            S((TB, D), BF16), S((TB, D), F32), S(inner, F32), S(outer, F32), S(inner, F32), S(outer, F32),
            S(inner, BF16), S(outer, BF16), S(inner, F32), S(outer, F32),
        ]
        + [S((6, D), F32)] * 4
        + [S((3, CW), F32)] * 4,
        in_specs=[any_] * 8 + [vm] * 10,
        out_specs=[any_] * 10 + [vm] * 8,
        scratch_shapes=[
            V((6, 2, HR, D), BF16), V((6, CW, D), BF16), V(inner, F32), V(outer, F32), V(inner, F32), V(outer, F32),
            V(inner, F32), V(outer, F32), V(inner, F32), V(outer, F32), V(inner, BF16), V(outer, BF16),
            V(inner, F32), V(outer, F32), V((TB, D), F32), V((TB, D), BF16), V((TB, D), BF16),
            pltpu.SemaphoreType.DMA((4,)), pltpu.SemaphoreType.DMA((6, 4)), pltpu.SemaphoreType.DMA((6, 4)),
        ],
        compiler_params=pltpu.CompilerParams(vmem_limit_bytes=60 * MB),
        name="update",
    )(*args)


def body(
    wide, tokens, cotangent, segments, padding, generative, in_weights, out_weights, in_momenta,
    out_momenta, in_average, out_average, shared_values, shared_moment1, shared_moment2,
    shared_average, split_values, split_moment1, split_moment2, split_average,
):
    flags = [v.reshape(TB // CW, CW) for v in (segments, padding, generative)]
    otok, ograd, mom, orth, vec, vec2 = run_layer(
        wide, tokens, cotangent, *flags, in_weights, out_weights, in_momenta, out_momenta,
        shared_values, split_values,
    )
    return tuple(
        run_update(
            otok, ograd, mom, orth, in_weights, out_weights, in_average, out_average, vec, vec2,
            shared_values, shared_moment1, shared_moment2, shared_average,
            split_values, split_moment1, split_moment2, split_average,
        )
    )


def solution(mesh):
    rows = P(("wide", "narrow"), None)
    flat = P(("wide", "narrow"))
    cols = P(None, None, "narrow")
    outs = P(None, "narrow", None)
    vec = P(None, "narrow")
    return jax.shard_map(
        functools.partial(body, mesh.shape["wide"]),
        mesh=mesh,
        in_specs=(
            rows, rows, flat, flat, flat, cols, outs, cols, outs, cols, outs,
            P(), P(), P(), P(), vec, vec, vec, vec,
        ),
        out_specs=(
            rows, rows, cols, outs, cols, outs, cols, outs, cols, outs,
            P(), P(), P(), P(), vec, vec, vec, vec,
        ),
        check_vma=False,
    )
```
